512 devices in a mesh: inst: 64 (over y, z), tp: 8 (over x, core).
Axes of the slice: x: 4, y: 8, z: 8, core: 2. Of those that a mesh axis runs over, the one named last changes fastest.
Arguments:
- queries: bfloat16 [256, 128, 128], P('inst', 'tp'), may hold values from -18 to 18
- new_keys: bfloat16 [256, 8, 128], P('inst', 'tp'), may hold values from -18 to 18
- new_values: bfloat16 [256, 8, 128], P('inst', 'tp'), may hold values from -6 to 6
- home_keys: bfloat16 [256, 256, 8, 128], P('inst', None, 'tp'), may hold values from -18 to 18
- home_values: bfloat16 [256, 256, 8, 128], P('inst', None, 'tp'), may hold values from -6 to 6
- home_len: int32 [256], P('inst'), may hold values from 1 to 256
- lent_keys: bfloat16 [4032, 32, 8, 128], P('inst', None, 'tp'), may hold values from -18 to 18
- lent_values: bfloat16 [4032, 32, 8, 128], P('inst', None, 'tp'), may hold values from -6 to 6
- lent_req: int32 [4032], replicated, may hold values from 0 to 255, as said below
- lent_len: int32 [4032], P('inst'), may hold values from 1 to 32
- out_weight: bfloat16 [16384, 16384], P('tp', 'inst'), may hold values from -0.046875 to 0.046875
- residual: bfloat16 [256, 16384], P('tp', 'inst'), may hold values from -0.29882812 to 0.29882812
Outputs:
- updated: bfloat16 [256, 16384], P('tp', 'inst')
The draws below stay inside these ranges and needn't reach their ends.
Inputs may be any that keep to these rules, and one draw needn't show every extreme that they name: Lent range s serves request lent_req[s], which is never homed on the instance that holds range s. Every instance holds exactly 1 lent range serving requests of each other home instance.
All inputs are finite; a program needn't handle non-finite values.
Results may differ from the reference program's by a relative error of at most 0.0051.
Values may be sent and summed in bfloat16 or wider, within the bound.
No kernel may reach another device: no remote copies, remote signals or barrier semaphores. Data moves between devices by JAX's collectives and lax.ppermute only.
A program may use at most 64 MiB of HBM per device.

```python
import math
import jax
import jax.numpy as jnp
from jax import lax

D = 16384
QH = 128
KVH = 8
HD = 128
REQ_DEV = 4
HOME_TOK = 256
LENT_TOK = 32
LENT = 63
REQUESTS = 256
SLOTS = 4032
N_INST = 64


def serving(key):
    key = jax.random.fold_in(key, 41)
    holder = jnp.arange(N_INST, dtype=jnp.int32)[:, None]
    offset = jnp.arange(LENT, dtype=jnp.int32)[None, :]
    homes = (holder + 1 + offset) % N_INST
    which = jax.random.randint(jax.random.fold_in(key, 3), (N_INST, LENT), 0, REQ_DEV)
    which = which.at[0, N_INST - 2].set(REQ_DEV - 1)
    which = which.at[1, N_INST - 2].set(0)
    return (homes * REQ_DEV + which).reshape(-1).astype(jnp.int32)


def draw_queries(key, part):
    key = jax.random.fold_in(key, 1)
    count = REQ_DEV * N_INST
    drawn = 2.0 * jnp.clip(jax.random.normal(jax.random.fold_in(key, 2), (count, QH, HD), jnp.float32), -4.0, 4.0)
    return drawn.astype(jnp.bfloat16)


def draw_new_keys(key, part):
    key = jax.random.fold_in(key, 11)
    count = REQ_DEV * N_INST
    drawn = jnp.clip(jax.random.normal(jax.random.fold_in(key, 2), (count, KVH, HD), jnp.float32), -6.0, 6.0)
    return drawn.astype(jnp.bfloat16)


def draw_home_keys(key, part):
    key = jax.random.fold_in(key, 21)
    count = REQ_DEV * N_INST
    rough = jnp.clip(jax.random.normal(jax.random.fold_in(key, 2), (count, HOME_TOK, KVH, HD), jnp.float32), -6.0, 6.0)
    return rough.astype(jnp.bfloat16)


def draw_lent_keys(key, part):
    key = jax.random.fold_in(key, 61)
    count = N_INST * LENT
    rough = jnp.clip(jax.random.normal(jax.random.fold_in(key, 2), (count, LENT_TOK, KVH, HD), jnp.float32), -6.0, 6.0)
    return rough.astype(jnp.bfloat16)


def draw_home_len(key, part):
    key = jax.random.fold_in(key, 31)
    count = REQ_DEV * N_INST
    lengths = jax.random.randint(key, (count,), 1, HOME_TOK + 1)
    return lengths.at[0].set(HOME_TOK).astype(jnp.int32)


def draw_lent_req(key, part):
    return serving(key)


def draw_lent_len(key, part):
    key = jax.random.fold_in(key, 51)
    ceiling = jax.random.randint(jax.random.fold_in(key, 1), (N_INST, 1), LENT_TOK // 4, LENT_TOK + 1)
    raw = jax.random.randint(jax.random.fold_in(key, 2), (N_INST, LENT), 0, LENT_TOK)
    lengths = 1 + raw * ceiling // LENT_TOK
    lengths = lengths.at[0, 0].set(LENT_TOK)
    return lengths.reshape(-1).astype(jnp.int32)


def levels(key, shape, cuts, low, high):
    level, own = 1.0, jax.random.fold_in(key, 6)
    for position, parts in cuts:
        steps = jnp.exp(jax.random.uniform(jax.random.fold_in(own, position), (parts,), jnp.float32, low / len(cuts), high / len(cuts)))
        level = level * jnp.repeat(steps, shape[position] // parts).reshape([-1 if axis == position else 1 for axis in range(len(shape))])
    return level


def centred(stream_key, extent, scale, bound, pieces=(), held_as=jnp.bfloat16):
    drawn = scale * jax.random.normal(stream_key, extent, jnp.float32)
    if pieces:
        drawn = drawn * levels(stream_key, extent, pieces, -0.22, 0.18)
    return jnp.clip(drawn, -bound, bound).astype(held_as)


def setup_inputs(seed: int = 0) -> dict:
    key_list = jax.random.split(jax.random.key(seed), 13)
    queries = draw_queries(jax.random.fold_in(key_list[12], 71), 0)
    new_keys = draw_new_keys(jax.random.fold_in(key_list[12], 71), 0)
    new_values = centred(key_list[2], (REQUESTS, KVH, HD), 1.0, 6.0, ((0, 64), (1, 8)))
    home_keys = draw_home_keys(jax.random.fold_in(key_list[12], 71), 0)
    home_values = centred(key_list[4], (REQUESTS, HOME_TOK, KVH, HD), 1.0, 6.0, ((0, 64), (2, 8)))
    home_len = draw_home_len(jax.random.fold_in(key_list[12], 71), 0)
    lent_keys = draw_lent_keys(jax.random.fold_in(key_list[12], 71), 0)
    lent_values = centred(key_list[7], (SLOTS, LENT_TOK, KVH, HD), 1.0, 6.0, ((0, 64), (2, 8)))
    lent_req = draw_lent_req(jax.random.fold_in(key_list[12], 71), 0)
    lent_len = draw_lent_len(jax.random.fold_in(key_list[12], 71), 0)
    out_weight = centred(key_list[10], (QH * HD, D), (QH * HD) ** -0.5, 0.046875, ((0, 8), (1, 64)))
    residual = centred(key_list[11], (REQUESTS, D), 0.05, 0.29882812, ((0, 8), (1, 64)))
    return dict(queries=queries, new_keys=new_keys, new_values=new_values, home_keys=home_keys, home_values=home_values, home_len=home_len, lent_keys=lent_keys, lent_values=lent_values, lent_req=lent_req, lent_len=lent_len, out_weight=out_weight, residual=residual)


VERY_LOW = -1e+30

def scores_of(query, keys, valid):
    raw = jnp.einsum('nkge,nske->nkgs', query.astype(jnp.float32), keys.astype(jnp.float32))
    raw = raw / math.sqrt(query.shape[-1])
    return jnp.where(valid[:, None, None, :], raw, VERY_LOW)

def mix(weights, values):
    rounded = lax.optimization_barrier(weights.astype(jnp.bfloat16)).astype(jnp.float32)
    return jnp.einsum('nkgs,nske->nkge', rounded, values.astype(jnp.float32))

def home_partial(query, new_key, new_value, keys, values, length):
    valid = jnp.arange(keys.shape[1]).astype(jnp.int32)[None, :] < length[:, None]
    scores = scores_of(query, keys, valid)
    fresh = jnp.einsum('nkge,nke->nkg', query.astype(jnp.float32), new_key.astype(jnp.float32))
    fresh = fresh / math.sqrt(query.shape[-1])
    top = jnp.maximum(lax.optimization_barrier(jnp.max(scores, axis=-1)), fresh)
    weights = jnp.exp(scores - top[..., None])
    own_weight = jnp.exp(fresh - top)
    total = lax.optimization_barrier(jnp.sum(weights, axis=-1)) + own_weight
    own_round = lax.optimization_barrier(own_weight.astype(jnp.bfloat16)).astype(jnp.float32)
    mixed = mix(weights, values) + own_round[..., None] * new_value.astype(jnp.float32)[:, :, None, :]
    return (top, total, mixed)

def slot_partial(query, keys, values, length):
    valid = jnp.arange(keys.shape[1]).astype(jnp.int32)[None, :] < length[:, None]
    scores = scores_of(query, keys, valid)
    top = lax.optimization_barrier(jnp.max(scores, axis=-1))
    weights = jnp.exp(scores - top[..., None])
    return (top, lax.optimization_barrier(jnp.sum(weights, axis=-1)), mix(weights, values))

def reference(queries, new_keys, new_values, home_keys, home_values, home_len, lent_keys, lent_values, lent_req, lent_len, out_weight, residual):
    group = QH // KVH
    requests = REQ_DEV * N_INST
    grouped = queries.reshape(N_INST, REQ_DEV, KVH, group, HD)
    home_parts = lax.map(lambda items: home_partial(*items), (grouped, new_keys.reshape(N_INST, REQ_DEV, KVH, HD), new_values.reshape(N_INST, REQ_DEV, KVH, HD), home_keys.reshape(N_INST, REQ_DEV, HOME_TOK, KVH, HD), home_values.reshape(N_INST, REQ_DEV, HOME_TOK, KVH, HD), home_len.reshape(N_INST, REQ_DEV)))
    slot_query = queries[lent_req].reshape(N_INST, LENT, KVH, group, HD)
    slot_parts = lax.map(lambda items: slot_partial(*items), (slot_query, lent_keys.reshape(N_INST, LENT, LENT_TOK, KVH, HD), lent_values.reshape(N_INST, LENT, LENT_TOK, KVH, HD), lent_len.reshape(N_INST, LENT)))
    slot_top = slot_parts[0].reshape(N_INST * LENT, KVH, group)
    slot_total = slot_parts[1].reshape(N_INST * LENT, KVH, group)
    slot_mixed = slot_parts[2].reshape(N_INST * LENT, KVH, group, HD)
    ident = jnp.arange(requests).astype(jnp.int32).reshape(N_INST, REQ_DEV)

    def combine(items):
        home_top, home_total, home_mixed, own_ids = items
        assign = (lent_req[None, :] == own_ids[:, None])[:, :, None, None]
        far_top = lax.optimization_barrier(jnp.max(jnp.where(assign, slot_top[None], VERY_LOW), axis=1))
        peak = jnp.maximum(home_top, far_top)
        weight = jnp.where(assign, jnp.exp(slot_top[None] - peak[:, None]), 0.0)
        near = jnp.exp(home_top - peak)
        total = home_total * near + lax.optimization_barrier(jnp.sum(weight * slot_total[None], axis=1))
        mixed = home_mixed * near[..., None] + jnp.einsum('rnkg,nkge->rkge', weight, slot_mixed, precision=lax.Precision.HIGHEST)
        return (mixed / total[..., None]).astype(jnp.bfloat16).reshape(REQ_DEV, QH * HD)
    attended = lax.map(combine, (home_parts[0], home_parts[1], home_parts[2], ident)).reshape(requests, QH * HD)
    projected = jnp.dot(attended, out_weight, preferred_element_type=jnp.float32)
    return (residual.astype(jnp.float32) + projected).astype(jnp.bfloat16)
```

```python
import math

import jax
import jax.numpy as jnp
from jax import lax
from jax.experimental import pallas as pl
from jax.experimental.pallas import tpu as pltpu
from jax.sharding import PartitionSpec as P

VERY_LOW = -1e30
SCALE = 1.0 / math.sqrt(128.0)
F32 = jnp.float32
BF16 = jnp.bfloat16
NT = (((1,), (1,)), ((), ()))
TN = (((0,), (0,)), ((), ()))
SMEM = pl.BlockSpec(memory_space=pltpu.SMEM)
VMEM = pl.BlockSpec(memory_space=pltpu.VMEM)


def dot(a, b, dims):
    return lax.dot_general(a, b, dims, preferred_element_type=F32)


def iota(shape, axis):
    return lax.broadcasted_iota(jnp.int32, shape, axis)


def slot_kernel(slot_ref, len_ref, q_ref, k_ref, v_ref, out_ref):
    owner = iota((32, 128), 1) >> 4
    token = iota((32, 128), 0)
    row = iota((8, 128), 0)
    for g in range(8):
        slots = [slot_ref[8 * g + j] for j in range(8)]
        query = q_ref[8 * g : 8 * g + 8].reshape(128, 128)
        raw = dot(jnp.concatenate([k_ref[s] for s in slots], axis=0), query, NT)
        scores = jnp.zeros((32, 128), F32)
        length = jnp.zeros((32, 128), jnp.int32)
        for j, s in enumerate(slots):
            scores = jnp.where(owner == j, raw[32 * j : 32 * j + 32], scores)
            length = jnp.where(owner == j, len_ref[s], length)
        scores = jnp.where(token < length, scores * SCALE, VERY_LOW)
        top = jnp.max(scores, axis=0, keepdims=True)
        weights = jnp.exp(scores - top)
        total = jnp.sum(weights, axis=0, keepdims=True)
        share = weights * (1.0 / total)
        blocks = jnp.concatenate(
            [jnp.where(owner == j, share, 0.0) for j in range(8)], axis=0
        ).astype(BF16)
        mixed = dot(blocks, jnp.concatenate([v_ref[s] for s in slots], axis=0), TN)
        lse = top + jnp.log(total)
        high = lse.astype(BF16).astype(F32)
        mid = (lse - high).astype(BF16).astype(F32)
        low = lse - high - mid
        stats = jnp.where(row == 0, high, jnp.where(row == 1, mid, jnp.where(row == 2, low, 0.0)))
        for j in range(8):
            out_ref[8 * g + j] = jnp.concatenate(
                [mixed[16 * j : 16 * j + 16], stats], axis=0
            ).astype(BF16)


def home_kernel(len_ref, q_ref, nk_ref, nv_ref, k_ref, v_ref, out_ref, lse_ref):
    query = q_ref[...].reshape(64, 128)
    query = jnp.concatenate([query, query], axis=0)
    owner = (iota((256, 128), 1) >> 4) & 3
    token = iota((256, 128), 0)
    scores = jnp.zeros((256, 128), F32)
    length = jnp.zeros((256, 128), jnp.int32)
    for r in range(4):
        scores = jnp.where(owner == r, dot(k_ref[r], query, NT), scores)
        length = jnp.where(owner == r, len_ref[r], length)
    scores = jnp.where(token < length, scores * SCALE, VERY_LOW)
    mine = ((iota((4, 128), 1) >> 4) & 3) == iota((4, 128), 0)
    fresh = dot(nk_ref[...], query, NT) * SCALE
    fresh = jnp.sum(jnp.where(mine, fresh, 0.0), axis=0, keepdims=True)
    top = jnp.maximum(jnp.max(scores, axis=0, keepdims=True), fresh)
    weights = jnp.exp(scores - top)
    own = jnp.exp(fresh - top)
    total = jnp.sum(weights, axis=0, keepdims=True) + own
    scale = 1.0 / total
    share = weights * scale
    mixed = dot(jnp.where(mine, own * scale, 0.0).astype(BF16), nv_ref[...], TN)
    for r in range(4):
        mixed += dot(jnp.where(owner == r, share, 0.0).astype(BF16), v_ref[r], TN)
    out_ref[...] = mixed[:64].astype(BF16)
    lse_ref[...] = top + jnp.log(total)


def merge_kernel(me_ref, req_ref, lse_ref, home_ref, recv_ref, out_ref):
    lane = iota((128, 128), 1)
    line = iota((128, 128), 0)
    spread = ((line >> 4) == (me_ref[0] & 7)) & ((line & 15) == (lane & 15))
    stats = recv_ref[:, 16:24, :].reshape(512, 128)
    stats = dot(stats, spread.astype(F32).astype(BF16), (((1,), (0,)), ((), ())))
    stats = stats.reshape(8, 8, 8, 128)
    group = iota((8, 128), 1) >> 4
    far = jnp.zeros((8, 8, 128), F32)
    for n in range(8):
        far = far + jnp.where((group == n)[None], stats[:, n], 0.0)
    far = jnp.sum(far, axis=1)
    near = lse_ref[...]
    which = (iota((1, 128), 1) >> 4)
    req = req_ref[...]
    tops = []
    for r in range(4):
        t = jnp.max(jnp.where(req == r, far, VERY_LOW), axis=0, keepdims=True)
        tops.append(jnp.maximum(t, jnp.where(which == r, near, VERY_LOW)))
    peak = jnp.concatenate(tops, axis=0)
    for shift in (16, 32, 64):
        peak = jnp.maximum(peak, pltpu.roll(peak, shift, 1))
    far_w, near_w, totals = [], [], []
    for r in range(4):
        p = peak[r : r + 1]
        f = jnp.where(req == r, jnp.exp(far - p), 0.0)
        n = jnp.where(which == r, jnp.exp(near - p), 0.0)
        far_w.append(f)
        near_w.append(n)
        totals.append(jnp.sum(f, axis=0, keepdims=True) + n)
    total = jnp.concatenate(totals, axis=0)
    for shift in (16, 32, 64):
        total = total + pltpu.roll(total, shift, 1)
    scale = 1.0 / total
    same = (iota((16, 128), 1) & 15) == iota((16, 128), 0)

    def spread_rows(rows):
        full = jnp.concatenate([jnp.where(same, row, 0.0) for row in rows], axis=0)
        high = full.astype(BF16)
        return high, (full - high.astype(F32)).astype(BF16)

    nn = (((1,), (0,)), ((), ()))
    high, low = spread_rows([near_w[r] * scale[r : r + 1] for r in range(4)])
    home = home_ref[...]
    acc = dot(high[:, :64], home, nn) + dot(low[:, :64], home, nn)
    far_w = [far_w[r] * scale[r : r + 1] for r in range(4)]
    for g in range(8):
        high, low = spread_rows([far_w[r][g : g + 1] for r in range(4)])
        block = recv_ref[8 * g : 8 * g + 8, :16, :].reshape(128, 128)
        acc += dot(high, block, nn) + dot(low, block, nn)
    out_ref[...] = acc.astype(BF16)


def project_kernel(a_ref, b_ref, w_ref, out_ref, rows_ref):
    q = iota((256, 256), 0)
    p = iota((256, 256), 1)
    move = p == 64 * ((q >> 2) & 3) + 16 * (q & 3) + (q >> 4)
    move = move.astype(F32).astype(BF16)
    nn = (((1,), (0,)), ((), ()))
    for b in range(16):
        parts = []
        for i in range(4 * b, 4 * b + 4):
            parts += [a_ref[i], b_ref[8 * (i % 8) + i // 8]]
        moved = dot(move, jnp.concatenate(parts, axis=0), nn).astype(BF16)
        for h in range(16):
            rows_ref[16 * b : 16 * b + 16, 128 * h : 128 * h + 128] = moved[16 * h : 16 * h + 16]
    out_ref[...] = dot(rows_ref[...], w_ref[...], nn).astype(BF16)


Z_GROUPS = [[8 * y + z for z in range(8)] for y in range(8)]
Y_GROUPS = [[8 * y + z for y in range(8)] for z in range(8)]


def spread_along(block, groups):
    copies = jnp.broadcast_to(block[None], (8,) + block.shape)
    return lax.all_to_all(
        copies, "inst", split_axis=0, concat_axis=0, tiled=True, axis_index_groups=groups
    )


def body(
    queries,
    new_keys,
    new_values,
    home_keys,
    home_values,
    home_len,
    lent_keys,
    lent_values,
    lent_req,
    lent_len,
    out_weight,
    residual,
):
    here = lax.axis_index("inst")
    table = lent_req.reshape(64, 63)
    mine = (table >> 2) == here
    source = jnp.sum(jnp.where(mine, table & 3, 0), axis=1)
    pick = source[:, None, None]
    q = queries[None]
    send = jnp.where(
        pick == 0, q[:, 0], jnp.where(pick == 1, q[:, 1], jnp.where(pick == 2, q[:, 2], q[:, 3]))
    )
    asked = lax.all_to_all(send, "inst", split_axis=0, concat_axis=0, tiled=True)
    own = lax.dynamic_slice_in_dim(table, here, 1, 0) >> 2
    order = jnp.arange(63, dtype=jnp.int32)[None, :]
    every = jnp.arange(64, dtype=jnp.int32)
    slot_of = jnp.sum(jnp.where(own == every[:, None], order, 0), axis=1)
    home_out, home_lse = pl.pallas_call(
        home_kernel,
        out_shape=(
            jax.ShapeDtypeStruct((64, 128), BF16),
            jax.ShapeDtypeStruct((1, 128), F32),
        ),
        in_specs=[SMEM] + [VMEM] * 5,
        out_specs=(VMEM, VMEM),
        name="home_part",
    )(
        home_len,
        queries,
        new_keys.reshape(4, 128),
        new_values.reshape(4, 128),
        home_keys.reshape(4, 256, 128),
        home_values.reshape(4, 256, 128),
    )
    parts = pl.pallas_call(
        slot_kernel,
        out_shape=jax.ShapeDtypeStruct((64, 24, 128), BF16),
        in_specs=[SMEM, SMEM] + [VMEM] * 3,
        out_specs=VMEM,
        name="slot_part",
    )(slot_of, lent_len, asked, lent_keys.reshape(63, 32, 128), lent_values.reshape(63, 32, 128))
    recv = lax.all_to_all(parts, "inst", split_axis=0, concat_axis=0, tiled=True)
    serves = jnp.where(every == here, -1, source)
    req = jnp.broadcast_to(serves.reshape(8, 8, 1), (8, 8, 16)).reshape(8, 128)
    attended = pl.pallas_call(
        merge_kernel,
        out_shape=jax.ShapeDtypeStruct((64, 128), BF16),
        in_specs=[SMEM] + [VMEM] * 4,
        out_specs=VMEM,
        name="merge_parts",
    )(here.reshape(1), req, home_lse, home_out, recv)
    first = spread_along(attended[:32], Z_GROUPS)
    second = spread_along(attended[32:], Y_GROUPS)
    first = spread_along(first, Y_GROUPS).reshape(64, 32, 128)
    second = spread_along(second, Z_GROUPS).reshape(64, 32, 128)
    partial = pl.pallas_call(
        project_kernel,
        out_shape=jax.ShapeDtypeStruct((256, 256), BF16),
        in_specs=[VMEM] * 3,
        out_specs=VMEM,
        scratch_shapes=[pltpu.VMEM((256, 2048), BF16)],
        name="project",
    )(first, second, out_weight)
    sums = lax.all_to_all(
        partial.reshape(8, 32, 256), "tp", split_axis=0, concat_axis=0, tiled=True
    )
    return (residual.astype(F32) + jnp.sum(sums.astype(F32), axis=0)).astype(BF16)


def solution(mesh):
    placed = (
        P("inst", "tp", None),
        P("inst", "tp", None),
        P("inst", "tp", None),
        P("inst", None, "tp", None),
        P("inst", None, "tp", None),
        P("inst"),
        P("inst", None, "tp", None),
        P("inst", None, "tp", None),
        P(),
        P("inst"),
        P("tp", "inst"),
        P("tp", "inst"),
    )
    return jax.shard_map(
        body, mesh=mesh, in_specs=placed, out_specs=P("tp", "inst"), check_vma=False
    )
```

```python
import math

import jax
import jax.numpy as jnp
from jax import lax
from jax.experimental import pallas as pl
from jax.experimental.pallas import tpu as pltpu
from jax.sharding import PartitionSpec as P

VERY_LOW = -1e30
SCALE = 1.0 / math.sqrt(128.0)
F32 = jnp.float32
BF16 = jnp.bfloat16
NT = (((1,), (1,)), ((), ()))
TN = (((0,), (0,)), ((), ()))
NN = (((1,), (0,)), ((), ()))
SMEM = pl.BlockSpec(memory_space=pltpu.SMEM)
VMEM = pl.BlockSpec(memory_space=pltpu.VMEM)


def dot(a, b, dims):
    return lax.dot_general(a, b, dims, preferred_element_type=F32)


def iota(shape, axis):
    return lax.broadcasted_iota(jnp.int32, shape, axis)


def thirds(x):
    high = x.astype(BF16).astype(F32)
    mid = (x - high).astype(BF16).astype(F32)
    return [high, mid, x - high - mid]


def halves(x):
    high = x.astype(BF16)
    return high, (x - high.astype(F32)).astype(BF16)


def slot_kernel(slot_ref, len_ref, q_ref, k_ref, v_ref, out_ref):
    owner = iota((32, 128), 1) >> 4
    token = iota((32, 128), 0)
    row = iota((8, 128), 0)
    for g in range(8):
        slots = [slot_ref[8 * g + j] for j in range(8)]
        query = q_ref[8 * g : 8 * g + 8].reshape(128, 128)
        raw = dot(jnp.concatenate([k_ref[s] for s in slots], axis=0), query, NT)
        scores = jnp.zeros((32, 128), F32)
        length = jnp.zeros((32, 128), jnp.int32)
        for j, s in enumerate(slots):
            scores = jnp.where(owner == j, raw[32 * j : 32 * j + 32], scores)
            length = jnp.where(owner == j, len_ref[s], length)
        scores = jnp.where(token < length, scores * SCALE, VERY_LOW)
        top = jnp.max(scores, axis=0, keepdims=True)
        weights = jnp.exp(scores - top)
        total = jnp.sum(weights, axis=0, keepdims=True)
        blocks = jnp.concatenate(
            [jnp.where(owner == j, weights, 0.0) for j in range(8)], axis=0
        ).astype(BF16)
        mixed = dot(blocks, jnp.concatenate([v_ref[s] for s in slots], axis=0), TN)
        stats = jnp.zeros((8, 128), F32)
        for i, part in enumerate(thirds(top) + thirds(total)):
            stats = jnp.where(row == i, part, stats)
        for j in range(8):
            out_ref[8 * g + j] = jnp.concatenate(
                [mixed[16 * j : 16 * j + 16], stats], axis=0
            ).astype(BF16)


def home_kernel(len_ref, q_ref, nk_ref, nv_ref, k_ref, v_ref, out_ref, stat_ref):
    query = q_ref[...].reshape(64, 128)
    query = jnp.concatenate([query, query], axis=0)
    owner = (iota((256, 128), 1) >> 4) & 3
    token = iota((256, 128), 0)
    scores = jnp.zeros((256, 128), F32)
    length = jnp.zeros((256, 128), jnp.int32)
    for r in range(4):
        scores = jnp.where(owner == r, dot(k_ref[r], query, NT), scores)
        length = jnp.where(owner == r, len_ref[r], length)
    scores = jnp.where(token < length, scores * SCALE, VERY_LOW)
    mine = ((iota((4, 128), 1) >> 4) & 3) == iota((4, 128), 0)
    fresh = dot(nk_ref[...], query, NT) * SCALE
    fresh = jnp.sum(jnp.where(mine, fresh, 0.0), axis=0, keepdims=True)
    top = jnp.maximum(jnp.max(scores, axis=0, keepdims=True), fresh)
    weights = jnp.exp(scores - top)
    own = jnp.exp(fresh - top)
    total = jnp.sum(weights, axis=0, keepdims=True) + own
    mixed = dot(jnp.where(mine, own, 0.0).astype(BF16), nv_ref[...], TN)
    for r in range(4):
        mixed += dot(jnp.where(owner == r, weights, 0.0).astype(BF16), v_ref[r], TN)
    out_ref[...] = mixed[:64]
    stat_ref[...] = jnp.concatenate([top, total], axis=0)


def merge_kernel(me_ref, req_ref, stat_ref, home_ref, recv_ref, a_ref, b_ref):
    lane = iota((128, 128), 1)
    line = iota((128, 128), 0)
    spread = ((line >> 4) == (me_ref[0] & 7)) & ((line & 15) == (lane & 15))
    stats = recv_ref[:, 16:24, :].reshape(512, 128)
    stats = dot(stats, spread.astype(F32).astype(BF16), NN).reshape(8, 8, 8, 128)
    group = iota((8, 128), 1) >> 4
    far = jnp.zeros((8, 8, 128), F32)
    for n in range(8):
        far = far + jnp.where((group == n)[None], stats[:, n], 0.0)
    far_top = far[:, 0] + far[:, 1] + far[:, 2]
    far_total = far[:, 3] + far[:, 4] + far[:, 5]
    near_top, near_total = stat_ref[0:1], stat_ref[1:2]
    which = iota((1, 128), 1) >> 4
    req = req_ref[...]
    tops = []
    for r in range(4):
        t = jnp.max(jnp.where(req == r, far_top, VERY_LOW), axis=0, keepdims=True)
        tops.append(jnp.maximum(t, jnp.where(which == r, near_top, VERY_LOW)))
    peak = jnp.concatenate(tops, axis=0)
    for shift in (16, 32, 64):
        peak = jnp.maximum(peak, pltpu.roll(peak, shift, 1))
    far_w, near_w, totals = [], [], []
    for r in range(4):
        p = peak[r : r + 1]
        f = jnp.where(req == r, jnp.exp(far_top - p), 0.0)
        n = jnp.where(which == r, jnp.exp(near_top - p), 0.0)
        far_w.append(f)
        near_w.append(n)
        totals.append(jnp.sum(f * far_total, axis=0, keepdims=True) + n * near_total)
    total = jnp.concatenate(totals, axis=0)
    for shift in (16, 32, 64):
        total = total + pltpu.roll(total, shift, 1)
    scale = 1.0 / total
    same = (iota((16, 128), 1) & 15) == iota((16, 128), 0)

    def spread_rows(rows):
        return halves(jnp.concatenate([jnp.where(same, row, 0.0) for row in rows], axis=0))

    high, low = spread_rows([near_w[r] * scale[r : r + 1] for r in range(4)])
    home_high, home_low = halves(home_ref[...])
    acc = dot(high[:, :64], home_high, NN) + dot(high[:, :64], home_low, NN)
    acc += dot(low[:, :64], home_high, NN)
    far_w = [far_w[r] * scale[r : r + 1] for r in range(4)]
    for g in range(8):
        high, low = spread_rows([far_w[r][g : g + 1] for r in range(4)])
        block = recv_ref[8 * g : 8 * g + 8, :16, :].reshape(128, 128)
        acc += dot(high, block, NN) + dot(low, block, NN)
    a_ref[...] = acc[:32].astype(BF16)
    b_ref[...] = acc[32:].astype(BF16)


def project_kernel(at_ref, *refs):
    a_refs, b_refs, w_ref = refs[:8], refs[8:16], refs[16]
    out_refs, rows_ref = refs[17:25], refs[25]
    q = iota((512, 512), 0)
    p = iota((512, 512), 1)
    r = q & 3
    move = p == 256 * (r >> 1) + 32 * ((q >> 2) & 7) + 16 * (r & 1) + (q >> 5)
    move = move.astype(F32).astype(BF16)
    for m in range(8):
        parts = [a_refs[m][...]] + [b[32 * m : 32 * m + 32] for b in b_refs]
        moved = dot(move, jnp.concatenate(parts, axis=0), NN).astype(BF16)
        for h in range(16):
            rows_ref[32 * m : 32 * m + 32, 128 * h : 128 * h + 128] = moved[32 * h : 32 * h + 32]
    partial = dot(rows_ref[...], w_ref[...], NN).astype(BF16)
    y, z, t = at_ref[0], at_ref[1], at_ref[2]
    q = iota((256, 256), 0)
    p = iota((256, 256), 1)
    order = p == 32 * ((y - t - (q >> 5)) & 7) + 4 * ((z - (q >> 2)) & 7) + (q & 3)
    placed = dot(order.astype(F32).astype(BF16), partial, NN).astype(BF16)
    for c in range(8):
        out_refs[c][...] = placed[32 * c : 32 * c + 32]


def along(axis, step):
    if axis == "z":
        return [(8 * y + z, 8 * y + (z + step) % 8) for y in range(8) for z in range(8)]
    return [(8 * y + z, 8 * ((y + step) % 8) + z) for y in range(8) for z in range(8)]


def spread_along(axis, block):
    return [block] + [lax.ppermute(block, "inst", along(axis, k)) for k in range(1, 8)]


def body(
    queries,
    new_keys,
    new_values,
    home_keys,
    home_values,
    home_len,
    lent_keys,
    lent_values,
    lent_req,
    lent_len,
    out_weight,
    residual,
):
    here = lax.axis_index("inst")
    table = lent_req.reshape(64, 63)
    mine = (table >> 2) == here
    source = jnp.sum(jnp.where(mine, table & 3, 0), axis=1)
    pick = source[:, None, None]
    q = queries[None]
    send = jnp.where(
        pick == 0, q[:, 0], jnp.where(pick == 1, q[:, 1], jnp.where(pick == 2, q[:, 2], q[:, 3]))
    )
    asked = lax.all_to_all(send, "inst", split_axis=0, concat_axis=0, tiled=True)
    own = lax.dynamic_slice_in_dim(table, here, 1, 0) >> 2
    order = jnp.arange(63, dtype=jnp.int32)[None, :]
    every = jnp.arange(64, dtype=jnp.int32)
    slot_of = jnp.sum(jnp.where(own == every[:, None], order, 0), axis=1)
    home_out, home_stat = pl.pallas_call(
        home_kernel,
        out_shape=(
            jax.ShapeDtypeStruct((64, 128), F32),
            jax.ShapeDtypeStruct((2, 128), F32),
        ),
        in_specs=[SMEM] + [VMEM] * 5,
        out_specs=(VMEM, VMEM),
        name="home_part",
    )(
        home_len,
        queries,
        new_keys.reshape(4, 128),
        new_values.reshape(4, 128),
        home_keys.reshape(4, 256, 128),
        home_values.reshape(4, 256, 128),
    )
    parts = pl.pallas_call(
        slot_kernel,
        out_shape=jax.ShapeDtypeStruct((64, 24, 128), BF16),
        in_specs=[SMEM, SMEM] + [VMEM] * 3,
        out_specs=VMEM,
        name="slot_part",
    )(slot_of, lent_len, asked, lent_keys.reshape(63, 32, 128), lent_values.reshape(63, 32, 128))
    recv = lax.all_to_all(parts, "inst", split_axis=0, concat_axis=0, tiled=True)
    serves = jnp.where(every == here, -1, source)
    req = jnp.broadcast_to(serves.reshape(8, 8, 1), (8, 8, 16)).reshape(8, 128)
    half = jax.ShapeDtypeStruct((32, 128), BF16)
    first, second = pl.pallas_call(
        merge_kernel,
        out_shape=(half, half),
        in_specs=[SMEM] + [VMEM] * 4,
        out_specs=(VMEM, VMEM),
        name="merge_parts",
    )(here.reshape(1), req, home_stat, home_out, recv)
    first = spread_along("z", first)
    second = spread_along("y", second)
    first = spread_along("y", jnp.concatenate(first, axis=0))
    second = spread_along("z", jnp.concatenate(second, axis=0))
    tp = lax.axis_index("tp")
    partial = pl.pallas_call(
        project_kernel,
        out_shape=(jax.ShapeDtypeStruct((32, 256), BF16),) * 8,
        in_specs=[SMEM] + [VMEM] * 17,
        out_specs=(VMEM,) * 8,
        scratch_shapes=[pltpu.VMEM((256, 2048), BF16)],
        name="project",
    )(jnp.stack([here >> 3, here & 7, tp]), *first, *second, out_weight)
    updated = residual.astype(F32) + partial[0].astype(F32)
    for c in range(1, 8):
        turn = [(t, (t + c) % 8) for t in range(8)]
        updated += lax.ppermute(partial[c], "tp", turn).astype(F32)
    return updated.astype(BF16)


def solution(mesh):
    placed = (
        P("inst", "tp", None),
        P("inst", "tp", None),
        P("inst", "tp", None),
        P("inst", None, "tp", None),
        P("inst", None, "tp", None),
        P("inst"),
        P("inst", None, "tp", None),
        P("inst", None, "tp", None),
        P(),
        P("inst"),
        P("tp", "inst"),
        P("tp", "inst"),
    )
    return jax.shard_map(
        body, mesh=mesh, in_specs=placed, out_specs=P("tp", "inst"), check_vma=False
    )
```

```python
import math

import jax
import jax.numpy as jnp
from jax import lax
from jax.experimental import pallas as pl
from jax.experimental.pallas import tpu as pltpu
from jax.sharding import Mesh, PartitionSpec as P

VERY_LOW = -1e30
SCALE = 1.0 / math.sqrt(128.0)
F32 = jnp.float32
BF16 = jnp.bfloat16
NT = (((1,), (1,)), ((), ()))
TN = (((0,), (0,)), ((), ()))
NN = (((1,), (0,)), ((), ()))
INST = ("y", "zh", "zp")
PARAMS = pltpu.CompilerParams(vmem_limit_bytes=16 * 2**20)
SMEM = pl.BlockSpec(memory_space=pltpu.SMEM)
VMEM = pl.BlockSpec(memory_space=pltpu.VMEM)


def dot(a, b, dims):
    return lax.dot_general(a, b, dims, preferred_element_type=F32)


def iota(shape, axis):
    return lax.broadcasted_iota(jnp.int32, shape, axis)


def thirds(x):
    high = x.astype(BF16).astype(F32)
    mid = (x - high).astype(BF16).astype(F32)
    return [high, mid, x - high - mid]


def halves(x):
    high = x.astype(BF16)
    return high, (x - high.astype(F32)).astype(BF16)


def slot_kernel(slot_ref, len_ref, q_ref, k_ref, v_ref, out_ref):
    owner = iota((32, 128), 1) >> 4
    token = iota((32, 128), 0)
    row = iota((8, 128), 0)
    for g in range(8):
        slots = [slot_ref[8 * g + j] for j in range(8)]
        query = q_ref[8 * g : 8 * g + 8].reshape(128, 128)
        raw = dot(jnp.concatenate([k_ref[s] for s in slots], axis=0), query, NT)
        scores = jnp.zeros((32, 128), F32)
        length = jnp.zeros((32, 128), jnp.int32)
        for j, s in enumerate(slots):
            scores = jnp.where(owner == j, raw[32 * j : 32 * j + 32], scores)
            length = jnp.where(owner == j, len_ref[s], length)
        scores = jnp.where(token < length, scores * SCALE, VERY_LOW)
        top = jnp.max(scores, axis=0, keepdims=True)
        weights = jnp.exp(scores - top)
        total = jnp.sum(weights, axis=0, keepdims=True)
        blocks = jnp.concatenate(
            [jnp.where(owner == j, weights, 0.0) for j in range(8)], axis=0
        ).astype(BF16)
        mixed = dot(blocks, jnp.concatenate([v_ref[s] for s in slots], axis=0), TN)
        stats = jnp.zeros((8, 128), F32)
        for i, part in enumerate(thirds(top) + thirds(total)):
            stats = jnp.where(row == i, part, stats)
        for j in range(8):
            out_ref[8 * g + j] = jnp.concatenate(
                [mixed[16 * j : 16 * j + 16], stats], axis=0
            ).astype(BF16)


def home_kernel(len_ref, q_ref, nk_ref, nv_ref, k_ref, v_ref, out_ref, stat_ref):
    query = q_ref[...].reshape(64, 128)
    query = jnp.concatenate([query, query], axis=0)
    owner = (iota((256, 128), 1) >> 4) & 3
    token = iota((256, 128), 0)
    scores = jnp.zeros((256, 128), F32)
    length = jnp.zeros((256, 128), jnp.int32)
    for r in range(4):
        scores = jnp.where(owner == r, dot(k_ref[r], query, NT), scores)
        length = jnp.where(owner == r, len_ref[r], length)
    scores = jnp.where(token < length, scores * SCALE, VERY_LOW)
    mine = ((iota((4, 128), 1) >> 4) & 3) == iota((4, 128), 0)
    fresh = dot(nk_ref[...], query, NT) * SCALE
    fresh = jnp.sum(jnp.where(mine, fresh, 0.0), axis=0, keepdims=True)
    top = jnp.maximum(jnp.max(scores, axis=0, keepdims=True), fresh)
    weights = jnp.exp(scores - top)
    own = jnp.exp(fresh - top)
    total = jnp.sum(weights, axis=0, keepdims=True) + own
    mixed = dot(jnp.where(mine, own, 0.0).astype(BF16), nv_ref[...], TN)
    for r in range(4):
        mixed += dot(jnp.where(owner == r, weights, 0.0).astype(BF16), v_ref[r], TN)
    out_ref[...] = mixed[:64]
    stat_ref[...] = jnp.concatenate([top, total], axis=0)


def merge_kernel(me_ref, req_ref, stat_ref, home_ref, recv_ref, out_ref):
    lane = iota((128, 128), 1)
    line = iota((128, 128), 0)
    spread = ((line >> 4) == (me_ref[0] & 7)) & ((line & 15) == (lane & 15))
    stats = recv_ref[:, 16:24, :].reshape(512, 128)
    stats = dot(stats, spread.astype(F32).astype(BF16), NN).reshape(8, 8, 8, 128)
    group = iota((8, 128), 1) >> 4
    far = jnp.zeros((8, 8, 128), F32)
    for n in range(8):
        far = far + jnp.where((group == n)[None], stats[:, n], 0.0)
    far_top = far[:, 0] + far[:, 1] + far[:, 2]
    far_total = far[:, 3] + far[:, 4] + far[:, 5]
    near_top, near_total = stat_ref[0:1], stat_ref[1:2]
    which = iota((1, 128), 1) >> 4
    req = req_ref[...]
    tops = []
    for r in range(4):
        t = jnp.max(jnp.where(req == r, far_top, VERY_LOW), axis=0, keepdims=True)
        tops.append(jnp.maximum(t, jnp.where(which == r, near_top, VERY_LOW)))
    peak = jnp.concatenate(tops, axis=0)
    for shift in (16, 32, 64):
        peak = jnp.maximum(peak, pltpu.roll(peak, shift, 1))
    far_w, near_w, totals = [], [], []
    for r in range(4):
        p = peak[r : r + 1]
        f = jnp.where(req == r, jnp.exp(far_top - p), 0.0)
        n = jnp.where(which == r, jnp.exp(near_top - p), 0.0)
        far_w.append(f)
        near_w.append(n)
        totals.append(jnp.sum(f * far_total, axis=0, keepdims=True) + n * near_total)
    total = jnp.concatenate(totals, axis=0)
    for shift in (16, 32, 64):
        total = total + pltpu.roll(total, shift, 1)
    scale = 1.0 / total
    same = (iota((16, 128), 1) & 15) == iota((16, 128), 0)

    def spread_rows(rows):
        return halves(jnp.concatenate([jnp.where(same, row, 0.0) for row in rows], axis=0))

    high, low = spread_rows([near_w[r] * scale[r : r + 1] for r in range(4)])
    home_high, home_low = halves(home_ref[...])
    acc = dot(high[:, :64], home_high, NN) + dot(high[:, :64], home_low, NN)
    acc += dot(low[:, :64], home_high, NN)
    far_w = [far_w[r] * scale[r : r + 1] for r in range(4)]
    for g in range(8):
        high, low = spread_rows([far_w[r][g : g + 1] for r in range(4)])
        block = recv_ref[8 * g : 8 * g + 8, :16, :].reshape(128, 128)
        acc += dot(high, block, NN) + dot(low, block, NN)
    out_ref[...] = acc.astype(BF16)


def project_kernel(parity_ref, rows_ref, mine_ref, other_ref, out_ref, wide_ref):
    q = iota((256, 256), 0)
    p = iota((256, 256), 1)
    move = p == 64 * ((q >> 2) & 3) + 16 * (q & 3) + (q >> 4)
    move = move.astype(F32).astype(BF16)
    for b in range(8):
        moved = dot(move, rows_ref[4 * b : 4 * b + 4].reshape(256, 128), NN).astype(BF16)
        for h in range(16):
            wide_ref[16 * b : 16 * b + 16, 128 * h : 128 * h + 128] = moved[16 * h : 16 * h + 16]
    parity = parity_ref[0]
    wide = wide_ref[...]
    out_ref[parity] = dot(wide, mine_ref[...], NN).astype(BF16).reshape(8, 16, 256)
    out_ref[1 - parity] = dot(wide, other_ref[...], NN).astype(BF16).reshape(8, 16, 256)


def body(
    queries,
    new_keys,
    new_values,
    home_keys,
    home_values,
    home_len,
    lent_keys,
    lent_values,
    lent_req,
    lent_len,
    out_weight,
    residual,
):
    here = lax.axis_index(INST)
    table = lent_req.reshape(64, 63)
    mine = (table >> 2) == here
    source = jnp.sum(jnp.where(mine, table & 3, 0), axis=1)
    pick = source[:, None, None]
    q = queries[None]
    send = jnp.where(
        pick == 0, q[:, 0], jnp.where(pick == 1, q[:, 1], jnp.where(pick == 2, q[:, 2], q[:, 3]))
    )
    asked = lax.all_to_all(send, INST, split_axis=0, concat_axis=0, tiled=True)
    own = lax.dynamic_slice_in_dim(table, here, 1, 0) >> 2
    order = jnp.arange(63, dtype=jnp.int32)[None, :]
    every = jnp.arange(64, dtype=jnp.int32)
    slot_of = jnp.sum(jnp.where(own == every[:, None], order, 0), axis=1)
    home_out, home_stat = pl.pallas_call(
        home_kernel,
        out_shape=(
            jax.ShapeDtypeStruct((64, 128), F32),
            jax.ShapeDtypeStruct((2, 128), F32),
        ),
        in_specs=[SMEM] + [VMEM] * 5,
        out_specs=(VMEM, VMEM),
        compiler_params=PARAMS,
        name="home_part",
    )(
        home_len,
        queries,
        new_keys.reshape(4, 128),
        new_values.reshape(4, 128),
        home_keys.reshape(4, 256, 128),
        home_values.reshape(4, 256, 128),
    )
    parts = pl.pallas_call(
        slot_kernel,
        out_shape=jax.ShapeDtypeStruct((64, 24, 128), BF16),
        in_specs=[SMEM, SMEM] + [VMEM] * 3,
        out_specs=VMEM,
        compiler_params=PARAMS,
        name="slot_part",
    )(slot_of, lent_len, asked, lent_keys.reshape(63, 32, 128), lent_values.reshape(63, 32, 128))
    recv = lax.all_to_all(parts, INST, split_axis=0, concat_axis=0, tiled=True)
    serves = jnp.where(every == here, -1, source)
    req = jnp.broadcast_to(serves.reshape(8, 8, 1), (8, 8, 16)).reshape(8, 128)
    attended = pl.pallas_call(
        merge_kernel,
        out_shape=jax.ShapeDtypeStruct((64, 128), BF16),
        in_specs=[SMEM] + [VMEM] * 4,
        out_specs=VMEM,
        compiler_params=PARAMS,
        name="merge_parts",
    )(here.reshape(1), req, home_stat, home_out, recv)
    copies = jnp.broadcast_to(attended[None], (32, 64, 128))
    rows = lax.all_to_all(copies, ("y", "zh"), split_axis=0, concat_axis=0, tiled=True)
    other_weight = lax.ppermute(out_weight, "zp", [(0, 1), (1, 0)])
    partial = pl.pallas_call(
        project_kernel,
        out_shape=jax.ShapeDtypeStruct((2, 8, 16, 256), BF16),
        in_specs=[SMEM] + [VMEM] * 3,
        out_specs=VMEM,
        scratch_shapes=[pltpu.VMEM((128, 2048), BF16)],
        compiler_params=PARAMS,
        name="project",
    )(lax.axis_index("zp").reshape(1), rows, out_weight, other_weight)
    sums = lax.all_to_all(
        partial.reshape(16, 16, 256), ("zp", "tp"), split_axis=0, concat_axis=0, tiled=True
    )
    summed = jnp.sum(sums.reshape(2, 8, 4, 4, 256).astype(F32), axis=1)
    summed = summed.transpose(1, 0, 2, 3).reshape(32, 256)
    return (residual.astype(F32) + summed).astype(BF16)


def solution(mesh):
    placed = (
        P(INST, "tp", None),
        P(INST, "tp", None),
        P(INST, "tp", None),
        P(INST, None, "tp", None),
        P(INST, None, "tp", None),
        P(INST),
        P(INST, None, "tp", None),
        P(INST, None, "tp", None),
        P(),
        P(INST),
        P("tp", INST),
        P("tp", INST),
    )
    fine = Mesh(mesh.devices.reshape(8, 4, 2, 8), INST + ("tp",))
    return jax.shard_map(
        body, mesh=fine, in_specs=placed, out_specs=P("tp", INST), check_vma=False
    )
```

```python
import math

import jax
import jax.numpy as jnp
from jax import lax
from jax.experimental import pallas as pl
from jax.experimental.pallas import tpu as pltpu
from jax.sharding import Mesh, PartitionSpec as P

VERY_LOW = -1e30
SCALE = 1.0 / math.sqrt(128.0)
F32 = jnp.float32
BF16 = jnp.bfloat16
NT = (((1,), (1,)), ((), ()))
TN = (((0,), (0,)), ((), ()))
NN = (((1,), (0,)), ((), ()))
INST = ("y", "zh", "zp")
PARAMS = pltpu.CompilerParams(vmem_limit_bytes=16 * 2**20)
SMEM = pl.BlockSpec(memory_space=pltpu.SMEM)
ANY = pl.BlockSpec(memory_space=pl.ANY)
VMEM = pl.BlockSpec(memory_space=pltpu.VMEM)


def dot(a, b, dims):
    return lax.dot_general(a, b, dims, preferred_element_type=F32)


def iota(shape, axis):
    return lax.broadcasted_iota(jnp.int32, shape, axis)


def thirds(x):
    high = x.astype(BF16).astype(F32)
    mid = (x - high).astype(BF16).astype(F32)
    return [high, mid, x - high - mid]


def halves(x):
    high = x.astype(BF16)
    return high, (x - high.astype(F32)).astype(BF16)


def ask_kernel(here_ref, table_ref, q_ref, send_ref, req_ref):
    here = here_ref[0]
    table = table_ref[...]
    found = jnp.where((table >> 2) == here, (table & 3) + 1, 0).astype(F32)
    lane = iota((1, 128), 1)
    rows = []
    for j in range(64):
        line, first = divmod(63 * j, 128)
        row = jnp.where(lane >= first, found[line : line + 1], 0.0)
        if first + 63 <= 128:
            row = jnp.where(lane < first + 63, row, 0.0)
        else:
            row = jnp.where(lane < first + 63 - 128, found[line + 1 : line + 2], row)
        rows.append(row)
    source = jnp.sum(jnp.concatenate(rows, axis=0), axis=1, keepdims=True) - 1.0
    source = jnp.broadcast_to(source, (64, 128))
    query = [q_ref[r].astype(F32) for r in range(4)]
    for j in range(64):
        s = jnp.broadcast_to(source[j : j + 1], (16, 128))
        picked = jnp.where(s == 1.0, query[1], query[0])
        picked = jnp.where(s == 2.0, query[2], picked)
        picked = jnp.where(s == 3.0, query[3], picked)
        send_ref[j] = picked.astype(BF16)
    group = iota((8, 128), 1) >> 4
    split = source.reshape(8, 8, 128)
    req = jnp.zeros((8, 128), F32)
    for n in range(8):
        req = jnp.where(group == n, split[:, n], req)
    req_ref[...] = req


def order_kernel(slot_ref, len_ref, k_ref, v_ref, keys_ref, values_ref, length_ref):
    group = iota((1, 128), 1) >> 4
    for g in range(8):
        row = jnp.zeros((1, 128), jnp.int32)
        for j in range(8):
            s = slot_ref[8 * g + j]
            keys_ref[8 * g + j] = k_ref[s]
            values_ref[8 * g + j] = v_ref[s]
            row = jnp.where(group == j, len_ref[s], row)
        length_ref[g : g + 1] = row


def slot_kernel(q_ref, k_ref, v_ref, length_ref, later_ref, out_ref):
    owner = iota((32, 128), 1) >> 4
    token = iota((32, 128), 0)
    row = iota((8, 128), 0)
    for g in range(8):
        here = pl.ds(8 * g, 8)
        raw = dot(k_ref[here].reshape(256, 128), q_ref[here].reshape(128, 128), NT)
        scores = raw[:32]
        for j in range(1, 8):
            scores = jnp.where(owner == j, raw[32 * j : 32 * j + 32], scores)
        scores = jnp.where(token < length_ref[g : g + 1], scores * SCALE, VERY_LOW)
        top = jnp.max(scores, axis=0, keepdims=True)
        weights = jnp.exp(scores - top)
        total = jnp.sum(weights, axis=0, keepdims=True)
        blocks = jnp.concatenate(
            [jnp.where(owner == j, weights, 0.0) for j in range(8)], axis=0
        ).astype(BF16)
        mixed = dot(blocks, v_ref[here].reshape(256, 128), TN)
        stats = jnp.zeros((8, 128), F32)
        for i, part in enumerate(thirds(top) + thirds(total)):
            stats = jnp.where(row == i, part, stats)
        for j in range(8):
            out_ref[8 * g + j] = jnp.concatenate(
                [mixed[16 * j : 16 * j + 16], stats], axis=0
            ).astype(BF16)


def home_kernel(
    len_ref, q_ref, nk_ref, nv_ref, k_ref, v_ref, residual_ref, out_ref, stat_ref, base_ref
):
    query = q_ref[...].reshape(64, 128)
    query = jnp.concatenate([query, query], axis=0)
    owner = (iota((256, 128), 1) >> 4) & 3
    token = iota((256, 128), 0)
    scores = jnp.zeros((256, 128), F32)
    length = jnp.zeros((256, 128), jnp.int32)
    for r in range(4):
        scores = jnp.where(owner == r, dot(k_ref[r], query, NT), scores)
        length = jnp.where(owner == r, len_ref[r], length)
    scores = jnp.where(token < length, scores * SCALE, VERY_LOW)
    mine = ((iota((4, 128), 1) >> 4) & 3) == iota((4, 128), 0)
    fresh = dot(nk_ref[...], query, NT) * SCALE
    fresh = jnp.sum(jnp.where(mine, fresh, 0.0), axis=0, keepdims=True)
    top = jnp.maximum(jnp.max(scores, axis=0, keepdims=True), fresh)
    weights = jnp.exp(scores - top)
    own = jnp.exp(fresh - top)
    total = jnp.sum(weights, axis=0, keepdims=True) + own
    mixed = dot(jnp.where(mine, own, 0.0).astype(BF16), nv_ref[...], TN)
    for r in range(4):
        mixed += dot(jnp.where(owner == r, weights, 0.0).astype(BF16), v_ref[r], TN)
    out_ref[...] = mixed[:64]
    stat_ref[...] = jnp.concatenate([top, total], axis=0)
    base_ref[...] = residual_ref[...].astype(F32)


def merge_kernel(me_ref, req_ref, stat_ref, home_ref, recv_ref, later_ref, out_ref):
    lane = iota((128, 128), 1)
    line = iota((128, 128), 0)
    spread = ((line >> 4) == (me_ref[0] & 7)) & ((line & 15) == (lane & 15))
    stats = recv_ref[:, 16:24, :].reshape(512, 128)
    stats = dot(stats, spread.astype(F32).astype(BF16), NN).reshape(8, 8, 8, 128)
    group = iota((8, 128), 1) >> 4
    far = jnp.zeros((8, 8, 128), F32)
    for n in range(8):
        far = far + jnp.where((group == n)[None], stats[:, n], 0.0)
    far_top = far[:, 0] + far[:, 1] + far[:, 2]
    far_total = far[:, 3] + far[:, 4] + far[:, 5]
    near_top, near_total = stat_ref[0:1], stat_ref[1:2]
    which = iota((1, 128), 1) >> 4
    req = req_ref[...]
    tops = []
    for r in range(4):
        t = jnp.max(jnp.where(req == r, far_top, VERY_LOW), axis=0, keepdims=True)
        tops.append(jnp.maximum(t, jnp.where(which == r, near_top, VERY_LOW)))
    peak = jnp.concatenate(tops, axis=0)
    for shift in (16, 32, 64):
        peak = jnp.maximum(peak, pltpu.roll(peak, shift, 1))
    far_w, near_w, totals = [], [], []
    for r in range(4):
        p = peak[r : r + 1]
        f = jnp.where(req == r, jnp.exp(far_top - p), 0.0)
        n = jnp.where(which == r, jnp.exp(near_top - p), 0.0)
        far_w.append(f)
        near_w.append(n)
        totals.append(jnp.sum(f * far_total, axis=0, keepdims=True) + n * near_total)
    total = jnp.concatenate(totals, axis=0)
    for shift in (16, 32, 64):
        total = total + pltpu.roll(total, shift, 1)
    scale = 1.0 / total
    same = (iota((16, 128), 1) & 15) == iota((16, 128), 0)

    def spread_rows(rows):
        return halves(jnp.concatenate([jnp.where(same, row, 0.0) for row in rows], axis=0))

    high, low = spread_rows([near_w[r] * scale[r : r + 1] for r in range(4)])
    home_high, home_low = halves(home_ref[...])
    acc = dot(high[:, :64], home_high, NN) + dot(high[:, :64], home_low, NN)
    acc += dot(low[:, :64], home_high, NN)
    far_w = [far_w[r] * scale[r : r + 1] for r in range(4)]
    for g in range(8):
        high, low = spread_rows([far_w[r][g : g + 1] for r in range(4)])
        block = recv_ref[8 * g : 8 * g + 8, :16, :].reshape(128, 128)
        acc += dot(high, block, NN) + dot(low, block, NN)
    out_ref[...] = jnp.broadcast_to(acc.astype(BF16)[None], (32, 64, 128))


def project_kernel(parity_ref, rows_ref, mine_ref, upper_ref, lower_ref, out_ref, wide_ref):
    q = iota((256, 256), 0)
    p = iota((256, 256), 1)
    move = p == 64 * ((q >> 2) & 3) + 16 * (q & 3) + (q >> 4)
    move = move.astype(F32).astype(BF16)
    for b in range(8):
        moved = dot(move, rows_ref[4 * b : 4 * b + 4].reshape(256, 128), NN).astype(BF16)
        for h in range(16):
            wide_ref[16 * b : 16 * b + 16, 128 * h : 128 * h + 128] = moved[16 * h : 16 * h + 16]
    parity = parity_ref[0]
    wide = wide_ref[...]
    out_ref[parity] = dot(wide, mine_ref[...], NN).astype(BF16).reshape(8, 16, 256)
    other = dot(wide[:, :1024], upper_ref[...], NN) + dot(wide[:, 1024:], lower_ref[...], NN)
    out_ref[1 - parity] = other.astype(BF16).reshape(8, 16, 256)


def body(
    queries,
    new_keys,
    new_values,
    home_keys,
    home_values,
    home_len,
    lent_keys,
    lent_values,
    lent_req,
    lent_len,
    out_weight,
    residual,
):
    here = lax.axis_index(INST)
    send, req = pl.pallas_call(
        ask_kernel,
        out_shape=(
            jax.ShapeDtypeStruct((64, 16, 128), BF16),
            jax.ShapeDtypeStruct((8, 128), F32),
        ),
        in_specs=[SMEM, VMEM, VMEM],
        out_specs=(VMEM, VMEM),
        compiler_params=PARAMS,
        name="ask_queries",
    )(here.reshape(1), jnp.pad(lent_req, (0, 64), constant_values=-4).reshape(32, 128), queries)
    asked = lax.all_to_all(send, INST, split_axis=0, concat_axis=0, tiled=True)
    swap = [(0, 1), (1, 0)]
    upper = lax.ppermute(out_weight[:1024], "zp", swap)
    lower = lax.ppermute(out_weight[1024:], "zp", swap)
    own = lax.dynamic_slice_in_dim(lent_req, here * 63, 63) >> 2
    order = jnp.arange(63, dtype=jnp.int32)
    every = jnp.arange(64, dtype=jnp.int32)
    slot_of = jnp.sum(jnp.where(own[None] == every[:, None], order[None], 0), axis=1)
    lent = jax.ShapeDtypeStruct((64, 32, 128), BF16)
    keys, values, length = pl.pallas_call(
        order_kernel,
        out_shape=(lent, lent, jax.ShapeDtypeStruct((8, 128), jnp.int32)),
        in_specs=[SMEM, SMEM, VMEM, VMEM],
        out_specs=(VMEM,) * 3,
        compiler_params=PARAMS,
        name="order_lent",
    )(slot_of, lent_len, lent_keys.reshape(63, 32, 128), lent_values.reshape(63, 32, 128))
    home_out, home_stat, base = pl.pallas_call(
        home_kernel,
        out_shape=(
            jax.ShapeDtypeStruct((64, 128), F32),
            jax.ShapeDtypeStruct((2, 128), F32),
            jax.ShapeDtypeStruct((32, 256), F32),
        ),
        in_specs=[SMEM] + [VMEM] * 6,
        out_specs=(VMEM,) * 3,
        compiler_params=PARAMS,
        name="home_part",
    )(
        home_len,
        queries,
        new_keys.reshape(4, 128),
        new_values.reshape(4, 128),
        home_keys.reshape(4, 256, 128),
        home_values.reshape(4, 256, 128),
        residual,
    )
    parts = pl.pallas_call(
        slot_kernel,
        out_shape=jax.ShapeDtypeStruct((64, 24, 128), BF16),
        in_specs=[VMEM] * 4 + [ANY],
        out_specs=VMEM,
        compiler_params=PARAMS,
        name="slot_part",
    )(asked, keys, values, length, upper)
    recv = lax.all_to_all(parts, INST, split_axis=0, concat_axis=0, tiled=True)
    copies = pl.pallas_call(
        merge_kernel,
        out_shape=jax.ShapeDtypeStruct((32, 64, 128), BF16),
        in_specs=[SMEM] + [VMEM] * 4 + [ANY],
        out_specs=VMEM,
        compiler_params=PARAMS,
        name="merge_parts",
    )(here.reshape(1), req, home_stat, home_out, recv, lower)
    rows = lax.all_to_all(copies, ("y", "zh"), split_axis=0, concat_axis=0, tiled=True)
    partial = pl.pallas_call(
        project_kernel,
        out_shape=jax.ShapeDtypeStruct((2, 8, 16, 256), BF16),
        in_specs=[SMEM] + [VMEM] * 4,
        out_specs=VMEM,
        scratch_shapes=[pltpu.VMEM((128, 2048), BF16)],
        compiler_params=PARAMS,
        name="project",
    )(lax.axis_index("zp").reshape(1), rows, out_weight, upper, lower)
    sums = lax.all_to_all(
        partial.reshape(16, 16, 256), ("zp", "tp"), split_axis=0, concat_axis=0, tiled=True
    )
    summed = jnp.sum(sums.reshape(2, 8, 4, 4, 256).astype(F32), axis=1)
    summed = summed.transpose(1, 0, 2, 3).reshape(32, 256)
    return (base + summed).astype(BF16)


def solution(mesh):
    placed = (
        P(INST, "tp", None),
        P(INST, "tp", None),
        P(INST, "tp", None),
        P(INST, None, "tp", None),
        P(INST, None, "tp", None),
        P(INST),
        P(INST, None, "tp", None),
        P(INST, None, "tp", None),
        P(),
        P(INST),
        P("tp", INST),
        P("tp", INST),
    )
    fine = Mesh(mesh.devices.reshape(8, 4, 2, 8), INST + ("tp",))
    return jax.shard_map(
        body, mesh=fine, in_specs=placed, out_specs=P("tp", INST), check_vma=False
    )
```

```python
import math

import jax
import jax.numpy as jnp
from jax import lax
from jax.experimental import pallas as pl
from jax.experimental.pallas import tpu as pltpu
from jax.sharding import Mesh, PartitionSpec as P

VERY_LOW = -1e30
SCALE = 1.0 / math.sqrt(128.0)
F32 = jnp.float32
BF16 = jnp.bfloat16
NT = (((1,), (1,)), ((), ()))
TN = (((0,), (0,)), ((), ()))
NN = (((1,), (0,)), ((), ()))
INST = ("y", "zh", "zp")
HALVES = [[8 * y + 2 * k + ((y + p) & 1) for y in range(8) for k in range(4)] for p in range(2)]
PARAMS = pltpu.CompilerParams(vmem_limit_bytes=16 * 2**20)
SMEM = pl.BlockSpec(memory_space=pltpu.SMEM)
VMEM = pl.BlockSpec(memory_space=pltpu.VMEM)


def dot(a, b, dims):
    return lax.dot_general(a, b, dims, preferred_element_type=F32)


def iota(shape, axis):
    return lax.broadcasted_iota(jnp.int32, shape, axis)


def thirds(x):
    high = x.astype(BF16).astype(F32)
    mid = (x - high).astype(BF16).astype(F32)
    return [high, mid, x - high - mid]


def halves(x):
    high = x.astype(BF16)
    return high, (x - high.astype(F32)).astype(BF16)


def ask_kernel(here_ref, table_ref, q_ref, send_ref, req_ref):
    here = here_ref[0]
    table = table_ref[...]
    found = jnp.where((table >> 2) == here, (table & 3) + 1, 0).astype(F32)
    lane = iota((1, 128), 1)
    rows = []
    for j in range(64):
        line, first = divmod(63 * j, 128)
        row = jnp.where(lane >= first, found[line : line + 1], 0.0)
        if first + 63 <= 128:
            row = jnp.where(lane < first + 63, row, 0.0)
        else:
            row = jnp.where(lane < first + 63 - 128, found[line + 1 : line + 2], row)
        rows.append(row)
    source = jnp.sum(jnp.concatenate(rows, axis=0), axis=1, keepdims=True) - 1.0
    source = jnp.broadcast_to(source, (64, 128))
    query = [q_ref[r].astype(F32) for r in range(4)]
    for j in range(64):
        s = jnp.broadcast_to(source[j : j + 1], (16, 128))
        picked = jnp.where(s == 1.0, query[1], query[0])
        picked = jnp.where(s == 2.0, query[2], picked)
        picked = jnp.where(s == 3.0, query[3], picked)
        send_ref[j] = picked.astype(BF16)
    group = iota((8, 128), 1) >> 4
    split = source.reshape(8, 8, 128)
    req = jnp.zeros((8, 128), F32)
    for n in range(8):
        req = jnp.where(group == n, split[:, n], req)
    req_ref[...] = req


def order_kernel(slot_ref, len_ref, k_ref, v_ref, keys_ref, values_ref, length_ref):
    group = iota((1, 128), 1) >> 4
    for g in range(8):
        row = jnp.zeros((1, 128), jnp.int32)
        for j in range(8):
            s = slot_ref[8 * g + j]
            keys_ref[8 * g + j] = k_ref[s]
            values_ref[8 * g + j] = v_ref[s]
            row = jnp.where(group == j, len_ref[s], row)
        length_ref[g : g + 1] = row


def slot_kernel(q_ref, k_ref, v_ref, length_ref, out_ref):
    owner = iota((32, 128), 1) >> 4
    token = iota((32, 128), 0)
    row = iota((8, 128), 0)
    for g in range(8):
        here = pl.ds(8 * g, 8)
        raw = dot(k_ref[here].reshape(256, 128), q_ref[here].reshape(128, 128), NT)
        scores = raw[:32]
        for j in range(1, 8):
            scores = jnp.where(owner == j, raw[32 * j : 32 * j + 32], scores)
        scores = jnp.where(token < length_ref[g : g + 1], scores * SCALE, VERY_LOW)
        top = jnp.max(scores, axis=0, keepdims=True)
        weights = jnp.exp(scores - top)
        total = jnp.sum(weights, axis=0, keepdims=True)
        blocks = jnp.concatenate(
            [jnp.where(owner == j, weights, 0.0) for j in range(8)], axis=0
        ).astype(BF16)
        mixed = dot(blocks, v_ref[here].reshape(256, 128), TN)
        stats = jnp.zeros((8, 128), F32)
        for i, part in enumerate(thirds(top) + thirds(total)):
            stats = jnp.where(row == i, part, stats)
        for j in range(8):
            out_ref[8 * g + j] = jnp.concatenate(
                [mixed[16 * j : 16 * j + 16], stats], axis=0
            ).astype(BF16)


def home_kernel(
    len_ref, q_ref, nk_ref, nv_ref, k_ref, v_ref, residual_ref, out_ref, stat_ref, base_ref
):
    query = q_ref[...].reshape(64, 128)
    query = jnp.concatenate([query, query], axis=0)
    owner = (iota((256, 128), 1) >> 4) & 3
    token = iota((256, 128), 0)
    scores = jnp.zeros((256, 128), F32)
    length = jnp.zeros((256, 128), jnp.int32)
    for r in range(4):
        scores = jnp.where(owner == r, dot(k_ref[r], query, NT), scores)
        length = jnp.where(owner == r, len_ref[r], length)
    scores = jnp.where(token < length, scores * SCALE, VERY_LOW)
    mine = ((iota((4, 128), 1) >> 4) & 3) == iota((4, 128), 0)
    fresh = dot(nk_ref[...], query, NT) * SCALE
    fresh = jnp.sum(jnp.where(mine, fresh, 0.0), axis=0, keepdims=True)
    top = jnp.maximum(jnp.max(scores, axis=0, keepdims=True), fresh)
    weights = jnp.exp(scores - top)
    own = jnp.exp(fresh - top)
    total = jnp.sum(weights, axis=0, keepdims=True) + own
    mixed = dot(jnp.where(mine, own, 0.0).astype(BF16), nv_ref[...], TN)
    for r in range(4):
        mixed += dot(jnp.where(owner == r, weights, 0.0).astype(BF16), v_ref[r], TN)
    out_ref[...] = mixed[:64]
    stat_ref[...] = jnp.concatenate([top, total], axis=0)
    base_ref[...] = residual_ref[...].astype(F32)


def merge_kernel(me_ref, req_ref, stat_ref, home_ref, recv_ref, out_ref):
    lane = iota((128, 128), 1)
    line = iota((128, 128), 0)
    spread = ((line >> 4) == (me_ref[0] & 7)) & ((line & 15) == (lane & 15))
    stats = recv_ref[:, 16:24, :].reshape(512, 128)
    stats = dot(stats, spread.astype(F32).astype(BF16), NN).reshape(8, 8, 8, 128)
    group = iota((8, 128), 1) >> 4
    far = jnp.zeros((8, 8, 128), F32)
    for n in range(8):
        far = far + jnp.where((group == n)[None], stats[:, n], 0.0)
    far_top = far[:, 0] + far[:, 1] + far[:, 2]
    far_total = far[:, 3] + far[:, 4] + far[:, 5]
    near_top, near_total = stat_ref[0:1], stat_ref[1:2]
    which = iota((1, 128), 1) >> 4
    req = req_ref[...]
    tops = []
    for r in range(4):
        t = jnp.max(jnp.where(req == r, far_top, VERY_LOW), axis=0, keepdims=True)
        tops.append(jnp.maximum(t, jnp.where(which == r, near_top, VERY_LOW)))
    peak = jnp.concatenate(tops, axis=0)
    for shift in (16, 32, 64):
        peak = jnp.maximum(peak, pltpu.roll(peak, shift, 1))
    far_w, near_w, totals = [], [], []
    for r in range(4):
        p = peak[r : r + 1]
        f = jnp.where(req == r, jnp.exp(far_top - p), 0.0)
        n = jnp.where(which == r, jnp.exp(near_top - p), 0.0)
        far_w.append(f)
        near_w.append(n)
        totals.append(jnp.sum(f * far_total, axis=0, keepdims=True) + n * near_total)
    total = jnp.concatenate(totals, axis=0)
    for shift in (16, 32, 64):
        total = total + pltpu.roll(total, shift, 1)
    scale = 1.0 / total
    same = (iota((16, 128), 1) & 15) == iota((16, 128), 0)

    def spread_rows(rows):
        return halves(jnp.concatenate([jnp.where(same, row, 0.0) for row in rows], axis=0))

    high, low = spread_rows([near_w[r] * scale[r : r + 1] for r in range(4)])
    home_high, home_low = halves(home_ref[...])
    acc = dot(high[:, :64], home_high, NN) + dot(high[:, :64], home_low, NN)
    acc += dot(low[:, :64], home_high, NN)
    far_w = [far_w[r] * scale[r : r + 1] for r in range(4)]
    for g in range(8):
        high, low = spread_rows([far_w[r][g : g + 1] for r in range(4)])
        block = recv_ref[8 * g : 8 * g + 8, :16, :].reshape(128, 128)
        acc += dot(high, block, NN) + dot(low, block, NN)
    out_ref[...] = jnp.broadcast_to(acc.astype(BF16)[None], (32, 64, 128))


def project_kernel(parity_ref, rows_ref, mine_ref, other_ref, out_ref, wide_ref):
    q = iota((256, 256), 0)
    p = iota((256, 256), 1)
    move = p == 64 * ((q >> 2) & 3) + 16 * (q & 3) + (q >> 4)
    move = move.astype(F32).astype(BF16)
    for b in range(8):
        moved = dot(move, rows_ref[4 * b : 4 * b + 4].reshape(256, 128), NN).astype(BF16)
        for h in range(16):
            wide_ref[16 * b : 16 * b + 16, 128 * h : 128 * h + 128] = moved[16 * h : 16 * h + 16]
    parity = parity_ref[0]
    wide = wide_ref[...]
    out_ref[parity] = dot(wide, mine_ref[...], NN).astype(BF16).reshape(8, 16, 256)
    out_ref[1 - parity] = dot(wide, other_ref[...], NN).astype(BF16).reshape(8, 16, 256)


def finish_kernel(turn_ref, sums_ref, base_ref, out_ref):
    turn = turn_ref[0]
    rows = []
    for parity in range(2):
        total = jnp.zeros((16, 256), F32)
        for t in range(8):
            total = total + sums_ref[8 * (turn ^ parity) + t].astype(F32)
        rows.append(total)
    rows = jnp.concatenate(
        [rows[z & 1][4 * (z >> 1) : 4 * (z >> 1) + 4] for z in range(8)], axis=0
    )
    out_ref[...] = (base_ref[...] + rows).astype(BF16)


def body(
    queries,
    new_keys,
    new_values,
    home_keys,
    home_values,
    home_len,
    lent_keys,
    lent_values,
    lent_req,
    lent_len,
    out_weight,
    residual,
):
    here = lax.axis_index(INST)
    send, req = pl.pallas_call(
        ask_kernel,
        out_shape=(
            jax.ShapeDtypeStruct((64, 16, 128), BF16),
            jax.ShapeDtypeStruct((8, 128), F32),
        ),
        in_specs=[SMEM, VMEM, VMEM],
        out_specs=(VMEM, VMEM),
        compiler_params=PARAMS,
        name="ask_queries",
    )(here.reshape(1), jnp.pad(lent_req, (0, 64), constant_values=-4).reshape(32, 128), queries)
    asked = lax.all_to_all(send, INST, split_axis=0, concat_axis=0, tiled=True)
    other_weight = lax.ppermute(out_weight, "zp", [(0, 1), (1, 0)])
    own = lax.dynamic_slice_in_dim(lent_req, here * 63, 63) >> 2
    order = jnp.arange(63, dtype=jnp.int32)
    every = jnp.arange(64, dtype=jnp.int32)
    slot_of = jnp.sum(jnp.where(own[None] == every[:, None], order[None], 0), axis=1)
    lent = jax.ShapeDtypeStruct((64, 32, 128), BF16)
    keys, values, length = pl.pallas_call(
        order_kernel,
        out_shape=(lent, lent, jax.ShapeDtypeStruct((8, 128), jnp.int32)),
        in_specs=[SMEM, SMEM, VMEM, VMEM],
        out_specs=(VMEM,) * 3,
        compiler_params=PARAMS,
        name="order_lent",
    )(slot_of, lent_len, lent_keys.reshape(63, 32, 128), lent_values.reshape(63, 32, 128))
    home_out, home_stat, base = pl.pallas_call(
        home_kernel,
        out_shape=(
            jax.ShapeDtypeStruct((64, 128), F32),
            jax.ShapeDtypeStruct((2, 128), F32),
            jax.ShapeDtypeStruct((32, 256), F32),
        ),
        in_specs=[SMEM] + [VMEM] * 6,
        out_specs=(VMEM,) * 3,
        compiler_params=PARAMS,
        name="home_part",
    )(
        home_len,
        queries,
        new_keys.reshape(4, 128),
        new_values.reshape(4, 128),
        home_keys.reshape(4, 256, 128),
        home_values.reshape(4, 256, 128),
        residual,
    )
    parts = pl.pallas_call(
        slot_kernel,
        out_shape=jax.ShapeDtypeStruct((64, 24, 128), BF16),
        in_specs=[VMEM] * 4,
        out_specs=VMEM,
        compiler_params=PARAMS,
        name="slot_part",
    )(asked, keys, values, length)
    recv = lax.all_to_all(parts, INST, split_axis=0, concat_axis=0, tiled=True)
    copies = pl.pallas_call(
        merge_kernel,
        out_shape=jax.ShapeDtypeStruct((32, 64, 128), BF16),
        in_specs=[SMEM] + [VMEM] * 4,
        out_specs=VMEM,
        compiler_params=PARAMS,
        name="merge_parts",
    )(here.reshape(1), req, home_stat, home_out, recv)
    rows = lax.all_to_all(
        copies, INST, split_axis=0, concat_axis=0, tiled=True, axis_index_groups=HALVES
    )
    partial = pl.pallas_call(
        project_kernel,
        out_shape=jax.ShapeDtypeStruct((2, 8, 16, 256), BF16),
        in_specs=[SMEM] + [VMEM] * 3,
        out_specs=VMEM,
        scratch_shapes=[pltpu.VMEM((128, 2048), BF16)],
        compiler_params=PARAMS,
        name="project",
    )(lax.axis_index("zp").reshape(1), rows, out_weight, other_weight)
    sums = lax.all_to_all(
        partial.reshape(16, 16, 256), ("zp", "tp"), split_axis=0, concat_axis=0, tiled=True
    )
    turn = (lax.axis_index("tp") + lax.axis_index("y")) & 1
    return pl.pallas_call(
        finish_kernel,
        out_shape=jax.ShapeDtypeStruct((32, 256), BF16),
        in_specs=[SMEM, VMEM, VMEM],
        out_specs=VMEM,
        compiler_params=PARAMS,
        name="finish",
    )(turn.reshape(1), sums, base)


def solution(mesh):
    placed = (
        P(INST, "tp", None),
        P(INST, "tp", None),
        P(INST, "tp", None),
        P(INST, None, "tp", None),
        P(INST, None, "tp", None),
        P(INST),
        P(INST, None, "tp", None),
        P(INST, None, "tp", None),
        P(),
        P(INST),
        P("tp", INST),
        P("tp", INST),
    )
    fine = Mesh(mesh.devices.reshape(8, 4, 2, 8), INST + ("tp",))
    return jax.shard_map(
        body, mesh=fine, in_specs=placed, out_specs=P("tp", INST), check_vma=False
    )
```

```python
import math

import jax
import jax.numpy as jnp
from jax import lax
from jax.experimental import pallas as pl
from jax.experimental.pallas import tpu as pltpu
from jax.sharding import Mesh, PartitionSpec as P

VERY_LOW = -1e30
ABSENT = 64.0
SCALE = 1.0 / math.sqrt(128.0)
F32 = jnp.float32
BF16 = jnp.bfloat16
NT = (((1,), (1,)), ((), ()))
TN = (((0,), (0,)), ((), ()))
NN = (((1,), (0,)), ((), ()))
INST = ("y", "zh", "zp")
HALVES = [[8 * y + 2 * k + ((y + p) & 1) for y in range(8) for k in range(4)] for p in range(2)]
PARAMS = pltpu.CompilerParams(vmem_limit_bytes=16 * 2**20)
SMEM = pl.BlockSpec(memory_space=pltpu.SMEM)
VMEM = pl.BlockSpec(memory_space=pltpu.VMEM)


def dot(a, b, dims):
    return lax.dot_general(a, b, dims, preferred_element_type=F32)


def iota(shape, axis):
    return lax.broadcasted_iota(jnp.int32, shape, axis)


def halves(x):
    high = x.astype(BF16)
    return high, (x - high.astype(F32)).astype(BF16)


def ask_kernel(here_ref, table_ref, q_ref, asked_ref, req_ref):
    here = here_ref[0]
    table = table_ref[...]
    found = jnp.where((table >> 2) == here, (table & 3) + 1, 0).astype(F32)
    lane = iota((1, 128), 1)
    rows = []
    for j in range(64):
        line, first = divmod(63 * j, 128)
        row = jnp.where(lane >= first, found[line : line + 1], 0.0)
        if first + 63 <= 128:
            row = jnp.where(lane < first + 63, row, 0.0)
        else:
            row = jnp.where(lane < first + 63 - 128, found[line + 1 : line + 2], row)
        rows.append(row)
    source = jnp.sum(jnp.concatenate(rows, axis=0), axis=1, keepdims=True) - 1.0
    source = jnp.broadcast_to(source, (64, 128))
    query = [q_ref[r].astype(F32) for r in range(4)]
    for j in range(64):
        s = jnp.broadcast_to(source[j : j + 1], (16, 128))
        picked = jnp.where(s == 1.0, query[1], query[0])
        picked = jnp.where(s == 2.0, query[2], picked)
        picked = jnp.where(s == 3.0, query[3], picked)
        asked_ref[j] = picked.astype(BF16)
    group = iota((8, 128), 1) >> 4
    split = source.reshape(8, 8, 128)
    req = jnp.zeros((8, 128), F32)
    for n in range(8):
        req = jnp.where(group == n, split[:, n], req)
    req_ref[...] = req


def pack_kernel(here_ref, req_ref, len_ref, k_ref, v_ref, out_ref):
    here = here_ref[0]
    token = iota((32, 128), 0)
    out_ref[here, :32] = jnp.full((32, 128), ABSENT, F32).astype(BF16)
    out_ref[here, 32:] = jnp.zeros((32, 128), F32).astype(BF16)
    for s in range(63):
        home = req_ref[63 * here + s] >> 2
        keys = jnp.where(token < len_ref[s], k_ref[s].astype(F32), ABSENT)
        out_ref[home, :32] = keys.astype(BF16)
        out_ref[home, 32:] = v_ref[s]


def home_kernel(
    len_ref, q_ref, nk_ref, nv_ref, k_ref, v_ref, residual_ref, out_ref, stat_ref, base_ref
):
    query = q_ref[...].reshape(64, 128)
    query = jnp.concatenate([query, query], axis=0)
    owner = (iota((256, 128), 1) >> 4) & 3
    token = iota((256, 128), 0)
    scores = jnp.zeros((256, 128), F32)
    length = jnp.zeros((256, 128), jnp.int32)
    for r in range(4):
        scores = jnp.where(owner == r, dot(k_ref[r], query, NT), scores)
        length = jnp.where(owner == r, len_ref[r], length)
    scores = jnp.where(token < length, scores * SCALE, VERY_LOW)
    mine = ((iota((4, 128), 1) >> 4) & 3) == iota((4, 128), 0)
    fresh = dot(nk_ref[...], query, NT) * SCALE
    fresh = jnp.sum(jnp.where(mine, fresh, 0.0), axis=0, keepdims=True)
    top = jnp.maximum(jnp.max(scores, axis=0, keepdims=True), fresh)
    weights = jnp.exp(scores - top)
    own = jnp.exp(fresh - top)
    total = jnp.sum(weights, axis=0, keepdims=True) + own
    mixed = dot(jnp.where(mine, own, 0.0).astype(BF16), nv_ref[...], TN)
    for r in range(4):
        mixed += dot(jnp.where(owner == r, weights, 0.0).astype(BF16), v_ref[r], TN)
    out_ref[...] = mixed[:64]
    stat_ref[...] = jnp.concatenate([top, total], axis=0)
    base_ref[...] = residual_ref[...].astype(F32)


def attend_kernel(q_ref, req_ref, stat_ref, home_ref, recv_ref, out_ref, mixed_ref):
    owner = iota((32, 128), 1) >> 4
    far_tops, far_totals = [], []
    for g in range(8):
        here = pl.ds(8 * g, 8)
        keys = recv_ref[here, :32, :].reshape(256, 128)
        raw = dot(keys, q_ref[here].reshape(128, 128), NT)
        mark = keys[:, :1].astype(F32)
        scores, marks = raw[:32], jnp.broadcast_to(mark[:32], (32, 128))
        for j in range(1, 8):
            scores = jnp.where(owner == j, raw[32 * j : 32 * j + 32], scores)
            marks = jnp.where(owner == j, mark[32 * j : 32 * j + 32], marks)
        scores = jnp.where(marks < 0.5 * ABSENT, scores * SCALE, VERY_LOW)
        top = jnp.max(scores, axis=0, keepdims=True)
        weights = jnp.exp(scores - top)
        far_tops.append(top)
        far_totals.append(jnp.sum(weights, axis=0, keepdims=True))
        blocks = jnp.concatenate(
            [jnp.where(owner == j, weights, 0.0) for j in range(8)], axis=0
        ).astype(BF16)
        values = recv_ref[here, 32:, :].reshape(256, 128)
        mixed_ref[128 * g : 128 * g + 128] = dot(blocks, values, TN)
    far_top = jnp.concatenate(far_tops, axis=0)
    far_total = jnp.concatenate(far_totals, axis=0)
    near_top, near_total = stat_ref[0:1], stat_ref[1:2]
    which = iota((1, 128), 1) >> 4
    req = req_ref[...]
    tops = []
    for r in range(4):
        t = jnp.max(jnp.where(req == r, far_top, VERY_LOW), axis=0, keepdims=True)
        tops.append(jnp.maximum(t, jnp.where(which == r, near_top, VERY_LOW)))
    peak = jnp.concatenate(tops, axis=0)
    for shift in (16, 32, 64):
        peak = jnp.maximum(peak, pltpu.roll(peak, shift, 1))
    far_w, near_w, totals = [], [], []
    for r in range(4):
        p = peak[r : r + 1]
        f = jnp.where(req == r, jnp.exp(far_top - p), 0.0)
        n = jnp.where(which == r, jnp.exp(near_top - p), 0.0)
        far_w.append(f)
        near_w.append(n)
        totals.append(jnp.sum(f * far_total, axis=0, keepdims=True) + n * near_total)
    total = jnp.concatenate(totals, axis=0)
    for shift in (16, 32, 64):
        total = total + pltpu.roll(total, shift, 1)
    scale = 1.0 / total
    same = (iota((16, 128), 1) & 15) == iota((16, 128), 0)

    def spread_rows(rows):
        return halves(jnp.concatenate([jnp.where(same, row, 0.0) for row in rows], axis=0))

    high, low = spread_rows([near_w[r] * scale[r : r + 1] for r in range(4)])
    home_high, home_low = halves(home_ref[...])
    acc = dot(high[:, :64], home_high, NN) + dot(high[:, :64], home_low, NN)
    acc += dot(low[:, :64], home_high, NN)
    far_w = [far_w[r] * scale[r : r + 1] for r in range(4)]
    for g in range(8):
        high, low = spread_rows([far_w[r][g : g + 1] for r in range(4)])
        mixed_high, mixed_low = halves(mixed_ref[128 * g : 128 * g + 128])
        acc += dot(high, mixed_high, NN) + dot(high, mixed_low, NN) + dot(low, mixed_high, NN)
    out_ref[...] = jnp.broadcast_to(acc.astype(BF16)[None], (32, 64, 128))


def project_kernel(parity_ref, rows_ref, mine_ref, other_ref, out_ref, wide_ref):
    q = iota((256, 256), 0)
    p = iota((256, 256), 1)
    move = p == 64 * ((q >> 2) & 3) + 16 * (q & 3) + (q >> 4)
    move = move.astype(F32).astype(BF16)
    for b in range(8):
        moved = dot(move, rows_ref[4 * b : 4 * b + 4].reshape(256, 128), NN).astype(BF16)
        for h in range(16):
            wide_ref[16 * b : 16 * b + 16, 128 * h : 128 * h + 128] = moved[16 * h : 16 * h + 16]
    parity = parity_ref[0]
    wide = wide_ref[...]
    out_ref[parity] = dot(wide, mine_ref[...], NN).astype(BF16).reshape(8, 16, 256)
    out_ref[1 - parity] = dot(wide, other_ref[...], NN).astype(BF16).reshape(8, 16, 256)


def finish_kernel(turn_ref, sums_ref, base_ref, out_ref):
    turn = turn_ref[0]
    rows = []
    for parity in range(2):
        total = jnp.zeros((16, 256), F32)
        for t in range(8):
            total = total + sums_ref[8 * (turn ^ parity) + t].astype(F32)
        rows.append(total)
    rows = jnp.concatenate(
        [rows[z & 1][4 * (z >> 1) : 4 * (z >> 1) + 4] for z in range(8)], axis=0
    )
    out_ref[...] = (base_ref[...] + rows).astype(BF16)


def body(
    queries,
    new_keys,
    new_values,
    home_keys,
    home_values,
    home_len,
    lent_keys,
    lent_values,
    lent_req,
    lent_len,
    out_weight,
    residual,
):
    here = lax.axis_index(INST)
    packed = pl.pallas_call(
        pack_kernel,
        out_shape=jax.ShapeDtypeStruct((64, 64, 128), BF16),
        in_specs=[SMEM] * 3 + [VMEM] * 2,
        out_specs=VMEM,
        compiler_params=PARAMS,
        name="pack_lent",
    )(
        here.reshape(1),
        lent_req,
        lent_len,
        lent_keys.reshape(63, 32, 128),
        lent_values.reshape(63, 32, 128),
    )
    recv = lax.all_to_all(packed, INST, split_axis=0, concat_axis=0, tiled=True)
    other_weight = lax.ppermute(out_weight, "zp", [(0, 1), (1, 0)])
    asked, req = pl.pallas_call(
        ask_kernel,
        out_shape=(
            jax.ShapeDtypeStruct((64, 16, 128), BF16),
            jax.ShapeDtypeStruct((8, 128), F32),
        ),
        in_specs=[SMEM, VMEM, VMEM],
        out_specs=(VMEM, VMEM),
        compiler_params=PARAMS,
        name="ask_queries",
    )(here.reshape(1), jnp.pad(lent_req, (0, 64), constant_values=-4).reshape(32, 128), queries)
    home_out, home_stat, base = pl.pallas_call(
        home_kernel,
        out_shape=(
            jax.ShapeDtypeStruct((64, 128), F32),
            jax.ShapeDtypeStruct((2, 128), F32),
            jax.ShapeDtypeStruct((32, 256), F32),
        ),
        in_specs=[SMEM] + [VMEM] * 6,
        out_specs=(VMEM,) * 3,
        compiler_params=PARAMS,
        name="home_part",
    )(
        home_len,
        queries,
        new_keys.reshape(4, 128),
        new_values.reshape(4, 128),
        home_keys.reshape(4, 256, 128),
        home_values.reshape(4, 256, 128),
        residual,
    )
    copies = pl.pallas_call(
        attend_kernel,
        out_shape=jax.ShapeDtypeStruct((32, 64, 128), BF16),
        in_specs=[VMEM] * 5,
        out_specs=VMEM,
        scratch_shapes=[pltpu.VMEM((1024, 128), F32)],
        compiler_params=PARAMS,
        name="attend",
    )(asked, req, home_stat, home_out, recv)
    rows = lax.all_to_all(
        copies, INST, split_axis=0, concat_axis=0, tiled=True, axis_index_groups=HALVES
    )
    partial = pl.pallas_call(
        project_kernel,
        out_shape=jax.ShapeDtypeStruct((2, 8, 16, 256), BF16),
        in_specs=[SMEM] + [VMEM] * 3,
        out_specs=VMEM,
        scratch_shapes=[pltpu.VMEM((128, 2048), BF16)],
        compiler_params=PARAMS,
        name="project",
    )(lax.axis_index("zp").reshape(1), rows, out_weight, other_weight)
    sums = lax.all_to_all(
        partial.reshape(16, 16, 256), ("zp", "tp"), split_axis=0, concat_axis=0, tiled=True
    )
    turn = (lax.axis_index("tp") + lax.axis_index("y")) & 1
    return pl.pallas_call(
        finish_kernel,
        out_shape=jax.ShapeDtypeStruct((32, 256), BF16),
        in_specs=[SMEM, VMEM, VMEM],
        out_specs=VMEM,
        compiler_params=PARAMS,
        name="finish",
    )(turn.reshape(1), sums, base)


def solution(mesh):
    placed = (
        P(INST, "tp", None),
        P(INST, "tp", None),
        P(INST, "tp", None),
        P(INST, None, "tp", None),
        P(INST, None, "tp", None),
        P(INST),
        P(INST, None, "tp", None),
        P(INST, None, "tp", None),
        P(),
        P(INST),
        P("tp", INST),
        P("tp", INST),
    )
    fine = Mesh(mesh.devices.reshape(8, 4, 2, 8), INST + ("tp",))
    return jax.shard_map(
        body, mesh=fine, in_specs=placed, out_specs=P("tp", INST), check_vma=False
    )
```

```python
import math

import jax
import jax.numpy as jnp
from jax import lax
from jax.experimental import pallas as pl
from jax.experimental.pallas import tpu as pltpu
from jax.sharding import Mesh, PartitionSpec as P

VERY_LOW = -1e30
ABSENT = 64.0
SCALE = 1.0 / math.sqrt(128.0)
F32 = jnp.float32
BF16 = jnp.bfloat16
NT = (((1,), (1,)), ((), ()))
TN = (((0,), (0,)), ((), ()))
NN = (((1,), (0,)), ((), ()))
INST = ("y", "zh", "zp")
HALVES = [[8 * y + 2 * k + ((y + p) & 1) for y in range(8) for k in range(4)] for p in range(2)]
PARAMS = pltpu.CompilerParams(vmem_limit_bytes=16 * 2**20)
SMEM = pl.BlockSpec(memory_space=pltpu.SMEM)
ANY = pl.BlockSpec(memory_space=pl.ANY)
VMEM = pl.BlockSpec(memory_space=pltpu.VMEM)


def dot(a, b, dims):
    return lax.dot_general(a, b, dims, preferred_element_type=F32)


def iota(shape, axis):
    return lax.broadcasted_iota(jnp.int32, shape, axis)


def halves(x):
    high = x.astype(BF16)
    return high, (x - high.astype(F32)).astype(BF16)


def ask_kernel(here_ref, table_ref, q_ref, asked_ref, req_ref):
    here = here_ref[0]
    table = table_ref[...]
    found = jnp.where((table >> 2) == here, (table & 3) + 1, 0).astype(F32)
    lane = iota((1, 128), 1)
    rows = []
    for j in range(64):
        line, first = divmod(63 * j, 128)
        row = jnp.where(lane >= first, found[line : line + 1], 0.0)
        if first + 63 <= 128:
            row = jnp.where(lane < first + 63, row, 0.0)
        else:
            row = jnp.where(lane < first + 63 - 128, found[line + 1 : line + 2], row)
        rows.append(row)
    source = jnp.sum(jnp.concatenate(rows, axis=0), axis=1, keepdims=True) - 1.0
    source = jnp.broadcast_to(source, (64, 128))
    query = [q_ref[r].astype(F32) for r in range(4)]
    for j in range(64):
        s = jnp.broadcast_to(source[j : j + 1], (16, 128))
        picked = jnp.where(s == 1.0, query[1], query[0])
        picked = jnp.where(s == 2.0, query[2], picked)
        picked = jnp.where(s == 3.0, query[3], picked)
        asked_ref[j] = picked.astype(BF16)
    group = iota((8, 128), 1) >> 4
    split = source.reshape(8, 8, 128)
    req = jnp.zeros((8, 128), F32)
    for n in range(8):
        req = jnp.where(group == n, split[:, n], req)
    req_ref[...] = req


def pack_kernel(here_ref, req_ref, len_ref, k_ref, v_ref, out_ref, keys_ref, values_ref, sems):
    here = here_ref[0]
    token = iota((32, 128), 0)
    keys_ref[here] = jnp.full((32, 128), ABSENT, F32).astype(BF16)
    for s in range(63):
        keys = jnp.where(token < len_ref[s], k_ref[s].astype(F32), ABSENT)
        keys_ref[req_ref[63 * here + s] >> 2] = keys.astype(BF16)
    send_keys = pltpu.make_async_copy(keys_ref, out_ref.at[:, pl.ds(0, 32)], sems.at[0])
    send_keys.start()
    values_ref[here] = jnp.zeros((32, 128), F32).astype(BF16)
    for s in range(63):
        values_ref[req_ref[63 * here + s] >> 2] = v_ref[s]
    send_values = pltpu.make_async_copy(values_ref, out_ref.at[:, pl.ds(32, 32)], sems.at[1])
    send_values.start()
    send_keys.wait()
    send_values.wait()


def home_kernel(
    len_ref, q_ref, nk_ref, nv_ref, k_ref, v_ref, residual_ref, out_ref, stat_ref, base_ref
):
    query = q_ref[...].reshape(64, 128)
    query = jnp.concatenate([query, query], axis=0)
    owner = (iota((256, 128), 1) >> 4) & 3
    token = iota((256, 128), 0)
    scores = jnp.zeros((256, 128), F32)
    length = jnp.zeros((256, 128), jnp.int32)
    for r in range(4):
        scores = jnp.where(owner == r, dot(k_ref[r], query, NT), scores)
        length = jnp.where(owner == r, len_ref[r], length)
    scores = jnp.where(token < length, scores * SCALE, VERY_LOW)
    mine = ((iota((4, 128), 1) >> 4) & 3) == iota((4, 128), 0)
    fresh = dot(nk_ref[...], query, NT) * SCALE
    fresh = jnp.sum(jnp.where(mine, fresh, 0.0), axis=0, keepdims=True)
    top = jnp.maximum(jnp.max(scores, axis=0, keepdims=True), fresh)
    weights = jnp.exp(scores - top)
    own = jnp.exp(fresh - top)
    total = jnp.sum(weights, axis=0, keepdims=True) + own
    mixed = dot(jnp.where(mine, own, 0.0).astype(BF16), nv_ref[...], TN)
    for r in range(4):
        mixed += dot(jnp.where(owner == r, weights, 0.0).astype(BF16), v_ref[r], TN)
    out_ref[...] = mixed[:64]
    stat_ref[...] = jnp.concatenate([top, total], axis=0)
    base_ref[...] = residual_ref[...].astype(F32)


def attend_kernel(q_ref, req_ref, stat_ref, home_ref, recv_ref, later_ref, out_ref, mixed_ref):
    owner = iota((32, 128), 1) >> 4
    far_tops, far_totals = [], []
    for g in range(8):
        here = pl.ds(8 * g, 8)
        keys = recv_ref[here, :32, :].reshape(256, 128)
        raw = dot(keys, q_ref[here].reshape(128, 128), NT)
        mark = keys.astype(F32)
        scores, marks = raw[:32], mark[:32]
        for j in range(1, 8):
            scores = jnp.where(owner == j, raw[32 * j : 32 * j + 32], scores)
            marks = jnp.where(owner == j, mark[32 * j : 32 * j + 32], marks)
        scores = jnp.where(marks < 0.5 * ABSENT, scores * SCALE, VERY_LOW)
        top = jnp.max(scores, axis=0, keepdims=True)
        weights = jnp.exp(scores - top)
        far_tops.append(top)
        far_totals.append(jnp.sum(weights, axis=0, keepdims=True))
        blocks = jnp.concatenate(
            [jnp.where(owner == j, weights, 0.0) for j in range(8)], axis=0
        ).astype(BF16)
        values = recv_ref[here, 32:, :].reshape(256, 128)
        mixed_ref[128 * g : 128 * g + 128] = dot(blocks, values, TN)
    far_top = jnp.concatenate(far_tops, axis=0)
    far_total = jnp.concatenate(far_totals, axis=0)
    near_top, near_total = stat_ref[0:1], stat_ref[1:2]
    which = iota((1, 128), 1) >> 4
    req = req_ref[...]
    tops = []
    for r in range(4):
        t = jnp.max(jnp.where(req == r, far_top, VERY_LOW), axis=0, keepdims=True)
        tops.append(jnp.maximum(t, jnp.where(which == r, near_top, VERY_LOW)))
    peak = jnp.concatenate(tops, axis=0)
    for shift in (16, 32, 64):
        peak = jnp.maximum(peak, pltpu.roll(peak, shift, 1))
    far_w, near_w, totals = [], [], []
    for r in range(4):
        p = peak[r : r + 1]
        f = jnp.where(req == r, jnp.exp(far_top - p), 0.0)
        n = jnp.where(which == r, jnp.exp(near_top - p), 0.0)
        far_w.append(f)
        near_w.append(n)
        totals.append(jnp.sum(f * far_total, axis=0, keepdims=True) + n * near_total)
    total = jnp.concatenate(totals, axis=0)
    for shift in (16, 32, 64):
        total = total + pltpu.roll(total, shift, 1)
    scale = 1.0 / total
    same = (iota((16, 128), 1) & 15) == iota((16, 128), 0)

    def spread_rows(rows):
        return halves(jnp.concatenate([jnp.where(same, row, 0.0) for row in rows], axis=0))

    high, low = spread_rows([near_w[r] * scale[r : r + 1] for r in range(4)])
    home_high, home_low = halves(home_ref[...])
    acc = dot(high[:, :64], home_high, NN) + dot(high[:, :64], home_low, NN)
    acc += dot(low[:, :64], home_high, NN)
    far_w = [far_w[r] * scale[r : r + 1] for r in range(4)]
    for g in range(8):
        high, low = spread_rows([far_w[r][g : g + 1] for r in range(4)])
        mixed_high, mixed_low = halves(mixed_ref[128 * g : 128 * g + 128])
        acc += dot(high, mixed_high, NN) + dot(high, mixed_low, NN) + dot(low, mixed_high, NN)
    out_ref[...] = jnp.broadcast_to(acc.astype(BF16)[None], (32, 64, 128))


def project_kernel(parity_ref, rows_ref, mine_ref, other_ref, out_ref, wide_ref):
    q = iota((256, 256), 0)
    p = iota((256, 256), 1)
    move = p == 64 * ((q >> 2) & 3) + 16 * (q & 3) + (q >> 4)
    move = move.astype(F32).astype(BF16)
    for b in range(8):
        moved = dot(move, rows_ref[4 * b : 4 * b + 4].reshape(256, 128), NN).astype(BF16)
        for h in range(16):
            wide_ref[16 * b : 16 * b + 16, 128 * h : 128 * h + 128] = moved[16 * h : 16 * h + 16]
    parity = parity_ref[0]
    wide = wide_ref[...]
    out_ref[parity] = dot(wide, mine_ref[...], NN).astype(BF16).reshape(8, 16, 256)
    out_ref[1 - parity] = dot(wide, other_ref[...], NN).astype(BF16).reshape(8, 16, 256)


def finish_kernel(turn_ref, sums_ref, base_ref, out_ref):
    turn = turn_ref[0]
    rows = []
    for parity in range(2):
        total = jnp.zeros((16, 256), F32)
        for t in range(8):
            total = total + sums_ref[8 * (turn ^ parity) + t].astype(F32)
        rows.append(total)
    rows = jnp.concatenate(
        [rows[z & 1][4 * (z >> 1) : 4 * (z >> 1) + 4] for z in range(8)], axis=0
    )
    out_ref[...] = (base_ref[...] + rows).astype(BF16)


def body(
    queries,
    new_keys,
    new_values,
    home_keys,
    home_values,
    home_len,
    lent_keys,
    lent_values,
    lent_req,
    lent_len,
    out_weight,
    residual,
):
    here = lax.axis_index(INST)
    packed = pl.pallas_call(
        pack_kernel,
        out_shape=jax.ShapeDtypeStruct((64, 64, 128), BF16),
        in_specs=[SMEM] * 3 + [VMEM] * 2,
        out_specs=ANY,
        scratch_shapes=[
            pltpu.VMEM((64, 32, 128), BF16),
            pltpu.VMEM((64, 32, 128), BF16),
            pltpu.SemaphoreType.DMA((2,)),
        ],
        compiler_params=PARAMS,
        name="pack_lent",
    )(
        here.reshape(1),
        lent_req,
        lent_len,
        lent_keys.reshape(63, 32, 128),
        lent_values.reshape(63, 32, 128),
    )
    recv = lax.all_to_all(packed, INST, split_axis=0, concat_axis=0, tiled=True)
    other_weight = lax.ppermute(out_weight, "zp", [(0, 1), (1, 0)])
    asked, req = pl.pallas_call(
        ask_kernel,
        out_shape=(
            jax.ShapeDtypeStruct((64, 16, 128), BF16),
            jax.ShapeDtypeStruct((8, 128), F32),
        ),
        in_specs=[SMEM, VMEM, VMEM],
        out_specs=(VMEM, VMEM),
        compiler_params=PARAMS,
        name="ask_queries",
    )(here.reshape(1), jnp.pad(lent_req, (0, 64), constant_values=-4).reshape(32, 128), queries)
    home_out, home_stat, base = pl.pallas_call(
        home_kernel,
        out_shape=(
            jax.ShapeDtypeStruct((64, 128), F32),
            jax.ShapeDtypeStruct((2, 128), F32),
            jax.ShapeDtypeStruct((32, 256), F32),
        ),
        in_specs=[SMEM] + [VMEM] * 6,
        out_specs=(VMEM,) * 3,
        compiler_params=PARAMS,
        name="home_part",
    )(
        home_len,
        queries,
        new_keys.reshape(4, 128),
        new_values.reshape(4, 128),
        home_keys.reshape(4, 256, 128),
        home_values.reshape(4, 256, 128),
        residual,
    )
    copies = pl.pallas_call(
        attend_kernel,
        out_shape=jax.ShapeDtypeStruct((32, 64, 128), BF16),
        in_specs=[VMEM] * 5 + [ANY],
        out_specs=VMEM,
        scratch_shapes=[pltpu.VMEM((1024, 128), F32)],
        compiler_params=PARAMS,
        name="attend",
    )(asked, req, home_stat, home_out, recv, other_weight)
    rows = lax.all_to_all(
        copies, INST, split_axis=0, concat_axis=0, tiled=True, axis_index_groups=HALVES
    )
    partial = pl.pallas_call(
        project_kernel,
        out_shape=jax.ShapeDtypeStruct((2, 8, 16, 256), BF16),
        in_specs=[SMEM] + [VMEM] * 3,
        out_specs=VMEM,
        scratch_shapes=[pltpu.VMEM((128, 2048), BF16)],
        compiler_params=PARAMS,
        name="project",
    )(lax.axis_index("zp").reshape(1), rows, out_weight, other_weight)
    sums = lax.all_to_all(
        partial.reshape(16, 16, 256), ("zp", "tp"), split_axis=0, concat_axis=0, tiled=True
    )
    turn = (lax.axis_index("tp") + lax.axis_index("y")) & 1
    return pl.pallas_call(
        finish_kernel,
        out_shape=jax.ShapeDtypeStruct((32, 256), BF16),
        in_specs=[SMEM, VMEM, VMEM],
        out_specs=VMEM,
        compiler_params=PARAMS,
        name="finish",
    )(turn.reshape(1), sums, base)


def solution(mesh):
    placed = (
        P(INST, "tp", None),
        P(INST, "tp", None),
        P(INST, "tp", None),
        P(INST, None, "tp", None),
        P(INST, None, "tp", None),
        P(INST),
        P(INST, None, "tp", None),
        P(INST, None, "tp", None),
        P(),
        P(INST),
        P("tp", INST),
        P("tp", INST),
    )
    fine = Mesh(mesh.devices.reshape(8, 4, 2, 8), INST + ("tp",))
    return jax.shard_map(
        body, mesh=fine, in_specs=placed, out_specs=P("tp", INST), check_vma=False
    )
```

```python
import math

import jax
import jax.numpy as jnp
from jax import lax
from jax.experimental import pallas as pl
from jax.experimental.pallas import tpu as pltpu
from jax.sharding import PartitionSpec as P

VERY_LOW = -1e30
ABSENT = 64.0
SCALE = 1.0 / math.sqrt(128.0)
F32 = jnp.float32
BF16 = jnp.bfloat16
NT = (((1,), (1,)), ((), ()))
TN = (((0,), (0,)), ((), ()))
NN = (((1,), (0,)), ((), ()))
INST = "inst"
PARAMS = pltpu.CompilerParams(vmem_limit_bytes=16 * 2**20)
SMEM = pl.BlockSpec(memory_space=pltpu.SMEM)
ANY = pl.BlockSpec(memory_space=pl.ANY)
VMEM = pl.BlockSpec(memory_space=pltpu.VMEM)


def dot(a, b, dims):
    return lax.dot_general(a, b, dims, preferred_element_type=F32)


def iota(shape, axis):
    return lax.broadcasted_iota(jnp.int32, shape, axis)


def halves(x):
    high = x.astype(BF16)
    return high, (x - high.astype(F32)).astype(BF16)


def ask_kernel(here_ref, table_ref, q_ref, asked_ref, req_ref):
    here = here_ref[0]
    table = table_ref[...]
    found = jnp.where((table >> 2) == here, (table & 3) + 1, 0).astype(F32)
    lane = iota((1, 128), 1)
    rows = []
    for j in range(64):
        line, first = divmod(63 * j, 128)
        row = jnp.where(lane >= first, found[line : line + 1], 0.0)
        if first + 63 <= 128:
            row = jnp.where(lane < first + 63, row, 0.0)
        else:
            row = jnp.where(lane < first + 63 - 128, found[line + 1 : line + 2], row)
        rows.append(row)
    source = jnp.sum(jnp.concatenate(rows, axis=0), axis=1, keepdims=True) - 1.0
    source = jnp.broadcast_to(source, (64, 128))
    query = [q_ref[r].astype(F32) for r in range(4)]
    for j in range(64):
        s = jnp.broadcast_to(source[j : j + 1], (16, 128))
        picked = jnp.where(s == 1.0, query[1], query[0])
        picked = jnp.where(s == 2.0, query[2], picked)
        picked = jnp.where(s == 3.0, query[3], picked)
        asked_ref[j] = picked.astype(BF16)
    group = iota((8, 128), 1) >> 4
    split = source.reshape(8, 8, 128)
    req = jnp.zeros((8, 128), F32)
    for n in range(8):
        req = jnp.where(group == n, split[:, n], req)
    req_ref[...] = req


def pack_kernel(here_ref, req_ref, len_ref, k_ref, v_ref, out_ref, keys_ref, values_ref, sems):
    here = here_ref[0]
    token = iota((32, 128), 0)
    keys_ref[here] = jnp.full((32, 128), ABSENT, F32).astype(BF16)
    for s in range(63):
        keys = jnp.where(token < len_ref[s], k_ref[s].astype(F32), ABSENT)
        keys_ref[req_ref[63 * here + s] >> 2] = keys.astype(BF16)
    send_keys = pltpu.make_async_copy(keys_ref, out_ref.at[:, pl.ds(0, 32)], sems.at[0])
    send_keys.start()
    values_ref[here] = jnp.zeros((32, 128), F32).astype(BF16)
    for s in range(63):
        values_ref[req_ref[63 * here + s] >> 2] = v_ref[s]
    send_values = pltpu.make_async_copy(values_ref, out_ref.at[:, pl.ds(32, 32)], sems.at[1])
    send_values.start()
    send_keys.wait()
    send_values.wait()


def home_kernel(
    len_ref, q_ref, nk_ref, nv_ref, k_ref, v_ref, residual_ref, out_ref, stat_ref, base_ref
):
    query = q_ref[...].reshape(64, 128)
    query = jnp.concatenate([query, query], axis=0)
    owner = (iota((256, 128), 1) >> 4) & 3
    token = iota((256, 128), 0)
    scores = jnp.zeros((256, 128), F32)
    length = jnp.zeros((256, 128), jnp.int32)
    for r in range(4):
        scores = jnp.where(owner == r, dot(k_ref[r], query, NT), scores)
        length = jnp.where(owner == r, len_ref[r], length)
    scores = jnp.where(token < length, scores * SCALE, VERY_LOW)
    mine = ((iota((4, 128), 1) >> 4) & 3) == iota((4, 128), 0)
    fresh = dot(nk_ref[...], query, NT) * SCALE
    fresh = jnp.sum(jnp.where(mine, fresh, 0.0), axis=0, keepdims=True)
    top = jnp.maximum(jnp.max(scores, axis=0, keepdims=True), fresh)
    weights = jnp.exp(scores - top)
    own = jnp.exp(fresh - top)
    total = jnp.sum(weights, axis=0, keepdims=True) + own
    mixed = dot(jnp.where(mine, own, 0.0).astype(BF16), nv_ref[...], TN)
    for r in range(4):
        mixed += dot(jnp.where(owner == r, weights, 0.0).astype(BF16), v_ref[r], TN)
    out_ref[...] = mixed[:64]
    stat_ref[...] = jnp.concatenate([top, total], axis=0)
    base_ref[...] = residual_ref[...].astype(F32)


def attend_kernel(q_ref, req_ref, stat_ref, home_ref, recv_ref, out_ref, mixed_ref):
    owner = iota((32, 128), 1) >> 4
    far_tops, far_totals = [], []
    for g in range(8):
        here = pl.ds(8 * g, 8)
        keys = recv_ref[here, :32, :].reshape(256, 128)
        raw = dot(keys, q_ref[here].reshape(128, 128), NT)
        mark = keys.astype(F32)
        scores, marks = raw[:32], mark[:32]
        for j in range(1, 8):
            scores = jnp.where(owner == j, raw[32 * j : 32 * j + 32], scores)
            marks = jnp.where(owner == j, mark[32 * j : 32 * j + 32], marks)
        scores = jnp.where(marks < 0.5 * ABSENT, scores * SCALE, VERY_LOW)
        top = jnp.max(scores, axis=0, keepdims=True)
        weights = jnp.exp(scores - top)
        far_tops.append(top)
        far_totals.append(jnp.sum(weights, axis=0, keepdims=True))
        blocks = jnp.concatenate(
            [jnp.where(owner == j, weights, 0.0) for j in range(8)], axis=0
        ).astype(BF16)
        values = recv_ref[here, 32:, :].reshape(256, 128)
        mixed_ref[128 * g : 128 * g + 128] = dot(blocks, values, TN)
    far_top = jnp.concatenate(far_tops, axis=0)
    far_total = jnp.concatenate(far_totals, axis=0)
    near_top, near_total = stat_ref[0:1], stat_ref[1:2]
    which = iota((1, 128), 1) >> 4
    req = req_ref[...]
    tops = []
    for r in range(4):
        t = jnp.max(jnp.where(req == r, far_top, VERY_LOW), axis=0, keepdims=True)
        tops.append(jnp.maximum(t, jnp.where(which == r, near_top, VERY_LOW)))
    peak = jnp.concatenate(tops, axis=0)
    for shift in (16, 32, 64):
        peak = jnp.maximum(peak, pltpu.roll(peak, shift, 1))
    far_w, near_w, totals = [], [], []
    for r in range(4):
        p = peak[r : r + 1]
        f = jnp.where(req == r, jnp.exp(far_top - p), 0.0)
        n = jnp.where(which == r, jnp.exp(near_top - p), 0.0)
        far_w.append(f)
        near_w.append(n)
        totals.append(jnp.sum(f * far_total, axis=0, keepdims=True) + n * near_total)
    total = jnp.concatenate(totals, axis=0)
    for shift in (16, 32, 64):
        total = total + pltpu.roll(total, shift, 1)
    scale = 1.0 / total
    same = (iota((16, 128), 1) & 15) == iota((16, 128), 0)

    def spread_rows(rows):
        return halves(jnp.concatenate([jnp.where(same, row, 0.0) for row in rows], axis=0))

    high, low = spread_rows([near_w[r] * scale[r : r + 1] for r in range(4)])
    home_high, home_low = halves(home_ref[...])
    acc = dot(high[:, :64], home_high, NN) + dot(high[:, :64], home_low, NN)
    acc += dot(low[:, :64], home_high, NN)
    far_w = [far_w[r] * scale[r : r + 1] for r in range(4)]
    for g in range(8):
        high, low = spread_rows([far_w[r][g : g + 1] for r in range(4)])
        mixed_high, mixed_low = halves(mixed_ref[128 * g : 128 * g + 128])
        acc += dot(high, mixed_high, NN) + dot(high, mixed_low, NN) + dot(low, mixed_high, NN)
    out_ref[...] = jnp.broadcast_to(acc.astype(BF16)[None], (64, 64, 128))


def project_kernel(rows_ref, weight_ref, out_ref, wide_ref):
    q = iota((256, 256), 0)
    p = iota((256, 256), 1)
    move = p == 64 * ((q >> 2) & 3) + 16 * (q & 3) + (q >> 4)
    move = move.astype(F32).astype(BF16)
    for b in range(16):
        moved = dot(move, rows_ref[4 * b : 4 * b + 4].reshape(256, 128), NN).astype(BF16)
        for h in range(16):
            wide_ref[16 * b : 16 * b + 16, 128 * h : 128 * h + 128] = moved[16 * h : 16 * h + 16]
    out_ref[...] = dot(wide_ref[...], weight_ref[...], NN).astype(BF16).reshape(8, 32, 256)


def finish_kernel(sums_ref, base_ref, out_ref):
    total = base_ref[...]
    for t in range(8):
        total = total + sums_ref[t].astype(F32)
    out_ref[...] = total.astype(BF16)


def body(
    queries,
    new_keys,
    new_values,
    home_keys,
    home_values,
    home_len,
    lent_keys,
    lent_values,
    lent_req,
    lent_len,
    out_weight,
    residual,
):
    here = lax.axis_index(INST)
    packed = pl.pallas_call(
        pack_kernel,
        out_shape=jax.ShapeDtypeStruct((64, 64, 128), BF16),
        in_specs=[SMEM] * 3 + [VMEM] * 2,
        out_specs=ANY,
        scratch_shapes=[
            pltpu.VMEM((64, 32, 128), BF16),
            pltpu.VMEM((64, 32, 128), BF16),
            pltpu.SemaphoreType.DMA((2,)),
        ],
        compiler_params=PARAMS,
        name="pack_lent",
    )(
        here.reshape(1),
        lent_req,
        lent_len,
        lent_keys.reshape(63, 32, 128),
        lent_values.reshape(63, 32, 128),
    )
    recv = lax.all_to_all(packed, INST, split_axis=0, concat_axis=0, tiled=True)
    asked, req = pl.pallas_call(
        ask_kernel,
        out_shape=(
            jax.ShapeDtypeStruct((64, 16, 128), BF16),
            jax.ShapeDtypeStruct((8, 128), F32),
        ),
        in_specs=[SMEM, VMEM, VMEM],
        out_specs=(VMEM, VMEM),
        compiler_params=PARAMS,
        name="ask_queries",
    )(here.reshape(1), jnp.pad(lent_req, (0, 64), constant_values=-4).reshape(32, 128), queries)
    home_out, home_stat, base = pl.pallas_call(
        home_kernel,
        out_shape=(
            jax.ShapeDtypeStruct((64, 128), F32),
            jax.ShapeDtypeStruct((2, 128), F32),
            jax.ShapeDtypeStruct((32, 256), F32),
        ),
        in_specs=[SMEM] + [VMEM] * 6,
        out_specs=(VMEM,) * 3,
        compiler_params=PARAMS,
        name="home_part",
    )(
        home_len,
        queries,
        new_keys.reshape(4, 128),
        new_values.reshape(4, 128),
        home_keys.reshape(4, 256, 128),
        home_values.reshape(4, 256, 128),
        residual,
    )
    copies = pl.pallas_call(
        attend_kernel,
        out_shape=jax.ShapeDtypeStruct((64, 64, 128), BF16),
        in_specs=[VMEM] * 5,
        out_specs=VMEM,
        scratch_shapes=[pltpu.VMEM((1024, 128), F32)],
        compiler_params=PARAMS,
        name="attend",
    )(asked, req, home_stat, home_out, recv)
    rows = lax.all_to_all(copies, INST, split_axis=0, concat_axis=0, tiled=True)
    partial = pl.pallas_call(
        project_kernel,
        out_shape=jax.ShapeDtypeStruct((8, 32, 256), BF16),
        in_specs=[VMEM] * 2,
        out_specs=VMEM,
        scratch_shapes=[pltpu.VMEM((256, 2048), BF16)],
        compiler_params=PARAMS,
        name="project",
    )(rows, out_weight)
    sums = lax.all_to_all(partial, "tp", split_axis=0, concat_axis=0, tiled=True)
    return pl.pallas_call(
        finish_kernel,
        out_shape=jax.ShapeDtypeStruct((32, 256), BF16),
        in_specs=[VMEM, VMEM],
        out_specs=VMEM,
        compiler_params=PARAMS,
        name="finish",
    )(sums, base)


def solution(mesh):
    placed = (
        P(INST, "tp", None),
        P(INST, "tp", None),
        P(INST, "tp", None),
        P(INST, None, "tp", None),
        P(INST, None, "tp", None),
        P(INST),
        P(INST, None, "tp", None),
        P(INST, None, "tp", None),
        P(),
        P(INST),
        P("tp", INST),
        P("tp", INST),
    )
    return jax.shard_map(
        body, mesh=mesh, in_specs=placed, out_specs=P("tp", INST), check_vma=False
    )
```

```python
import math

import jax
import jax.numpy as jnp
from jax import lax
from jax.experimental import pallas as pl
from jax.experimental.pallas import tpu as pltpu
from jax.sharding import Mesh, PartitionSpec as P

VERY_LOW = -1e30
ABSENT = 64.0
SCALE = 1.0 / math.sqrt(128.0)
F32 = jnp.float32
BF16 = jnp.bfloat16
NT = (((1,), (1,)), ((), ()))
TN = (((0,), (0,)), ((), ()))
NN = (((1,), (0,)), ((), ()))
INST = ("y", "zh", "zp")
HALVES = [[8 * y + 2 * k + ((y + p) & 1) for y in range(8) for k in range(4)] for p in range(2)]
PARAMS = pltpu.CompilerParams(vmem_limit_bytes=16 * 2**20)
SMEM = pl.BlockSpec(memory_space=pltpu.SMEM)
ANY = pl.BlockSpec(memory_space=pl.ANY)
VMEM = pl.BlockSpec(memory_space=pltpu.VMEM)


def dot(a, b, dims):
    return lax.dot_general(a, b, dims, preferred_element_type=F32)


def iota(shape, axis):
    return lax.broadcasted_iota(jnp.int32, shape, axis)


def halves(x):
    high = x.astype(BF16)
    return high, (x - high.astype(F32)).astype(BF16)


def ask_kernel(
    here_ref, table_ref, q_ref, weight_ref, done_ref, asked_ref, req_ref, upper_ref, lower_ref
):
    upper_ref[...] = weight_ref[:1024]
    lower_ref[...] = weight_ref[1024:]
    here = here_ref[0]
    table = table_ref[...]
    found = jnp.where((table >> 2) == here, (table & 3) + 1, 0).astype(F32)
    lane = iota((1, 128), 1)
    rows = []
    for j in range(64):
        line, first = divmod(63 * j, 128)
        row = jnp.where(lane >= first, found[line : line + 1], 0.0)
        if first + 63 <= 128:
            row = jnp.where(lane < first + 63, row, 0.0)
        else:
            row = jnp.where(lane < first + 63 - 128, found[line + 1 : line + 2], row)
        rows.append(row)
    source = jnp.sum(jnp.concatenate(rows, axis=0), axis=1, keepdims=True) - 1.0
    source = jnp.broadcast_to(source, (64, 128))
    query = [q_ref[r].astype(F32) for r in range(4)]
    for j in range(64):
        s = jnp.broadcast_to(source[j : j + 1], (16, 128))
        picked = jnp.where(s == 1.0, query[1], query[0])
        picked = jnp.where(s == 2.0, query[2], picked)
        picked = jnp.where(s == 3.0, query[3], picked)
        asked_ref[j] = picked.astype(BF16)
    group = iota((8, 128), 1) >> 4
    split = source.reshape(8, 8, 128)
    req = jnp.zeros((8, 128), F32)
    for n in range(8):
        req = jnp.where(group == n, split[:, n], req)
    req_ref[...] = req


def pack_kernel(
    req_ref, len_ref, k_ref, v_ref, out_ref, done_ref,
    req_in, len_in, k_in, v_in, keys_ref, values_ref, sems
):
    loads = [
        pltpu.make_async_copy(source, target, sems.at[i])
        for i, (source, target) in enumerate(
            [(req_ref, req_in), (len_ref, len_in), (k_ref, k_in), (v_ref, v_in)]
        )
    ]
    for load in loads:
        load.start()
    here = (lax.axis_index("y") * 4 + lax.axis_index("zh")) * 2 + lax.axis_index("zp")
    token = iota((32, 128), 0)
    keys_ref[here] = jnp.full((32, 128), ABSENT, F32).astype(BF16)
    values_ref[here] = jnp.zeros((32, 128), F32).astype(BF16)
    done_ref[...] = jnp.zeros((8, 128), F32)
    for load in loads[:3]:
        load.wait()
    for s in range(63):
        keys = jnp.where(token < len_in[s], k_in[s].astype(F32), ABSENT)
        keys_ref[req_in[63 * here + s] >> 2] = keys.astype(BF16)
    send_keys = pltpu.make_async_copy(keys_ref, out_ref.at[:, pl.ds(0, 32)], sems.at[4])
    send_keys.start()
    loads[3].wait()
    for s in range(63):
        values_ref[req_in[63 * here + s] >> 2] = v_in[s]
    send_values = pltpu.make_async_copy(values_ref, out_ref.at[:, pl.ds(32, 32)], sems.at[5])
    send_values.start()
    send_keys.wait()
    send_values.wait()


def home_kernel(
    len_ref, q_ref, nk_ref, nv_ref, k_ref, v_ref, residual_ref, out_ref, stat_ref, base_ref
):
    query = q_ref[...].reshape(64, 128)
    query = jnp.concatenate([query, query], axis=0)
    owner = (iota((256, 128), 1) >> 4) & 3
    token = iota((256, 128), 0)
    scores = jnp.zeros((256, 128), F32)
    length = jnp.zeros((256, 128), jnp.int32)
    for r in range(4):
        scores = jnp.where(owner == r, dot(k_ref[r], query, NT), scores)
        length = jnp.where(owner == r, len_ref[r], length)
    scores = jnp.where(token < length, scores * SCALE, VERY_LOW)
    mine = ((iota((4, 128), 1) >> 4) & 3) == iota((4, 128), 0)
    fresh = dot(nk_ref[...], query, NT) * SCALE
    fresh = jnp.sum(jnp.where(mine, fresh, 0.0), axis=0, keepdims=True)
    top = jnp.maximum(jnp.max(scores, axis=0, keepdims=True), fresh)
    weights = jnp.exp(scores - top)
    own = jnp.exp(fresh - top)
    total = jnp.sum(weights, axis=0, keepdims=True) + own
    mixed = dot(jnp.where(mine, own, 0.0).astype(BF16), nv_ref[...], TN)
    for r in range(4):
        mixed += dot(jnp.where(owner == r, weights, 0.0).astype(BF16), v_ref[r], TN)
    out_ref[...] = mixed[:64]
    stat_ref[...] = jnp.concatenate([top, total], axis=0)
    base_ref[...] = residual_ref[...].astype(F32)


def attend_kernel(q_ref, req_ref, stat_ref, home_ref, recv_ref, out_ref, mixed_ref):
    owner = iota((32, 128), 1) >> 4
    far_tops, far_totals = [], []
    for g in range(8):
        here = pl.ds(8 * g, 8)
        keys = recv_ref[here, :32, :].reshape(256, 128)
        raw = dot(keys, q_ref[here].reshape(128, 128), NT)
        mark = keys.astype(F32)
        scores, marks = raw[:32], mark[:32]
        for j in range(1, 8):
            scores = jnp.where(owner == j, raw[32 * j : 32 * j + 32], scores)
            marks = jnp.where(owner == j, mark[32 * j : 32 * j + 32], marks)
        scores = jnp.where(marks < 0.5 * ABSENT, scores * SCALE, VERY_LOW)
        top = jnp.max(scores, axis=0, keepdims=True)
        weights = jnp.exp(scores - top)
        far_tops.append(top)
        far_totals.append(jnp.sum(weights, axis=0, keepdims=True))
        blocks = jnp.concatenate(
            [jnp.where(owner == j, weights, 0.0) for j in range(8)], axis=0
        ).astype(BF16)
        values = recv_ref[here, 32:, :].reshape(256, 128)
        mixed_ref[128 * g : 128 * g + 128] = dot(blocks, values, TN)
    far_top = jnp.concatenate(far_tops, axis=0)
    far_total = jnp.concatenate(far_totals, axis=0)
    near_top, near_total = stat_ref[0:1], stat_ref[1:2]
    which = iota((1, 128), 1) >> 4
    req = req_ref[...]
    tops = []
    for r in range(4):
        t = jnp.max(jnp.where(req == r, far_top, VERY_LOW), axis=0, keepdims=True)
        tops.append(jnp.maximum(t, jnp.where(which == r, near_top, VERY_LOW)))
    peak = jnp.concatenate(tops, axis=0)
    for shift in (16, 32, 64):
        peak = jnp.maximum(peak, pltpu.roll(peak, shift, 1))
    far_w, near_w, totals = [], [], []
    for r in range(4):
        p = peak[r : r + 1]
        f = jnp.where(req == r, jnp.exp(far_top - p), 0.0)
        n = jnp.where(which == r, jnp.exp(near_top - p), 0.0)
        far_w.append(f)
        near_w.append(n)
        totals.append(jnp.sum(f * far_total, axis=0, keepdims=True) + n * near_total)
    total = jnp.concatenate(totals, axis=0)
    for shift in (16, 32, 64):
        total = total + pltpu.roll(total, shift, 1)
    scale = 1.0 / total
    same = (iota((16, 128), 1) & 15) == iota((16, 128), 0)

    def spread_rows(rows):
        return halves(jnp.concatenate([jnp.where(same, row, 0.0) for row in rows], axis=0))

    high, low = spread_rows([near_w[r] * scale[r : r + 1] for r in range(4)])
    home_high, home_low = halves(home_ref[...])
    acc = dot(high[:, :64], home_high, NN) + dot(high[:, :64], home_low, NN)
    acc += dot(low[:, :64], home_high, NN)
    far_w = [far_w[r] * scale[r : r + 1] for r in range(4)]
    for g in range(8):
        high, low = spread_rows([far_w[r][g : g + 1] for r in range(4)])
        mixed_high, mixed_low = halves(mixed_ref[128 * g : 128 * g + 128])
        acc += dot(high, mixed_high, NN) + dot(high, mixed_low, NN) + dot(low, mixed_high, NN)
    out_ref[...] = jnp.broadcast_to(acc.astype(BF16)[None], (32, 64, 128))


def project_kernel(parity_ref, rows_ref, mine_ref, upper_ref, lower_ref, out_ref, wide_ref):
    q = iota((256, 256), 0)
    p = iota((256, 256), 1)
    move = p == 64 * ((q >> 2) & 3) + 16 * (q & 3) + (q >> 4)
    move = move.astype(F32).astype(BF16)
    for b in range(8):
        moved = dot(move, rows_ref[4 * b : 4 * b + 4].reshape(256, 128), NN).astype(BF16)
        for h in range(16):
            wide_ref[16 * b : 16 * b + 16, 128 * h : 128 * h + 128] = moved[16 * h : 16 * h + 16]
    parity = parity_ref[0]
    wide = wide_ref[...]
    out_ref[parity] = dot(wide, mine_ref[...], NN).astype(BF16).reshape(8, 16, 256)
    other = dot(wide[:, :1024], upper_ref[...], NN) + dot(wide[:, 1024:], lower_ref[...], NN)
    out_ref[1 - parity] = other.astype(BF16).reshape(8, 16, 256)


def finish_kernel(turn_ref, sums_ref, base_ref, out_ref):
    turn = turn_ref[0]
    rows = []
    for parity in range(2):
        total = jnp.zeros((16, 256), F32)
        for t in range(8):
            total = total + sums_ref[8 * (turn ^ parity) + t].astype(F32)
        rows.append(total)
    rows = jnp.concatenate(
        [rows[z & 1][4 * (z >> 1) : 4 * (z >> 1) + 4] for z in range(8)], axis=0
    )
    out_ref[...] = (base_ref[...] + rows).astype(BF16)


def body(
    queries,
    new_keys,
    new_values,
    home_keys,
    home_values,
    home_len,
    lent_keys,
    lent_values,
    lent_req,
    lent_len,
    out_weight,
    residual,
):
    here = lax.axis_index(INST)
    packed, done = pl.pallas_call(
        pack_kernel,
        out_shape=(
            jax.ShapeDtypeStruct((64, 64, 128), BF16),
            jax.ShapeDtypeStruct((8, 128), F32),
        ),
        in_specs=[ANY] * 4,
        out_specs=(ANY, VMEM),
        scratch_shapes=[
            pltpu.SMEM((4032,), jnp.int32),
            pltpu.SMEM((63,), jnp.int32),
            pltpu.VMEM((63, 32, 128), BF16),
            pltpu.VMEM((63, 32, 128), BF16),
            pltpu.VMEM((64, 32, 128), BF16),
            pltpu.VMEM((64, 32, 128), BF16),
            pltpu.SemaphoreType.DMA((6,)),
        ],
        name="pack_lent",
    )(
        lent_req,
        lent_len,
        lent_keys.reshape(63, 32, 128),
        lent_values.reshape(63, 32, 128),
    )
    recv = lax.all_to_all(packed, INST, split_axis=0, concat_axis=0, tiled=True)
    weight_half = jax.ShapeDtypeStruct((1024, 256), BF16)
    asked, req, upper, lower = pl.pallas_call(
        ask_kernel,
        out_shape=(
            jax.ShapeDtypeStruct((64, 16, 128), BF16),
            jax.ShapeDtypeStruct((8, 128), F32),
            weight_half,
            weight_half,
        ),
        in_specs=[SMEM, VMEM, VMEM, VMEM, ANY],
        out_specs=(VMEM,) * 4,
        compiler_params=PARAMS,
        name="ask_queries",
    )(
        here.reshape(1),
        jnp.pad(lent_req, (0, 64), constant_values=-4).reshape(32, 128),
        queries,
        out_weight,
        done,
    )
    swap = [(0, 1), (1, 0)]
    upper = lax.ppermute(upper, "zp", swap)
    lower = lax.ppermute(lower, "zp", swap)
    home_out, home_stat, base = pl.pallas_call(
        home_kernel,
        out_shape=(
            jax.ShapeDtypeStruct((64, 128), F32),
            jax.ShapeDtypeStruct((2, 128), F32),
            jax.ShapeDtypeStruct((32, 256), F32),
        ),
        in_specs=[SMEM] + [VMEM] * 6,
        out_specs=(VMEM,) * 3,
        compiler_params=PARAMS,
        name="home_part",
    )(
        home_len,
        queries,
        new_keys.reshape(4, 128),
        new_values.reshape(4, 128),
        home_keys.reshape(4, 256, 128),
        home_values.reshape(4, 256, 128),
        residual,
    )
    copies = pl.pallas_call(
        attend_kernel,
        out_shape=jax.ShapeDtypeStruct((32, 64, 128), BF16),
        in_specs=[VMEM] * 5,
        out_specs=VMEM,
        scratch_shapes=[pltpu.VMEM((1024, 128), F32)],
        compiler_params=PARAMS,
        name="attend",
    )(asked, req, home_stat, home_out, recv)
    rows = lax.all_to_all(
        copies, INST, split_axis=0, concat_axis=0, tiled=True, axis_index_groups=HALVES
    )
    partial = pl.pallas_call(
        project_kernel,
        out_shape=jax.ShapeDtypeStruct((2, 8, 16, 256), BF16),
        in_specs=[SMEM] + [VMEM] * 4,
        out_specs=VMEM,
        scratch_shapes=[pltpu.VMEM((128, 2048), BF16)],
        compiler_params=PARAMS,
        name="project",
    )(lax.axis_index("zp").reshape(1), rows, out_weight, upper, lower)
    sums = lax.all_to_all(
        partial.reshape(16, 16, 256), ("zp", "tp"), split_axis=0, concat_axis=0, tiled=True
    )
    turn = (lax.axis_index("tp") + lax.axis_index("y")) & 1
    return pl.pallas_call(
        finish_kernel,
        out_shape=jax.ShapeDtypeStruct((32, 256), BF16),
        in_specs=[SMEM, VMEM, VMEM],
        out_specs=VMEM,
        compiler_params=PARAMS,
        name="finish",
    )(turn.reshape(1), sums, base)


def solution(mesh):
    placed = (
        P(INST, "tp", None),
        P(INST, "tp", None),
        P(INST, "tp", None),
        P(INST, None, "tp", None),
        P(INST, None, "tp", None),
        P(INST),
        P(INST, None, "tp", None),
        P(INST, None, "tp", None),
        P(),
        P(INST),
        P("tp", INST),
        P("tp", INST),
    )
    fine = Mesh(mesh.devices.reshape(8, 4, 2, 8), INST + ("tp",))
    return jax.shard_map(
        body, mesh=fine, in_specs=placed, out_specs=P("tp", INST), check_vma=False
    )
```

```python
import math

import jax
import jax.numpy as jnp
from jax import lax
from jax.experimental import pallas as pl
from jax.experimental.pallas import tpu as pltpu
from jax.sharding import PartitionSpec as P

VERY_LOW = -1e30
ABSENT = 64.0
RAISE = 4096.0
SCALE = 1.0 / math.sqrt(128.0)
F32 = jnp.float32
BF16 = jnp.bfloat16
NT = (((1,), (1,)), ((), ()))
TN = (((0,), (0,)), ((), ()))
NN = (((1,), (0,)), ((), ()))
INST = "inst"
PARAMS = pltpu.CompilerParams(vmem_limit_bytes=16 * 2**20)
SMEM = pl.BlockSpec(memory_space=pltpu.SMEM)
ANY = pl.BlockSpec(memory_space=pl.ANY)
VMEM = pl.BlockSpec(memory_space=pltpu.VMEM)


def dot(a, b, dims):
    return lax.dot_general(a, b, dims, preferred_element_type=F32)


def iota(shape, axis):
    return lax.broadcasted_iota(jnp.int32, shape, axis)


def halves(x):
    high = x.astype(BF16)
    return high, (x - high.astype(F32)).astype(BF16)


def ask_kernel(here_ref, table_ref, q_ref, asked_ref, req_ref):
    here = here_ref[0]
    table = table_ref[...]
    found = jnp.where((table >> 2) == here, (table & 3) + 1, 0).astype(F32)
    lane = iota((1, 128), 1)
    rows = []
    for j in range(64):
        line, first = divmod(63 * j, 128)
        row = jnp.where(lane >= first, found[line : line + 1], 0.0)
        if first + 63 <= 128:
            row = jnp.where(lane < first + 63, row, 0.0)
        else:
            row = jnp.where(lane < first + 63 - 128, found[line + 1 : line + 2], row)
        rows.append(row)
    source = jnp.sum(jnp.concatenate(rows, axis=0), axis=1, keepdims=True) - 1.0
    source = jnp.broadcast_to(source, (64, 128))
    query = [q_ref[r].astype(F32) for r in range(4)]
    for j in range(64):
        s = jnp.broadcast_to(source[j : j + 1], (16, 128))
        picked = jnp.where(s == 1.0, query[1], query[0])
        picked = jnp.where(s == 2.0, query[2], picked)
        picked = jnp.where(s == 3.0, query[3], picked)
        asked_ref[j] = picked.astype(BF16)
    group = iota((8, 128), 1) >> 4
    split = source.reshape(8, 8, 128)
    req = jnp.zeros((8, 128), F32)
    for n in range(8):
        req = jnp.where(group == n, split[:, n], req)
    req_ref[...] = req


def pack_kernel(
    req_ref, len_ref, k_ref, v_ref, out_ref,
    req_in, len_in, k_in, v_in, keys_ref, values_ref, sems
):
    loads = [
        pltpu.make_async_copy(source, target, sems.at[i])
        for i, (source, target) in enumerate(
            [(req_ref, req_in), (len_ref, len_in), (k_ref, k_in), (v_ref, v_in)]
        )
    ]
    for load in loads:
        load.start()
    here = lax.axis_index(INST)
    token = iota((32, 128), 0)
    keys_ref[here] = jnp.full((32, 128), ABSENT, F32).astype(BF16)
    values_ref[here] = jnp.zeros((32, 128), F32).astype(BF16)
    for load in loads[:3]:
        load.wait()
    for s in range(63):
        keys = jnp.where(token < len_in[s], k_in[s].astype(F32), ABSENT)
        keys_ref[req_in[63 * here + s] >> 2] = keys.astype(BF16)
    send_keys = pltpu.make_async_copy(keys_ref, out_ref.at[:, pl.ds(0, 32)], sems.at[4])
    send_keys.start()
    loads[3].wait()
    for s in range(63):
        values_ref[req_in[63 * here + s] >> 2] = v_in[s]
    send_values = pltpu.make_async_copy(values_ref, out_ref.at[:, pl.ds(32, 32)], sems.at[5])
    send_values.start()
    send_keys.wait()
    send_values.wait()


def home_kernel(
    len_ref, q_ref, nk_ref, nv_ref, k_ref, v_ref, residual_ref, out_ref, stat_ref, base_ref
):
    query = q_ref[...].reshape(64, 128)
    query = jnp.concatenate([query, query], axis=0)
    owner = (iota((256, 128), 1) >> 4) & 3
    token = iota((256, 128), 0)
    scores = jnp.zeros((256, 128), F32)
    length = jnp.zeros((256, 128), jnp.int32)
    for r in range(4):
        scores = jnp.where(owner == r, dot(k_ref[r], query, NT), scores)
        length = jnp.where(owner == r, len_ref[r], length)
    scores = jnp.where(token < length, scores * SCALE, VERY_LOW)
    mine = ((iota((4, 128), 1) >> 4) & 3) == iota((4, 128), 0)
    fresh = dot(nk_ref[...], query, NT) * SCALE
    fresh = jnp.sum(jnp.where(mine, fresh, 0.0), axis=0, keepdims=True)
    top = jnp.maximum(jnp.max(scores, axis=0, keepdims=True), fresh)
    weights = jnp.exp(scores - top)
    own = jnp.exp(fresh - top)
    total = jnp.sum(weights, axis=0, keepdims=True) + own
    mixed = dot(jnp.where(mine, own, 0.0).astype(BF16), nv_ref[...], TN)
    for r in range(4):
        mixed += dot(jnp.where(owner == r, weights, 0.0).astype(BF16), v_ref[r], TN)
    out_ref[...] = mixed[:64]
    stat_ref[...] = jnp.concatenate([top, total], axis=0)
    base_ref[...] = residual_ref[...].astype(F32)


def attend_kernel(q_ref, req_ref, stat_ref, home_ref, recv_ref, out_ref, mixed_ref):
    owner = iota((32, 128), 1) >> 4
    far_tops, far_totals = [], []
    for g in range(8):
        here = pl.ds(8 * g, 8)
        keys = recv_ref[here, :32, :].reshape(256, 128)
        raw = dot(keys, q_ref[here].reshape(128, 128), NT)
        mark = keys.astype(F32)
        scores, marks = raw[:32], mark[:32]
        for j in range(1, 8):
            scores = jnp.where(owner == j, raw[32 * j : 32 * j + 32], scores)
            marks = jnp.where(owner == j, mark[32 * j : 32 * j + 32], marks)
        scores = jnp.where(marks < 0.5 * ABSENT, scores * SCALE, VERY_LOW)
        top = jnp.max(scores, axis=0, keepdims=True)
        weights = jnp.exp(scores - top)
        far_tops.append(top)
        far_totals.append(jnp.sum(weights, axis=0, keepdims=True))
        blocks = jnp.concatenate(
            [jnp.where(owner == j, weights, 0.0) for j in range(8)], axis=0
        ).astype(BF16)
        values = recv_ref[here, 32:, :].reshape(256, 128)
        mixed_ref[128 * g : 128 * g + 128] = dot(blocks, values, TN)
    far_top = jnp.concatenate(far_tops, axis=0)
    far_total = jnp.concatenate(far_totals, axis=0)
    near_top, near_total = stat_ref[0:1], stat_ref[1:2]
    which = iota((1, 128), 1) >> 4
    req = req_ref[...]
    tops = []
    for r in range(4):
        t = jnp.max(jnp.where(req == r, far_top, VERY_LOW), axis=0, keepdims=True)
        tops.append(jnp.maximum(t, jnp.where(which == r, near_top, VERY_LOW)))
    peak = jnp.concatenate(tops, axis=0)
    for shift in (16, 32, 64):
        peak = jnp.maximum(peak, pltpu.roll(peak, shift, 1))
    far_w, near_w, totals = [], [], []
    for r in range(4):
        p = peak[r : r + 1]
        f = jnp.where(req == r, jnp.exp(far_top - p), 0.0)
        n = jnp.where(which == r, jnp.exp(near_top - p), 0.0)
        far_w.append(f)
        near_w.append(n)
        totals.append(jnp.sum(f * far_total, axis=0, keepdims=True) + n * near_total)
    total = jnp.concatenate(totals, axis=0)
    for shift in (16, 32, 64):
        total = total + pltpu.roll(total, shift, 1)
    scale = 1.0 / total
    same = (iota((16, 128), 1) & 15) == iota((16, 128), 0)

    def spread_rows(rows):
        return halves(jnp.concatenate([jnp.where(same, row, 0.0) for row in rows], axis=0))

    high, low = spread_rows([near_w[r] * scale[r : r + 1] for r in range(4)])
    home_high, home_low = halves(home_ref[...])
    acc = dot(high[:, :64], home_high, NN) + dot(high[:, :64], home_low, NN)
    acc += dot(low[:, :64], home_high, NN)
    far_w = [far_w[r] * scale[r : r + 1] for r in range(4)]
    for g in range(8):
        high, low = spread_rows([far_w[r][g : g + 1] for r in range(4)])
        mixed_high, mixed_low = halves(mixed_ref[128 * g : 128 * g + 128])
        acc += dot(high, mixed_high, NN) + dot(high, mixed_low, NN) + dot(low, mixed_high, NN)
    out_ref[...] = (acc.astype(BF16).astype(F32) * RAISE).astype(BF16)


def project_kernel(rows_ref, weight_ref, out_ref, wide_ref):
    q = iota((256, 256), 0)
    p = iota((256, 256), 1)
    move = p == 64 * ((q >> 2) & 3) + 16 * (q & 3) + (q >> 4)
    move = move.astype(F32).astype(BF16)
    for b in range(16):
        moved = dot(move, rows_ref[4 * b : 4 * b + 4].reshape(256, 128), NN).astype(BF16)
        for h in range(16):
            wide_ref[16 * b : 16 * b + 16, 128 * h : 128 * h + 128] = moved[16 * h : 16 * h + 16]
    partial = dot(wide_ref[...], weight_ref[...], NN) * (1.0 / RAISE)
    out_ref[...] = partial.astype(BF16).reshape(8, 32, 256)


def finish_kernel(sums_ref, base_ref, out_ref):
    total = base_ref[...]
    for t in range(8):
        total = total + sums_ref[t].astype(F32)
    out_ref[...] = total.astype(BF16)


def body(
    queries,
    new_keys,
    new_values,
    home_keys,
    home_values,
    home_len,
    lent_keys,
    lent_values,
    lent_req,
    lent_len,
    out_weight,
    residual,
):
    here = lax.axis_index(INST)
    packed = pl.pallas_call(
        pack_kernel,
        out_shape=jax.ShapeDtypeStruct((64, 64, 128), BF16),
        in_specs=[ANY] * 4,
        out_specs=ANY,
        scratch_shapes=[
            pltpu.SMEM((4032,), jnp.int32),
            pltpu.SMEM((63,), jnp.int32),
            pltpu.VMEM((63, 32, 128), BF16),
            pltpu.VMEM((63, 32, 128), BF16),
            pltpu.VMEM((64, 32, 128), BF16),
            pltpu.VMEM((64, 32, 128), BF16),
            pltpu.SemaphoreType.DMA((6,)),
        ],
        name="pack_lent",
    )(
        lent_req,
        lent_len,
        lent_keys.reshape(63, 32, 128),
        lent_values.reshape(63, 32, 128),
    )
    recv = lax.all_to_all(packed, INST, split_axis=0, concat_axis=0, tiled=True)
    asked, req = pl.pallas_call(
        ask_kernel,
        out_shape=(
            jax.ShapeDtypeStruct((64, 16, 128), BF16),
            jax.ShapeDtypeStruct((8, 128), F32),
        ),
        in_specs=[SMEM, VMEM, VMEM],
        out_specs=(VMEM, VMEM),
        compiler_params=PARAMS,
        name="ask_queries",
    )(here.reshape(1), jnp.pad(lent_req, (0, 64), constant_values=-4).reshape(32, 128), queries)
    home_out, home_stat, base = pl.pallas_call(
        home_kernel,
        out_shape=(
            jax.ShapeDtypeStruct((64, 128), F32),
            jax.ShapeDtypeStruct((2, 128), F32),
            jax.ShapeDtypeStruct((32, 256), F32),
        ),
        in_specs=[SMEM] + [VMEM] * 6,
        out_specs=(VMEM,) * 3,
        compiler_params=PARAMS,
        name="home_part",
    )(
        home_len,
        queries,
        new_keys.reshape(4, 128),
        new_values.reshape(4, 128),
        home_keys.reshape(4, 256, 128),
        home_values.reshape(4, 256, 128),
        residual,
    )
    attended = pl.pallas_call(
        attend_kernel,
        out_shape=jax.ShapeDtypeStruct((64, 128), BF16),
        in_specs=[VMEM] * 5,
        out_specs=VMEM,
        scratch_shapes=[pltpu.VMEM((1024, 128), F32)],
        compiler_params=PARAMS,
        name="attend",
    )(asked, req, home_stat, home_out, recv)
    rows = lax.all_gather(attended.astype(jnp.float16), INST, axis=0).astype(BF16)
    partial = pl.pallas_call(
        project_kernel,
        out_shape=jax.ShapeDtypeStruct((8, 32, 256), BF16),
        in_specs=[VMEM] * 2,
        out_specs=VMEM,
        scratch_shapes=[pltpu.VMEM((256, 2048), BF16)],
        compiler_params=PARAMS,
        name="project",
    )(rows, out_weight)
    sums = lax.all_to_all(partial, "tp", split_axis=0, concat_axis=0, tiled=True)
    return pl.pallas_call(
        finish_kernel,
        out_shape=jax.ShapeDtypeStruct((32, 256), BF16),
        in_specs=[VMEM, VMEM],
        out_specs=VMEM,
        compiler_params=PARAMS,
        name="finish",
    )(sums, base)


def solution(mesh):
    placed = (
        P(INST, "tp", None),
        P(INST, "tp", None),
        P(INST, "tp", None),
        P(INST, None, "tp", None),
        P(INST, None, "tp", None),
        P(INST),
        P(INST, None, "tp", None),
        P(INST, None, "tp", None),
        P(),
        P(INST),
        P("tp", INST),
        P("tp", INST),
    )
    return jax.shard_map(
        body, mesh=mesh, in_specs=placed, out_specs=P("tp", INST), check_vma=False
    )
```

```python
import math

import jax
import jax.numpy as jnp
from jax import lax
from jax.experimental import pallas as pl
from jax.experimental.pallas import tpu as pltpu
from jax.sharding import Mesh, PartitionSpec as P

VERY_LOW = -1e30
ABSENT = 64.0
RAISE = 4096.0
SCALE = 1.0 / math.sqrt(128.0)
F32 = jnp.float32
BF16 = jnp.bfloat16
NT = (((1,), (1,)), ((), ()))
TN = (((0,), (0,)), ((), ()))
NN = (((1,), (0,)), ((), ()))
INST = ("y", "zh", "zp")
PARAMS = pltpu.CompilerParams(vmem_limit_bytes=16 * 2**20)
SMEM = pl.BlockSpec(memory_space=pltpu.SMEM)
ANY = pl.BlockSpec(memory_space=pl.ANY)
VMEM = pl.BlockSpec(memory_space=pltpu.VMEM)


def dot(a, b, dims):
    return lax.dot_general(a, b, dims, preferred_element_type=F32)


def iota(shape, axis):
    return lax.broadcasted_iota(jnp.int32, shape, axis)


def halves(x):
    high = x.astype(BF16)
    return high, (x - high.astype(F32)).astype(BF16)


def ask_kernel(here_ref, table_ref, q_ref, asked_ref, req_ref):
    here = here_ref[0]
    table = table_ref[...]
    found = jnp.where((table >> 2) == here, (table & 3) + 1, 0).astype(F32)
    lane = iota((1, 128), 1)
    rows = []
    for j in range(64):
        line, first = divmod(63 * j, 128)
        row = jnp.where(lane >= first, found[line : line + 1], 0.0)
        if first + 63 <= 128:
            row = jnp.where(lane < first + 63, row, 0.0)
        else:
            row = jnp.where(lane < first + 63 - 128, found[line + 1 : line + 2], row)
        rows.append(row)
    source = jnp.sum(jnp.concatenate(rows, axis=0), axis=1, keepdims=True) - 1.0
    source = jnp.broadcast_to(source, (64, 128))
    query = [q_ref[r].astype(F32) for r in range(4)]
    for j in range(64):
        s = jnp.broadcast_to(source[j : j + 1], (16, 128))
        picked = jnp.where(s == 1.0, query[1], query[0])
        picked = jnp.where(s == 2.0, query[2], picked)
        picked = jnp.where(s == 3.0, query[3], picked)
        asked_ref[j] = picked.astype(BF16)
    group = iota((8, 128), 1) >> 4
    split = source.reshape(8, 8, 128)
    req = jnp.zeros((8, 128), F32)
    for n in range(8):
        req = jnp.where(group == n, split[:, n], req)
    req_ref[...] = req


def pack_kernel(
    req_ref, len_ref, k_ref, v_ref, out_ref,
    req_in, len_in, k_in, v_in, keys_ref, values_ref, sems
):
    loads = [
        pltpu.make_async_copy(source, target, sems.at[i])
        for i, (source, target) in enumerate(
            [(req_ref, req_in), (len_ref, len_in), (k_ref, k_in), (v_ref, v_in)]
        )
    ]
    for load in loads:
        load.start()
    here = lax.axis_index(INST)
    token = iota((32, 128), 0)
    keys_ref[here] = jnp.full((32, 128), ABSENT, F32).astype(BF16)
    values_ref[here] = jnp.zeros((32, 128), F32).astype(BF16)
    for load in loads[:3]:
        load.wait()
    for s in range(63):
        keys = jnp.where(token < len_in[s], k_in[s].astype(F32), ABSENT)
        keys_ref[req_in[63 * here + s] >> 2] = keys.astype(BF16)
    send_keys = pltpu.make_async_copy(keys_ref, out_ref.at[:, pl.ds(0, 32)], sems.at[4])
    send_keys.start()
    loads[3].wait()
    for s in range(63):
        values_ref[req_in[63 * here + s] >> 2] = v_in[s]
    send_values = pltpu.make_async_copy(values_ref, out_ref.at[:, pl.ds(32, 32)], sems.at[5])
    send_values.start()
    send_keys.wait()
    send_values.wait()


def home_kernel(
    len_ref, q_ref, nk_ref, nv_ref, k_ref, v_ref, residual_ref, out_ref, stat_ref, base_ref
):
    query = q_ref[...].reshape(64, 128)
    query = jnp.concatenate([query, query], axis=0)
    owner = (iota((256, 128), 1) >> 4) & 3
    token = iota((256, 128), 0)
    scores = jnp.zeros((256, 128), F32)
    length = jnp.zeros((256, 128), jnp.int32)
    for r in range(4):
        scores = jnp.where(owner == r, dot(k_ref[r], query, NT), scores)
        length = jnp.where(owner == r, len_ref[r], length)
    scores = jnp.where(token < length, scores * SCALE, VERY_LOW)
    mine = ((iota((4, 128), 1) >> 4) & 3) == iota((4, 128), 0)
    fresh = dot(nk_ref[...], query, NT) * SCALE
    fresh = jnp.sum(jnp.where(mine, fresh, 0.0), axis=0, keepdims=True)
    top = jnp.maximum(jnp.max(scores, axis=0, keepdims=True), fresh)
    weights = jnp.exp(scores - top)
    own = jnp.exp(fresh - top)
    total = jnp.sum(weights, axis=0, keepdims=True) + own
    mixed = dot(jnp.where(mine, own, 0.0).astype(BF16), nv_ref[...], TN)
    for r in range(4):
        mixed += dot(jnp.where(owner == r, weights, 0.0).astype(BF16), v_ref[r], TN)
    out_ref[...] = mixed[:64]
    stat_ref[...] = jnp.concatenate([top, total], axis=0)
    base_ref[...] = residual_ref[...].astype(F32)


def attend_kernel(q_ref, req_ref, stat_ref, home_ref, recv_ref, out_ref, mixed_ref):
    owner = iota((32, 128), 1) >> 4
    far_tops, far_totals = [], []
    for g in range(8):
        here = pl.ds(8 * g, 8)
        keys = recv_ref[here, :32, :].reshape(256, 128)
        raw = dot(keys, q_ref[here].reshape(128, 128), NT)
        mark = keys.astype(F32)
        scores, marks = raw[:32], mark[:32]
        for j in range(1, 8):
            scores = jnp.where(owner == j, raw[32 * j : 32 * j + 32], scores)
            marks = jnp.where(owner == j, mark[32 * j : 32 * j + 32], marks)
        scores = jnp.where(marks < 0.5 * ABSENT, scores * SCALE, VERY_LOW)
        top = jnp.max(scores, axis=0, keepdims=True)
        weights = jnp.exp(scores - top)
        far_tops.append(top)
        far_totals.append(jnp.sum(weights, axis=0, keepdims=True))
        blocks = jnp.concatenate(
            [jnp.where(owner == j, weights, 0.0) for j in range(8)], axis=0
        ).astype(BF16)
        values = recv_ref[here, 32:, :].reshape(256, 128)
        mixed_ref[128 * g : 128 * g + 128] = dot(blocks, values, TN)
    far_top = jnp.concatenate(far_tops, axis=0)
    far_total = jnp.concatenate(far_totals, axis=0)
    near_top, near_total = stat_ref[0:1], stat_ref[1:2]
    which = iota((1, 128), 1) >> 4
    req = req_ref[...]
    tops = []
    for r in range(4):
        t = jnp.max(jnp.where(req == r, far_top, VERY_LOW), axis=0, keepdims=True)
        tops.append(jnp.maximum(t, jnp.where(which == r, near_top, VERY_LOW)))
    peak = jnp.concatenate(tops, axis=0)
    for shift in (16, 32, 64):
        peak = jnp.maximum(peak, pltpu.roll(peak, shift, 1))
    far_w, near_w, totals = [], [], []
    for r in range(4):
        p = peak[r : r + 1]
        f = jnp.where(req == r, jnp.exp(far_top - p), 0.0)
        n = jnp.where(which == r, jnp.exp(near_top - p), 0.0)
        far_w.append(f)
        near_w.append(n)
        totals.append(jnp.sum(f * far_total, axis=0, keepdims=True) + n * near_total)
    total = jnp.concatenate(totals, axis=0)
    for shift in (16, 32, 64):
        total = total + pltpu.roll(total, shift, 1)
    scale = 1.0 / total
    same = (iota((16, 128), 1) & 15) == iota((16, 128), 0)

    def spread_rows(rows):
        return halves(jnp.concatenate([jnp.where(same, row, 0.0) for row in rows], axis=0))

    high, low = spread_rows([near_w[r] * scale[r : r + 1] for r in range(4)])
    home_high, home_low = halves(home_ref[...])
    acc = dot(high[:, :64], home_high, NN) + dot(high[:, :64], home_low, NN)
    acc += dot(low[:, :64], home_high, NN)
    far_w = [far_w[r] * scale[r : r + 1] for r in range(4)]
    for g in range(8):
        high, low = spread_rows([far_w[r][g : g + 1] for r in range(4)])
        mixed_high, mixed_low = halves(mixed_ref[128 * g : 128 * g + 128])
        acc += dot(high, mixed_high, NN) + dot(high, mixed_low, NN) + dot(low, mixed_high, NN)
    out_ref[...] = (acc.astype(BF16).astype(F32) * RAISE).astype(BF16)


def project_kernel(parity_ref, rows_ref, mine_ref, other_ref, out_ref, wide_ref):
    q = iota((256, 256), 0)
    p = iota((256, 256), 1)
    move = p == 64 * ((q >> 2) & 3) + 16 * (q & 3) + (q >> 4)
    move = move.astype(F32).astype(BF16)
    for b in range(8):
        moved = dot(move, rows_ref[4 * b : 4 * b + 4].reshape(256, 128), NN).astype(BF16)
        for h in range(16):
            wide_ref[16 * b : 16 * b + 16, 128 * h : 128 * h + 128] = moved[16 * h : 16 * h + 16]
    parity = parity_ref[0]
    wide = wide_ref[...]
    mine = dot(wide, mine_ref[...], NN) * (1.0 / RAISE)
    out_ref[parity] = mine.astype(BF16).reshape(8, 16, 256)
    other = dot(wide, other_ref[...], NN) * (1.0 / RAISE)
    out_ref[1 - parity] = other.astype(BF16).reshape(8, 16, 256)


def finish_kernel(sums_ref, base_ref, out_ref):
    rows = []
    for parity in range(2):
        total = jnp.zeros((16, 256), F32)
        for t in range(8):
            total = total + sums_ref[8 * parity + t].astype(F32)
        rows.append(total)
    rows = jnp.concatenate(
        [rows[z & 1][4 * (z >> 1) : 4 * (z >> 1) + 4] for z in range(8)], axis=0
    )
    out_ref[...] = (base_ref[...] + rows).astype(BF16)


def body(
    queries,
    new_keys,
    new_values,
    home_keys,
    home_values,
    home_len,
    lent_keys,
    lent_values,
    lent_req,
    lent_len,
    out_weight,
    residual,
):
    here = lax.axis_index(INST)
    packed = pl.pallas_call(
        pack_kernel,
        out_shape=jax.ShapeDtypeStruct((64, 64, 128), BF16),
        in_specs=[ANY] * 4,
        out_specs=ANY,
        scratch_shapes=[
            pltpu.SMEM((4032,), jnp.int32),
            pltpu.SMEM((63,), jnp.int32),
            pltpu.VMEM((63, 32, 128), BF16),
            pltpu.VMEM((63, 32, 128), BF16),
            pltpu.VMEM((64, 32, 128), BF16),
            pltpu.VMEM((64, 32, 128), BF16),
            pltpu.SemaphoreType.DMA((6,)),
        ],
        name="pack_lent",
    )(
        lent_req,
        lent_len,
        lent_keys.reshape(63, 32, 128),
        lent_values.reshape(63, 32, 128),
    )
    recv = lax.all_to_all(packed, INST, split_axis=0, concat_axis=0, tiled=True)
    other_weight = lax.ppermute(out_weight, "zp", [(0, 1), (1, 0)])
    asked, req = pl.pallas_call(
        ask_kernel,
        out_shape=(
            jax.ShapeDtypeStruct((64, 16, 128), BF16),
            jax.ShapeDtypeStruct((8, 128), F32),
        ),
        in_specs=[SMEM, VMEM, VMEM],
        out_specs=(VMEM, VMEM),
        compiler_params=PARAMS,
        name="ask_queries",
    )(here.reshape(1), jnp.pad(lent_req, (0, 64), constant_values=-4).reshape(32, 128), queries)
    home_out, home_stat, base = pl.pallas_call(
        home_kernel,
        out_shape=(
            jax.ShapeDtypeStruct((64, 128), F32),
            jax.ShapeDtypeStruct((2, 128), F32),
            jax.ShapeDtypeStruct((32, 256), F32),
        ),
        in_specs=[SMEM] + [VMEM] * 6,
        out_specs=(VMEM,) * 3,
        compiler_params=PARAMS,
        name="home_part",
    )(
        home_len,
        queries,
        new_keys.reshape(4, 128),
        new_values.reshape(4, 128),
        home_keys.reshape(4, 256, 128),
        home_values.reshape(4, 256, 128),
        residual,
    )
    attended = pl.pallas_call(
        attend_kernel,
        out_shape=jax.ShapeDtypeStruct((64, 128), BF16),
        in_specs=[VMEM] * 5,
        out_specs=VMEM,
        scratch_shapes=[pltpu.VMEM((1024, 128), F32)],
        compiler_params=PARAMS,
        name="attend",
    )(asked, req, home_stat, home_out, recv)
    rows = lax.all_gather(attended.astype(jnp.float16), "zh", axis=0)
    rows = lax.all_gather(rows, "y", axis=0).astype(BF16).reshape(32, 64, 128)
    partial = pl.pallas_call(
        project_kernel,
        out_shape=jax.ShapeDtypeStruct((2, 8, 16, 256), BF16),
        in_specs=[SMEM] + [VMEM] * 3,
        out_specs=VMEM,
        scratch_shapes=[pltpu.VMEM((128, 2048), BF16)],
        compiler_params=PARAMS,
        name="project",
    )(lax.axis_index("zp").reshape(1), rows, out_weight, other_weight)
    sums = lax.all_to_all(
        partial.reshape(16, 16, 256), ("zp", "tp"), split_axis=0, concat_axis=0, tiled=True
    )
    return pl.pallas_call(
        finish_kernel,
        out_shape=jax.ShapeDtypeStruct((32, 256), BF16),
        in_specs=[VMEM, VMEM],
        out_specs=VMEM,
        compiler_params=PARAMS,
        name="finish",
    )(sums, base)


def solution(mesh):
    placed = (
        P(INST, "tp", None),
        P(INST, "tp", None),
        P(INST, "tp", None),
        P(INST, None, "tp", None),
        P(INST, None, "tp", None),
        P(INST),
        P(INST, None, "tp", None),
        P(INST, None, "tp", None),
        P(),
        P(INST),
        P("tp", INST),
        P("tp", INST),
    )
    fine = Mesh(mesh.devices.reshape(8, 4, 2, 8), INST + ("tp",))
    return jax.shard_map(
        body, mesh=fine, in_specs=placed, out_specs=P("tp", INST), check_vma=False
    )
```

```python
import math

import jax
import jax.numpy as jnp
from jax import lax
from jax.experimental import pallas as pl
from jax.experimental.pallas import tpu as pltpu
from jax.sharding import Mesh, PartitionSpec as P

VERY_LOW = -1e30
ABSENT = 64.0
SCALE = 1.0 / math.sqrt(128.0)
F32 = jnp.float32
BF16 = jnp.bfloat16
NT = (((1,), (1,)), ((), ()))
TN = (((0,), (0,)), ((), ()))
NN = (((1,), (0,)), ((), ()))
INST = ("yh", "yp", "zh", "zp")
HALVES = [[8 * y + 2 * k + ((y + p) & 1) for y in range(8) for k in range(4)] for p in range(2)]
SWAP = [(d, d ^ (64 if d & 1 else 8)) for d in range(512)]
PARAMS = pltpu.CompilerParams(vmem_limit_bytes=16 * 2**20)
SMEM = pl.BlockSpec(memory_space=pltpu.SMEM)
ANY = pl.BlockSpec(memory_space=pl.ANY)
VMEM = pl.BlockSpec(memory_space=pltpu.VMEM)


def dot(a, b, dims):
    return lax.dot_general(a, b, dims, preferred_element_type=F32)


def iota(shape, axis):
    return lax.broadcasted_iota(jnp.int32, shape, axis)


def halves(x):
    high = x.astype(BF16)
    return high, (x - high.astype(F32)).astype(BF16)


def ask_kernel(here_ref, table_ref, q_ref, asked_ref, req_ref):
    here = here_ref[0]
    table = table_ref[...]
    found = jnp.where((table >> 2) == here, (table & 3) + 1, 0).astype(F32)
    lane = iota((1, 128), 1)
    rows = []
    for j in range(64):
        line, first = divmod(63 * j, 128)
        row = jnp.where(lane >= first, found[line : line + 1], 0.0)
        if first + 63 <= 128:
            row = jnp.where(lane < first + 63, row, 0.0)
        else:
            row = jnp.where(lane < first + 63 - 128, found[line + 1 : line + 2], row)
        rows.append(row)
    source = jnp.sum(jnp.concatenate(rows, axis=0), axis=1, keepdims=True) - 1.0
    source = jnp.broadcast_to(source, (64, 128))
    query = [q_ref[r].astype(F32) for r in range(4)]
    for j in range(64):
        s = jnp.broadcast_to(source[j : j + 1], (16, 128))
        picked = jnp.where(s == 1.0, query[1], query[0])
        picked = jnp.where(s == 2.0, query[2], picked)
        picked = jnp.where(s == 3.0, query[3], picked)
        asked_ref[j] = picked.astype(BF16)
    group = iota((8, 128), 1) >> 4
    split = source.reshape(8, 8, 128)
    req = jnp.zeros((8, 128), F32)
    for n in range(8):
        req = jnp.where(group == n, split[:, n], req)
    req_ref[...] = req


def pack_kernel(
    req_ref, len_ref, k_ref, v_ref, out_ref,
    req_in, len_in, k_in, v_in, keys_ref, values_ref, sems
):
    loads = [
        pltpu.make_async_copy(source, target, sems.at[i])
        for i, (source, target) in enumerate(
            [(req_ref, req_in), (len_ref, len_in), (k_ref, k_in), (v_ref, v_in)]
        )
    ]
    for load in loads:
        load.start()
    here = lax.axis_index(INST)
    token = iota((32, 128), 0)
    keys_ref[here] = jnp.full((32, 128), ABSENT, F32).astype(BF16)
    values_ref[here] = jnp.zeros((32, 128), F32).astype(BF16)
    for load in loads[:3]:
        load.wait()
    for s in range(63):
        keys = jnp.where(token < len_in[s], k_in[s].astype(F32), ABSENT)
        keys_ref[req_in[63 * here + s] >> 2] = keys.astype(BF16)
    send_keys = pltpu.make_async_copy(keys_ref, out_ref.at[:, pl.ds(0, 32)], sems.at[4])
    send_keys.start()
    loads[3].wait()
    for s in range(63):
        values_ref[req_in[63 * here + s] >> 2] = v_in[s]
    send_values = pltpu.make_async_copy(values_ref, out_ref.at[:, pl.ds(32, 32)], sems.at[5])
    send_values.start()
    send_keys.wait()
    send_values.wait()


def home_kernel(
    len_ref, q_ref, nk_ref, nv_ref, k_ref, v_ref, residual_ref, out_ref, stat_ref, base_ref
):
    query = q_ref[...].reshape(64, 128)
    query = jnp.concatenate([query, query], axis=0)
    owner = (iota((256, 128), 1) >> 4) & 3
    token = iota((256, 128), 0)
    scores = jnp.zeros((256, 128), F32)
    length = jnp.zeros((256, 128), jnp.int32)
    for r in range(4):
        scores = jnp.where(owner == r, dot(k_ref[r], query, NT), scores)
        length = jnp.where(owner == r, len_ref[r], length)
    scores = jnp.where(token < length, scores * SCALE, VERY_LOW)
    mine = ((iota((4, 128), 1) >> 4) & 3) == iota((4, 128), 0)
    fresh = dot(nk_ref[...], query, NT) * SCALE
    fresh = jnp.sum(jnp.where(mine, fresh, 0.0), axis=0, keepdims=True)
    top = jnp.maximum(jnp.max(scores, axis=0, keepdims=True), fresh)
    weights = jnp.exp(scores - top)
    own = jnp.exp(fresh - top)
    total = jnp.sum(weights, axis=0, keepdims=True) + own
    mixed = dot(jnp.where(mine, own, 0.0).astype(BF16), nv_ref[...], TN)
    for r in range(4):
        mixed += dot(jnp.where(owner == r, weights, 0.0).astype(BF16), v_ref[r], TN)
    out_ref[...] = mixed[:64]
    stat_ref[...] = jnp.concatenate([top, total], axis=0)
    base_ref[...] = residual_ref[...].astype(F32)


def attend_kernel(q_ref, req_ref, stat_ref, home_ref, recv_ref, out_ref, mixed_ref):
    owner = iota((32, 128), 1) >> 4
    far_tops, far_totals = [], []
    for g in range(8):
        here = pl.ds(8 * g, 8)
        keys = recv_ref[here, :32, :].reshape(256, 128)
        raw = dot(keys, q_ref[here].reshape(128, 128), NT)
        mark = keys.astype(F32)
        scores, marks = raw[:32], mark[:32]
        for j in range(1, 8):
            scores = jnp.where(owner == j, raw[32 * j : 32 * j + 32], scores)
            marks = jnp.where(owner == j, mark[32 * j : 32 * j + 32], marks)
        scores = jnp.where(marks < 0.5 * ABSENT, scores * SCALE, VERY_LOW)
        top = jnp.max(scores, axis=0, keepdims=True)
        weights = jnp.exp(scores - top)
        far_tops.append(top)
        far_totals.append(jnp.sum(weights, axis=0, keepdims=True))
        blocks = jnp.concatenate(
            [jnp.where(owner == j, weights, 0.0) for j in range(8)], axis=0
        ).astype(BF16)
        values = recv_ref[here, 32:, :].reshape(256, 128)
        mixed_ref[128 * g : 128 * g + 128] = dot(blocks, values, TN)
    far_top = jnp.concatenate(far_tops, axis=0)
    far_total = jnp.concatenate(far_totals, axis=0)
    near_top, near_total = stat_ref[0:1], stat_ref[1:2]
    which = iota((1, 128), 1) >> 4
    req = req_ref[...]
    tops = []
    for r in range(4):
        t = jnp.max(jnp.where(req == r, far_top, VERY_LOW), axis=0, keepdims=True)
        tops.append(jnp.maximum(t, jnp.where(which == r, near_top, VERY_LOW)))
    peak = jnp.concatenate(tops, axis=0)
    for shift in (16, 32, 64):
        peak = jnp.maximum(peak, pltpu.roll(peak, shift, 1))
    far_w, near_w, totals = [], [], []
    for r in range(4):
        p = peak[r : r + 1]
        f = jnp.where(req == r, jnp.exp(far_top - p), 0.0)
        n = jnp.where(which == r, jnp.exp(near_top - p), 0.0)
        far_w.append(f)
        near_w.append(n)
        totals.append(jnp.sum(f * far_total, axis=0, keepdims=True) + n * near_total)
    total = jnp.concatenate(totals, axis=0)
    for shift in (16, 32, 64):
        total = total + pltpu.roll(total, shift, 1)
    scale = 1.0 / total
    same = (iota((16, 128), 1) & 15) == iota((16, 128), 0)

    def spread_rows(rows):
        return halves(jnp.concatenate([jnp.where(same, row, 0.0) for row in rows], axis=0))

    high, low = spread_rows([near_w[r] * scale[r : r + 1] for r in range(4)])
    home_high, home_low = halves(home_ref[...])
    acc = dot(high[:, :64], home_high, NN) + dot(high[:, :64], home_low, NN)
    acc += dot(low[:, :64], home_high, NN)
    far_w = [far_w[r] * scale[r : r + 1] for r in range(4)]
    for g in range(8):
        high, low = spread_rows([far_w[r][g : g + 1] for r in range(4)])
        mixed_high, mixed_low = halves(mixed_ref[128 * g : 128 * g + 128])
        acc += dot(high, mixed_high, NN) + dot(high, mixed_low, NN) + dot(low, mixed_high, NN)
    out_ref[...] = jnp.broadcast_to(acc.astype(BF16)[None], (32, 64, 128))


def project_kernel(rows_ref, mine_ref, other_ref, out_ref, wide_ref):
    q = iota((256, 256), 0)
    p = iota((256, 256), 1)
    move = p == 64 * ((q >> 2) & 3) + 16 * (q & 3) + (q >> 4)
    move = move.astype(F32).astype(BF16)
    for b in range(8):
        moved = dot(move, rows_ref[4 * b : 4 * b + 4].reshape(256, 128), NN).astype(BF16)
        for h in range(16):
            wide_ref[16 * b : 16 * b + 16, 128 * h : 128 * h + 128] = moved[16 * h : 16 * h + 16]
    wide = wide_ref[...]
    yp, zp, core = lax.axis_index("yp"), lax.axis_index("zp"), lax.axis_index("tp") & 1
    out_ref[2 * (1 - yp) + (1 - zp)] = jnp.zeros((8, 16, 256), BF16)
    out_ref[2 * (yp ^ (1 - core)) + (zp ^ core)] = jnp.zeros((8, 16, 256), BF16)
    out_ref[2 * yp + zp] = dot(wide, mine_ref[...], NN).astype(BF16).reshape(8, 16, 256)
    other = dot(wide, other_ref[...], NN).astype(BF16).reshape(8, 16, 256)
    out_ref[2 * (yp ^ core) + (zp ^ (1 - core))] = other


def finish_kernel(sums_ref, base_ref, out_ref):
    yp, zp, t = lax.axis_index("yp"), lax.axis_index("zp"), lax.axis_index("tp")
    mine = jnp.zeros((16, 256), F32)
    other = jnp.zeros((16, 256), F32)
    for s in range(8):
        mine = mine + sums_ref[8 * (2 * yp + zp) + s].astype(F32)
        core = s & 1
        other = other + sums_ref[8 * (2 * (yp ^ core) + (zp ^ (1 - core))) + s].astype(F32)
    turn = (yp + zp + t) & 1
    rows = [jnp.where(turn == 0, mine, other), jnp.where(turn == 0, other, mine)]
    rows = jnp.concatenate(
        [rows[z & 1][4 * (z >> 1) : 4 * (z >> 1) + 4] for z in range(8)], axis=0
    )
    out_ref[...] = (base_ref[...] + rows).astype(BF16)


def body(
    queries,
    new_keys,
    new_values,
    home_keys,
    home_values,
    home_len,
    lent_keys,
    lent_values,
    lent_req,
    lent_len,
    out_weight,
    residual,
):
    here = lax.axis_index(INST)
    packed = pl.pallas_call(
        pack_kernel,
        out_shape=jax.ShapeDtypeStruct((64, 64, 128), BF16),
        in_specs=[ANY] * 4,
        out_specs=ANY,
        scratch_shapes=[
            pltpu.SMEM((4032,), jnp.int32),
            pltpu.SMEM((63,), jnp.int32),
            pltpu.VMEM((63, 32, 128), BF16),
            pltpu.VMEM((63, 32, 128), BF16),
            pltpu.VMEM((64, 32, 128), BF16),
            pltpu.VMEM((64, 32, 128), BF16),
            pltpu.SemaphoreType.DMA((6,)),
        ],
        name="pack_lent",
    )(
        lent_req,
        lent_len,
        lent_keys.reshape(63, 32, 128),
        lent_values.reshape(63, 32, 128),
    )
    recv = lax.all_to_all(packed, INST, split_axis=0, concat_axis=0, tiled=True)
    other_weight = lax.ppermute(out_weight, INST + ("tp",), SWAP)
    asked, req = pl.pallas_call(
        ask_kernel,
        out_shape=(
            jax.ShapeDtypeStruct((64, 16, 128), BF16),
            jax.ShapeDtypeStruct((8, 128), F32),
        ),
        in_specs=[SMEM, VMEM, VMEM],
        out_specs=(VMEM, VMEM),
        compiler_params=PARAMS,
        name="ask_queries",
    )(here.reshape(1), jnp.pad(lent_req, (0, 64), constant_values=-4).reshape(32, 128), queries)
    home_out, home_stat, base = pl.pallas_call(
        home_kernel,
        out_shape=(
            jax.ShapeDtypeStruct((64, 128), F32),
            jax.ShapeDtypeStruct((2, 128), F32),
            jax.ShapeDtypeStruct((32, 256), F32),
        ),
        in_specs=[SMEM] + [VMEM] * 6,
        out_specs=(VMEM,) * 3,
        compiler_params=PARAMS,
        name="home_part",
    )(
        home_len,
        queries,
        new_keys.reshape(4, 128),
        new_values.reshape(4, 128),
        home_keys.reshape(4, 256, 128),
        home_values.reshape(4, 256, 128),
        residual,
    )
    copies = pl.pallas_call(
        attend_kernel,
        out_shape=jax.ShapeDtypeStruct((32, 64, 128), BF16),
        in_specs=[VMEM] * 5,
        out_specs=VMEM,
        scratch_shapes=[pltpu.VMEM((1024, 128), F32)],
        compiler_params=PARAMS,
        name="attend",
    )(asked, req, home_stat, home_out, recv)
    rows = lax.all_to_all(
        copies, INST, split_axis=0, concat_axis=0, tiled=True, axis_index_groups=HALVES
    )
    partial = pl.pallas_call(
        project_kernel,
        out_shape=jax.ShapeDtypeStruct((4, 8, 16, 256), BF16),
        in_specs=[VMEM] * 3,
        out_specs=VMEM,
        scratch_shapes=[pltpu.VMEM((128, 2048), BF16)],
        compiler_params=PARAMS,
        name="project",
    )(rows, out_weight, other_weight)
    sums = lax.all_to_all(
        partial.reshape(32, 16, 256), ("yp", "zp", "tp"), split_axis=0, concat_axis=0, tiled=True
    )
    return pl.pallas_call(
        finish_kernel,
        out_shape=jax.ShapeDtypeStruct((32, 256), BF16),
        in_specs=[VMEM, VMEM],
        out_specs=VMEM,
        compiler_params=PARAMS,
        name="finish",
    )(sums, base)


def solution(mesh):
    placed = (
        P(INST, "tp", None),
        P(INST, "tp", None),
        P(INST, "tp", None),
        P(INST, None, "tp", None),
        P(INST, None, "tp", None),
        P(INST),
        P(INST, None, "tp", None),
        P(INST, None, "tp", None),
        P(),
        P(INST),
        P("tp", INST),
        P("tp", INST),
    )
    fine = Mesh(mesh.devices.reshape(4, 2, 4, 2, 8), INST + ("tp",))
    return jax.shard_map(
        body, mesh=fine, in_specs=placed, out_specs=P("tp", INST), check_vma=False
    )
```

```python
import math

import jax
import jax.numpy as jnp
from jax import lax
from jax.experimental import pallas as pl
from jax.experimental.pallas import tpu as pltpu
from jax.sharding import Mesh, PartitionSpec as P

VERY_LOW = -1e30
ABSENT = 64.0
SCALE = 1.0 / math.sqrt(128.0)
F32 = jnp.float32
BF16 = jnp.bfloat16
NT = (((1,), (1,)), ((), ()))
TN = (((0,), (0,)), ((), ()))
NN = (((1,), (0,)), ((), ()))
INST = ("yh", "yp", "zh", "zp")
HALVES = [[8 * y + 2 * k + ((y + p) & 1) for y in range(8) for k in range(4)] for p in range(2)]
SWAP = [(d, d ^ (64 if d & 1 else 8)) for d in range(512)]
PARAMS = pltpu.CompilerParams(vmem_limit_bytes=16 * 2**20)
SMEM = pl.BlockSpec(memory_space=pltpu.SMEM)
ANY = pl.BlockSpec(memory_space=pl.ANY)
VMEM = pl.BlockSpec(memory_space=pltpu.VMEM)


def dot(a, b, dims):
    return lax.dot_general(a, b, dims, preferred_element_type=F32)


def iota(shape, axis):
    return lax.broadcasted_iota(jnp.int32, shape, axis)


def halves(x):
    high = x.astype(BF16)
    return high, (x - high.astype(F32)).astype(BF16)


def ask_kernel(here_ref, table_ref, q_ref, asked_ref, req_ref):
    here = here_ref[0]
    table = table_ref[...]
    found = jnp.where((table >> 2) == here, (table & 3) + 1, 0).astype(F32)
    lane = iota((1, 128), 1)
    rows = []
    for j in range(64):
        line, first = divmod(63 * j, 128)
        row = jnp.where(lane >= first, found[line : line + 1], 0.0)
        if first + 63 <= 128:
            row = jnp.where(lane < first + 63, row, 0.0)
        else:
            row = jnp.where(lane < first + 63 - 128, found[line + 1 : line + 2], row)
        rows.append(row)
    source = jnp.sum(jnp.concatenate(rows, axis=0), axis=1, keepdims=True) - 1.0
    source = jnp.broadcast_to(source, (64, 128))
    query = [q_ref[r].astype(F32) for r in range(4)]
    for g in range(8):
        rows = []
        for j in range(8 * g, 8 * g + 8):
            s = jnp.broadcast_to(source[j : j + 1], (16, 128))
            picked = jnp.where(s == 1.0, query[1], query[0])
            picked = jnp.where(s == 2.0, query[2], picked)
            rows.append(jnp.where(s == 3.0, query[3], picked))
        asked_ref[g] = jnp.concatenate(rows, axis=0).T.astype(BF16)
    group = iota((8, 128), 1) >> 4
    split = source.reshape(8, 8, 128)
    req = jnp.zeros((8, 128), F32)
    for n in range(8):
        req = jnp.where(group == n, split[:, n], req)
    req_ref[...] = req


def pack_kernel(
    req_ref, len_ref, k_ref, v_ref, out_ref,
    req_in, len_in, k_in, v_in, keys_ref, values_ref, sems
):
    loads = [
        pltpu.make_async_copy(source, target, sems.at[i])
        for i, (source, target) in enumerate(
            [(req_ref, req_in), (len_ref, len_in), (k_ref, k_in), (v_ref, v_in)]
        )
    ]
    for load in loads:
        load.start()
    here = lax.axis_index(INST)
    token = iota((32, 128), 0)
    keys_ref[here] = jnp.full((32, 128), ABSENT, F32).astype(BF16)
    values_ref[here] = jnp.zeros((32, 128), F32).astype(BF16)
    for load in loads[:3]:
        load.wait()
    for s in range(63):
        keys = jnp.where(token < len_in[s], k_in[s].astype(F32), ABSENT)
        keys_ref[req_in[63 * here + s] >> 2] = keys.astype(BF16)
    send_keys = pltpu.make_async_copy(keys_ref, out_ref.at[:, pl.ds(0, 32)], sems.at[4])
    send_keys.start()
    loads[3].wait()
    for s in range(63):
        values_ref[req_in[63 * here + s] >> 2] = v_in[s]
    send_values = pltpu.make_async_copy(values_ref, out_ref.at[:, pl.ds(32, 32)], sems.at[5])
    send_values.start()
    send_keys.wait()
    send_values.wait()


def home_kernel(
    len_ref, q_ref, nk_ref, nv_ref, k_ref, v_ref, residual_ref, out_ref, stat_ref, base_ref
):
    query = q_ref[...].reshape(64, 128)
    query = jnp.concatenate([query, query], axis=0)
    owner = (iota((256, 128), 1) >> 4) & 3
    token = iota((256, 128), 0)
    scores = jnp.zeros((256, 128), F32)
    length = jnp.zeros((256, 128), jnp.int32)
    for r in range(4):
        scores = jnp.where(owner == r, dot(k_ref[r], query, NT), scores)
        length = jnp.where(owner == r, len_ref[r], length)
    scores = jnp.where(token < length, scores * SCALE, VERY_LOW)
    mine = ((iota((4, 128), 1) >> 4) & 3) == iota((4, 128), 0)
    fresh = dot(nk_ref[...], query, NT) * SCALE
    fresh = jnp.sum(jnp.where(mine, fresh, 0.0), axis=0, keepdims=True)
    top = jnp.maximum(jnp.max(scores, axis=0, keepdims=True), fresh)
    weights = jnp.exp(scores - top)
    own = jnp.exp(fresh - top)
    total = jnp.sum(weights, axis=0, keepdims=True) + own
    mixed = dot(jnp.where(mine, own, 0.0).astype(BF16), nv_ref[...], TN)
    for r in range(4):
        mixed += dot(jnp.where(owner == r, weights, 0.0).astype(BF16), v_ref[r], TN)
    out_ref[...] = mixed[:64]
    stat_ref[...] = jnp.concatenate([top, total], axis=0)
    base_ref[...] = residual_ref[...].astype(F32)


def attend_kernel(q_ref, req_ref, stat_ref, home_ref, recv_ref, out_ref, mixed_ref):
    owner = iota((32, 128), 1) >> 4
    far_tops, far_totals = [], []
    for g in range(8):
        here = pl.ds(8 * g, 8)
        keys = recv_ref[here, :32, :].reshape(256, 128)
        raw = dot(keys, q_ref[g], NN)
        mark = keys.astype(F32)
        scores, marks = raw[:32], mark[:32]
        for j in range(1, 8):
            scores = jnp.where(owner == j, raw[32 * j : 32 * j + 32], scores)
            marks = jnp.where(owner == j, mark[32 * j : 32 * j + 32], marks)
        scores = jnp.where(marks < 0.5 * ABSENT, scores * SCALE, VERY_LOW)
        top = jnp.max(scores, axis=0, keepdims=True)
        weights = jnp.exp(scores - top)
        far_tops.append(top)
        far_totals.append(jnp.sum(weights, axis=0, keepdims=True))
        blocks = jnp.concatenate(
            [jnp.where(owner == j, weights, 0.0) for j in range(8)], axis=0
        ).astype(BF16)
        values = recv_ref[here, 32:, :].reshape(256, 128)
        mixed_ref[128 * g : 128 * g + 128] = dot(blocks, values, TN)
    far_top = jnp.concatenate(far_tops, axis=0)
    far_total = jnp.concatenate(far_totals, axis=0)
    near_top, near_total = stat_ref[0:1], stat_ref[1:2]
    which = iota((1, 128), 1) >> 4
    req = req_ref[...]
    tops = []
    for r in range(4):
        t = jnp.max(jnp.where(req == r, far_top, VERY_LOW), axis=0, keepdims=True)
        tops.append(jnp.maximum(t, jnp.where(which == r, near_top, VERY_LOW)))
    peak = jnp.concatenate(tops, axis=0)
    for shift in (16, 32, 64):
        peak = jnp.maximum(peak, pltpu.roll(peak, shift, 1))
    far_w, near_w, totals = [], [], []
    for r in range(4):
        p = peak[r : r + 1]
        f = jnp.where(req == r, jnp.exp(far_top - p), 0.0)
        n = jnp.where(which == r, jnp.exp(near_top - p), 0.0)
        far_w.append(f)
        near_w.append(n)
        totals.append(jnp.sum(f * far_total, axis=0, keepdims=True) + n * near_total)
    total = jnp.concatenate(totals, axis=0)
    for shift in (16, 32, 64):
        total = total + pltpu.roll(total, shift, 1)
    scale = 1.0 / total
    same = (iota((16, 128), 1) & 15) == iota((16, 128), 0)

    def spread_rows(rows):
        return halves(jnp.concatenate([jnp.where(same, row, 0.0) for row in rows], axis=0))

    high, low = spread_rows([near_w[r] * scale[r : r + 1] for r in range(4)])
    home_high, home_low = halves(home_ref[...])
    acc = dot(high[:, :64], home_high, NN) + dot(high[:, :64], home_low, NN)
    acc += dot(low[:, :64], home_high, NN)
    far_w = [far_w[r] * scale[r : r + 1] for r in range(4)]
    for g in range(8):
        high, low = spread_rows([far_w[r][g : g + 1] for r in range(4)])
        mixed_high, mixed_low = halves(mixed_ref[128 * g : 128 * g + 128])
        acc += dot(high, mixed_high, NN) + dot(high, mixed_low, NN) + dot(low, mixed_high, NN)
    out_ref[...] = jnp.broadcast_to(acc.astype(BF16)[None], (32, 64, 128))


def project_kernel(rows_ref, mine_ref, other_ref, out_ref, wide_ref):
    q = iota((256, 256), 0)
    p = iota((256, 256), 1)
    move = p == 64 * ((q >> 2) & 3) + 16 * (q & 3) + (q >> 4)
    move = move.astype(F32).astype(BF16)
    for b in range(8):
        moved = dot(move, rows_ref[4 * b : 4 * b + 4].reshape(256, 128), NN).astype(BF16)
        for h in range(16):
            wide_ref[16 * b : 16 * b + 16, 128 * h : 128 * h + 128] = moved[16 * h : 16 * h + 16]
    wide = wide_ref[...]
    yp, zp, core = lax.axis_index("yp"), lax.axis_index("zp"), lax.axis_index("tp") & 1
    out_ref[2 * (1 - yp) + (1 - zp)] = jnp.zeros((8, 16, 256), BF16)
    out_ref[2 * (yp ^ (1 - core)) + (zp ^ core)] = jnp.zeros((8, 16, 256), BF16)
    out_ref[2 * yp + zp] = dot(wide, mine_ref[...], NN).astype(BF16).reshape(8, 16, 256)
    other = dot(wide, other_ref[...], NN).astype(BF16).reshape(8, 16, 256)
    out_ref[2 * (yp ^ core) + (zp ^ (1 - core))] = other


def finish_kernel(turn_ref, sums_ref, base_ref, out_ref):
    yp, zp = lax.axis_index("yp"), lax.axis_index("zp")
    mine = jnp.zeros((16, 256), F32)
    other = jnp.zeros((16, 256), F32)
    for s in range(8):
        mine = mine + sums_ref[8 * (2 * yp + zp) + s].astype(F32)
        core = s & 1
        other = other + sums_ref[8 * (2 * (yp ^ core) + (zp ^ (1 - core))) + s].astype(F32)
    turn = turn_ref[0]
    rows = [jnp.where(turn == 0, mine, other), jnp.where(turn == 0, other, mine)]
    rows = jnp.concatenate(
        [rows[z & 1][4 * (z >> 1) : 4 * (z >> 1) + 4] for z in range(8)], axis=0
    )
    out_ref[...] = (base_ref[...] + rows).astype(BF16)


def body(
    queries,
    new_keys,
    new_values,
    home_keys,
    home_values,
    home_len,
    lent_keys,
    lent_values,
    lent_req,
    lent_len,
    out_weight,
    residual,
):
    here = lax.axis_index(INST)
    packed = pl.pallas_call(
        pack_kernel,
        out_shape=jax.ShapeDtypeStruct((64, 64, 128), BF16),
        in_specs=[ANY] * 4,
        out_specs=ANY,
        scratch_shapes=[
            pltpu.SMEM((4032,), jnp.int32),
            pltpu.SMEM((63,), jnp.int32),
            pltpu.VMEM((63, 32, 128), BF16),
            pltpu.VMEM((63, 32, 128), BF16),
            pltpu.VMEM((64, 32, 128), BF16),
            pltpu.VMEM((64, 32, 128), BF16),
            pltpu.SemaphoreType.DMA((6,)),
        ],
        name="pack_lent",
    )(
        lent_req,
        lent_len,
        lent_keys.reshape(63, 32, 128),
        lent_values.reshape(63, 32, 128),
    )
    recv = lax.all_to_all(packed, INST, split_axis=0, concat_axis=0, tiled=True)
    other_weight = lax.ppermute(out_weight, INST + ("tp",), SWAP)
    asked, req = pl.pallas_call(
        ask_kernel,
        out_shape=(
            jax.ShapeDtypeStruct((8, 128, 128), BF16),
            jax.ShapeDtypeStruct((8, 128), F32),
        ),
        in_specs=[SMEM, VMEM, VMEM],
        out_specs=(VMEM, VMEM),
        compiler_params=PARAMS,
        name="ask_queries",
    )(here.reshape(1), jnp.pad(lent_req, (0, 64), constant_values=-4).reshape(32, 128), queries)
    home_out, home_stat, base = pl.pallas_call(
        home_kernel,
        out_shape=(
            jax.ShapeDtypeStruct((64, 128), F32),
            jax.ShapeDtypeStruct((2, 128), F32),
            jax.ShapeDtypeStruct((32, 256), F32),
        ),
        in_specs=[SMEM] + [VMEM] * 6,
        out_specs=(VMEM,) * 3,
        compiler_params=PARAMS,
        name="home_part",
    )(
        home_len,
        queries,
        new_keys.reshape(4, 128),
        new_values.reshape(4, 128),
        home_keys.reshape(4, 256, 128),
        home_values.reshape(4, 256, 128),
        residual,
    )
    copies = pl.pallas_call(
        attend_kernel,
        out_shape=jax.ShapeDtypeStruct((32, 64, 128), BF16),
        in_specs=[VMEM] * 5,
        out_specs=VMEM,
        scratch_shapes=[pltpu.VMEM((1024, 128), F32)],
        compiler_params=PARAMS,
        name="attend",
    )(asked, req, home_stat, home_out, recv)
    rows = lax.all_to_all(
        copies, INST, split_axis=0, concat_axis=0, tiled=True, axis_index_groups=HALVES
    )
    partial = pl.pallas_call(
        project_kernel,
        out_shape=jax.ShapeDtypeStruct((4, 8, 16, 256), BF16),
        in_specs=[VMEM] * 3,
        out_specs=VMEM,
        scratch_shapes=[pltpu.VMEM((128, 2048), BF16)],
        compiler_params=PARAMS,
        name="project",
    )(rows, out_weight, other_weight)
    sums = lax.all_to_all(
        partial.reshape(32, 16, 256), ("yp", "zp", "tp"), split_axis=0, concat_axis=0, tiled=True
    )
    turn = (lax.axis_index("yp") + lax.axis_index("zp") + lax.axis_index("tp")) & 1
    return pl.pallas_call(
        finish_kernel,
        out_shape=jax.ShapeDtypeStruct((32, 256), BF16),
        in_specs=[SMEM, VMEM, VMEM],
        out_specs=VMEM,
        compiler_params=PARAMS,
        name="finish",
    )(turn.reshape(1), sums, base)


def solution(mesh):
    placed = (
        P(INST, "tp", None),
        P(INST, "tp", None),
        P(INST, "tp", None),
        P(INST, None, "tp", None),
        P(INST, None, "tp", None),
        P(INST),
        P(INST, None, "tp", None),
        P(INST, None, "tp", None),
        P(),
        P(INST),
        P("tp", INST),
        P("tp", INST),
    )
    fine = Mesh(mesh.devices.reshape(4, 2, 4, 2, 8), INST + ("tp",))
    return jax.shard_map(
        body, mesh=fine, in_specs=placed, out_specs=P("tp", INST), check_vma=False
    )
```

```python
import math

import jax
import jax.numpy as jnp
from jax import lax
from jax.experimental import pallas as pl
from jax.experimental.pallas import tpu as pltpu
from jax.sharding import Mesh, PartitionSpec as P

VERY_LOW = -1e30
ABSENT = 64.0
SCALE = 1.0 / math.sqrt(128.0)
F32 = jnp.float32
BF16 = jnp.bfloat16
NT = (((1,), (1,)), ((), ()))
TN = (((0,), (0,)), ((), ()))
NN = (((1,), (0,)), ((), ()))
INST = ("y", "zh", "zp")
PARAMS = pltpu.CompilerParams(vmem_limit_bytes=16 * 2**20)
SMEM = pl.BlockSpec(memory_space=pltpu.SMEM)
ANY = pl.BlockSpec(memory_space=pl.ANY)
VMEM = pl.BlockSpec(memory_space=pltpu.VMEM)


def dot(a, b, dims):
    return lax.dot_general(a, b, dims, preferred_element_type=F32)


def iota(shape, axis):
    return lax.broadcasted_iota(jnp.int32, shape, axis)


def halves(x):
    high = x.astype(BF16)
    return high, (x - high.astype(F32)).astype(BF16)


def ask_kernel(
    here_ref, table_ref, q_ref, weight_ref, done_ref, asked_ref, req_ref, sent_ref
):
    first = pl.multiple_of((1 - lax.axis_index("zp")) * 1024, 1024)
    sent_ref[...] = weight_ref[pl.ds(first, 1024)]
    here = here_ref[0]
    table = table_ref[...]
    found = jnp.where((table >> 2) == here, (table & 3) + 1, 0).astype(F32)
    lane = iota((1, 128), 1)
    rows = []
    for j in range(64):
        line, first = divmod(63 * j, 128)
        row = jnp.where(lane >= first, found[line : line + 1], 0.0)
        if first + 63 <= 128:
            row = jnp.where(lane < first + 63, row, 0.0)
        else:
            row = jnp.where(lane < first + 63 - 128, found[line + 1 : line + 2], row)
        rows.append(row)
    source = jnp.sum(jnp.concatenate(rows, axis=0), axis=1, keepdims=True) - 1.0
    source = jnp.broadcast_to(source, (64, 128))
    query = [q_ref[r].astype(F32) for r in range(4)]
    for g in range(8):
        rows = []
        for j in range(8 * g, 8 * g + 8):
            s = jnp.broadcast_to(source[j : j + 1], (16, 128))
            picked = jnp.where(s == 1.0, query[1], query[0])
            picked = jnp.where(s == 2.0, query[2], picked)
            rows.append(jnp.where(s == 3.0, query[3], picked))
        asked_ref[g] = jnp.concatenate(rows, axis=0).T.astype(BF16)
    group = iota((8, 128), 1) >> 4
    split = source.reshape(8, 8, 128)
    req = jnp.zeros((8, 128), F32)
    for n in range(8):
        req = jnp.where(group == n, split[:, n], req)
    req_ref[...] = req


def pack_kernel(
    req_ref, len_ref, k_ref, v_ref, out_ref, done_ref,
    req_in, len_in, k_in, v_in, keys_ref, values_ref, sems
):
    loads = [
        pltpu.make_async_copy(source, target, sems.at[i])
        for i, (source, target) in enumerate(
            [(req_ref, req_in), (len_ref, len_in), (k_ref, k_in), (v_ref, v_in)]
        )
    ]
    for load in loads:
        load.start()
    here = lax.axis_index(INST)
    done_ref[...] = jnp.zeros((8, 128), F32)
    token = iota((32, 128), 0)
    keys_ref[here] = jnp.full((32, 128), ABSENT, F32).astype(BF16)
    values_ref[here] = jnp.zeros((32, 128), F32).astype(BF16)
    for load in loads[:3]:
        load.wait()
    for s in range(63):
        keys = jnp.where(token < len_in[s], k_in[s].astype(F32), ABSENT)
        keys_ref[req_in[63 * here + s] >> 2] = keys.astype(BF16)
    send_keys = pltpu.make_async_copy(keys_ref, out_ref.at[:, pl.ds(0, 32)], sems.at[4])
    send_keys.start()
    loads[3].wait()
    for s in range(63):
        values_ref[req_in[63 * here + s] >> 2] = v_in[s]
    send_values = pltpu.make_async_copy(values_ref, out_ref.at[:, pl.ds(32, 32)], sems.at[5])
    send_values.start()
    send_keys.wait()
    send_values.wait()


def home_kernel(
    len_ref, q_ref, nk_ref, nv_ref, k_ref, v_ref, residual_ref, out_ref, stat_ref, base_ref
):
    query = q_ref[...].reshape(64, 128)
    query = jnp.concatenate([query, query], axis=0)
    owner = (iota((256, 128), 1) >> 4) & 3
    token = iota((256, 128), 0)
    scores = jnp.zeros((256, 128), F32)
    length = jnp.zeros((256, 128), jnp.int32)
    for r in range(4):
        scores = jnp.where(owner == r, dot(k_ref[r], query, NT), scores)
        length = jnp.where(owner == r, len_ref[r], length)
    scores = jnp.where(token < length, scores * SCALE, VERY_LOW)
    mine = ((iota((4, 128), 1) >> 4) & 3) == iota((4, 128), 0)
    fresh = dot(nk_ref[...], query, NT) * SCALE
    fresh = jnp.sum(jnp.where(mine, fresh, 0.0), axis=0, keepdims=True)
    top = jnp.maximum(jnp.max(scores, axis=0, keepdims=True), fresh)
    weights = jnp.exp(scores - top)
    own = jnp.exp(fresh - top)
    total = jnp.sum(weights, axis=0, keepdims=True) + own
    mixed = dot(jnp.where(mine, own, 0.0).astype(BF16), nv_ref[...], TN)
    for r in range(4):
        mixed += dot(jnp.where(owner == r, weights, 0.0).astype(BF16), v_ref[r], TN)
    out_ref[...] = mixed[:64]
    stat_ref[...] = jnp.concatenate([top, total], axis=0)
    base_ref[...] = residual_ref[...].astype(F32)


def attend_kernel(q_ref, req_ref, stat_ref, home_ref, recv_ref, out_ref, mixed_ref):
    owner = iota((32, 128), 1) >> 4
    far_tops, far_totals = [], []
    for g in range(8):
        here = pl.ds(8 * g, 8)
        keys = recv_ref[here, :32, :].reshape(256, 128)
        raw = dot(keys, q_ref[g], NN)
        mark = keys.astype(F32)
        scores, marks = raw[:32], mark[:32]
        for j in range(1, 8):
            scores = jnp.where(owner == j, raw[32 * j : 32 * j + 32], scores)
            marks = jnp.where(owner == j, mark[32 * j : 32 * j + 32], marks)
        scores = jnp.where(marks < 0.5 * ABSENT, scores * SCALE, VERY_LOW)
        top = jnp.max(scores, axis=0, keepdims=True)
        weights = jnp.exp(scores - top)
        far_tops.append(top)
        far_totals.append(jnp.sum(weights, axis=0, keepdims=True))
        blocks = jnp.concatenate(
            [jnp.where(owner == j, weights, 0.0) for j in range(8)], axis=0
        ).astype(BF16)
        values = recv_ref[here, 32:, :].reshape(256, 128)
        mixed_ref[128 * g : 128 * g + 128] = dot(blocks, values, TN)
    far_top = jnp.concatenate(far_tops, axis=0)
    far_total = jnp.concatenate(far_totals, axis=0)
    near_top, near_total = stat_ref[0:1], stat_ref[1:2]
    which = iota((1, 128), 1) >> 4
    req = req_ref[...]
    tops = []
    for r in range(4):
        t = jnp.max(jnp.where(req == r, far_top, VERY_LOW), axis=0, keepdims=True)
        tops.append(jnp.maximum(t, jnp.where(which == r, near_top, VERY_LOW)))
    peak = jnp.concatenate(tops, axis=0)
    for shift in (16, 32, 64):
        peak = jnp.maximum(peak, pltpu.roll(peak, shift, 1))
    far_w, near_w, totals = [], [], []
    for r in range(4):
        p = peak[r : r + 1]
        f = jnp.where(req == r, jnp.exp(far_top - p), 0.0)
        n = jnp.where(which == r, jnp.exp(near_top - p), 0.0)
        far_w.append(f)
        near_w.append(n)
        totals.append(jnp.sum(f * far_total, axis=0, keepdims=True) + n * near_total)
    total = jnp.concatenate(totals, axis=0)
    for shift in (16, 32, 64):
        total = total + pltpu.roll(total, shift, 1)
    scale = 1.0 / total
    same = (iota((16, 128), 1) & 15) == iota((16, 128), 0)

    def spread_rows(rows):
        return halves(jnp.concatenate([jnp.where(same, row, 0.0) for row in rows], axis=0))

    high, low = spread_rows([near_w[r] * scale[r : r + 1] for r in range(4)])
    home_high, home_low = halves(home_ref[...])
    acc = dot(high[:, :64], home_high, NN) + dot(high[:, :64], home_low, NN)
    acc += dot(low[:, :64], home_high, NN)
    far_w = [far_w[r] * scale[r : r + 1] for r in range(4)]
    for g in range(8):
        high, low = spread_rows([far_w[r][g : g + 1] for r in range(4)])
        mixed_high, mixed_low = halves(mixed_ref[128 * g : 128 * g + 128])
        acc += dot(high, mixed_high, NN) + dot(high, mixed_low, NN) + dot(low, mixed_high, NN)
    lower = jnp.concatenate([acc[16 * r : 16 * r + 8] for r in range(4)], axis=0)
    upper = jnp.concatenate([acc[16 * r + 8 : 16 * r + 16] for r in range(4)], axis=0)
    split = jnp.concatenate([lower, upper], axis=0).astype(BF16).reshape(1, 2, 32, 128)
    out_ref[...] = jnp.broadcast_to(split, (32, 2, 32, 128)).reshape(64, 32, 128)


def join_kernel(mine_ref, received_ref, out_ref):
    zp = lax.axis_index("zp")
    out_ref[zp] = mine_ref[pl.ds(pl.multiple_of(zp * 1024, 1024), 1024)]
    out_ref[1 - zp] = received_ref[...]


def project_kernel(rows_ref, weight_ref, out_ref, wide_ref):
    q = iota((256, 256), 0)
    p = iota((256, 256), 1)
    move = p == 32 * ((q >> 2) & 7) + 8 * (q & 3) + (q >> 5)
    move = move.astype(F32).astype(BF16)
    for b in range(8):
        moved = dot(move, rows_ref[8 * b : 8 * b + 8].reshape(256, 128), NN).astype(BF16)
        for h in range(8):
            wide_ref[32 * b : 32 * b + 32, 128 * h : 128 * h + 128] = moved[32 * h : 32 * h + 32]
    wide = wide_ref[...]
    for c in range(2):
        out_ref[c] = dot(wide, weight_ref[c], NN).astype(BF16).reshape(8, 32, 256)


def finish_kernel(sums_ref, base_ref, out_ref):
    total = base_ref[...]
    for s in range(16):
        total = total + sums_ref[s].astype(F32)
    out_ref[...] = total.astype(BF16)


def body(
    queries,
    new_keys,
    new_values,
    home_keys,
    home_values,
    home_len,
    lent_keys,
    lent_values,
    lent_req,
    lent_len,
    out_weight,
    residual,
):
    here = lax.axis_index(INST)
    packed, done = pl.pallas_call(
        pack_kernel,
        out_shape=(
            jax.ShapeDtypeStruct((64, 64, 128), BF16),
            jax.ShapeDtypeStruct((8, 128), F32),
        ),
        in_specs=[ANY] * 4,
        out_specs=(ANY, VMEM),
        scratch_shapes=[
            pltpu.SMEM((4032,), jnp.int32),
            pltpu.SMEM((63,), jnp.int32),
            pltpu.VMEM((63, 32, 128), BF16),
            pltpu.VMEM((63, 32, 128), BF16),
            pltpu.VMEM((64, 32, 128), BF16),
            pltpu.VMEM((64, 32, 128), BF16),
            pltpu.SemaphoreType.DMA((6,)),
        ],
        name="pack_lent",
    )(
        lent_req,
        lent_len,
        lent_keys.reshape(63, 32, 128),
        lent_values.reshape(63, 32, 128),
    )
    recv = lax.all_to_all(packed, INST, split_axis=0, concat_axis=0, tiled=True)
    asked, req, sent = pl.pallas_call(
        ask_kernel,
        out_shape=(
            jax.ShapeDtypeStruct((8, 128, 128), BF16),
            jax.ShapeDtypeStruct((8, 128), F32),
            jax.ShapeDtypeStruct((1024, 256), BF16),
        ),
        in_specs=[SMEM, VMEM, VMEM, VMEM, ANY],
        out_specs=(VMEM,) * 3,
        compiler_params=PARAMS,
        name="ask_queries",
    )(
        here.reshape(1),
        jnp.pad(lent_req, (0, 64), constant_values=-4).reshape(32, 128),
        queries,
        out_weight,
        done,
    )
    received = lax.ppermute(sent, "zp", [(0, 1), (1, 0)])
    home_out, home_stat, base = pl.pallas_call(
        home_kernel,
        out_shape=(
            jax.ShapeDtypeStruct((64, 128), F32),
            jax.ShapeDtypeStruct((2, 128), F32),
            jax.ShapeDtypeStruct((32, 256), F32),
        ),
        in_specs=[SMEM] + [VMEM] * 6,
        out_specs=(VMEM,) * 3,
        compiler_params=PARAMS,
        name="home_part",
    )(
        home_len,
        queries,
        new_keys.reshape(4, 128),
        new_values.reshape(4, 128),
        home_keys.reshape(4, 256, 128),
        home_values.reshape(4, 256, 128),
        residual,
    )
    copies = pl.pallas_call(
        attend_kernel,
        out_shape=jax.ShapeDtypeStruct((64, 32, 128), BF16),
        in_specs=[VMEM] * 5,
        out_specs=VMEM,
        scratch_shapes=[pltpu.VMEM((1024, 128), F32)],
        compiler_params=PARAMS,
        name="attend",
    )(asked, req, home_stat, home_out, recv)
    rows = lax.all_to_all(copies, INST, split_axis=0, concat_axis=0, tiled=True)
    weights = pl.pallas_call(
        join_kernel,
        out_shape=jax.ShapeDtypeStruct((2, 1024, 256), BF16),
        in_specs=[VMEM, VMEM],
        out_specs=VMEM,
        compiler_params=PARAMS,
        cost_estimate=pl.CostEstimate(flops=10**11, bytes_accessed=2**21, transcendentals=0),
        name="join_weights",
    )(out_weight, received)
    partial = pl.pallas_call(
        project_kernel,
        out_shape=jax.ShapeDtypeStruct((2, 8, 32, 256), BF16),
        in_specs=[VMEM, VMEM],
        out_specs=VMEM,
        scratch_shapes=[pltpu.VMEM((256, 1024), BF16)],
        compiler_params=PARAMS,
        name="project",
    )(rows, weights)
    sums = lax.all_to_all(
        partial.reshape(16, 32, 256), ("zp", "tp"), split_axis=0, concat_axis=0, tiled=True
    )
    return pl.pallas_call(
        finish_kernel,
        out_shape=jax.ShapeDtypeStruct((32, 256), BF16),
        in_specs=[VMEM, VMEM],
        out_specs=VMEM,
        compiler_params=PARAMS,
        name="finish",
    )(sums, base)


def solution(mesh):
    placed = (
        P(INST, "tp", None),
        P(INST, "tp", None),
        P(INST, "tp", None),
        P(INST, None, "tp", None),
        P(INST, None, "tp", None),
        P(INST),
        P(INST, None, "tp", None),
        P(INST, None, "tp", None),
        P(),
        P(INST),
        P("tp", INST),
        P("tp", INST),
    )
    fine = Mesh(mesh.devices.reshape(8, 4, 2, 8), INST + ("tp",))
    return jax.shard_map(
        body, mesh=fine, in_specs=placed, out_specs=P("tp", INST), check_vma=False
    )
```

```python
import math

import jax
import jax.numpy as jnp
from jax import lax
from jax.experimental import pallas as pl
from jax.experimental.pallas import tpu as pltpu
from jax.sharding import Mesh, PartitionSpec as P

VERY_LOW = -1e30
ABSENT = 64.0
SCALE = 1.0 / math.sqrt(128.0)
F32 = jnp.float32
BF16 = jnp.bfloat16
NT = (((1,), (1,)), ((), ()))
TN = (((0,), (0,)), ((), ()))
NN = (((1,), (0,)), ((), ()))
INST = ("y", "zh", "zp")
FIRST = 52
ORDER = [[(FIRST + k) % 64 for k in range(64)]]
PARAMS = pltpu.CompilerParams(vmem_limit_bytes=16 * 2**20)
SMEM = pl.BlockSpec(memory_space=pltpu.SMEM)
ANY = pl.BlockSpec(memory_space=pl.ANY)
VMEM = pl.BlockSpec(memory_space=pltpu.VMEM)


def dot(a, b, dims):
    return lax.dot_general(a, b, dims, preferred_element_type=F32)


def iota(shape, axis):
    return lax.broadcasted_iota(jnp.int32, shape, axis)


def halves(x):
    high = x.astype(BF16)
    return high, (x - high.astype(F32)).astype(BF16)


def ask_kernel(
    here_ref, table_ref, q_ref, weight_ref, packed_ref, asked_ref, req_ref, sent_ref
):
    first = pl.multiple_of((1 - lax.axis_index("zp")) * 1024, 1024)
    sent_ref[...] = weight_ref[pl.ds(first, 1024)]
    here = here_ref[0]
    table = table_ref[...]
    found = jnp.where((table >> 2) == here, (table & 3) + 1, 0).astype(F32)
    lane = iota((1, 128), 1)
    rows = []
    for j in ORDER[0]:
        line, first = divmod(63 * j, 128)
        row = jnp.where(lane >= first, found[line : line + 1], 0.0)
        if first + 63 <= 128:
            row = jnp.where(lane < first + 63, row, 0.0)
        else:
            row = jnp.where(lane < first + 63 - 128, found[line + 1 : line + 2], row)
        rows.append(row)
    source = jnp.sum(jnp.concatenate(rows, axis=0), axis=1, keepdims=True) - 1.0
    source = jnp.broadcast_to(source, (64, 128))
    query = [q_ref[r].astype(F32) for r in range(4)]
    for g in range(8):
        rows = []
        for j in range(8 * g, 8 * g + 8):
            s = jnp.broadcast_to(source[j : j + 1], (16, 128))
            picked = jnp.where(s == 1.0, query[1], query[0])
            picked = jnp.where(s == 2.0, query[2], picked)
            rows.append(jnp.where(s == 3.0, query[3], picked))
        asked_ref[g] = jnp.concatenate(rows, axis=0).T.astype(BF16)
    group = iota((8, 128), 1) >> 4
    split = source.reshape(8, 8, 128)
    req = jnp.zeros((8, 128), F32)
    for n in range(8):
        req = jnp.where(group == n, split[:, n], req)
    req_ref[...] = req


def pack_kernel(
    req_ref, len_ref, k_ref, v_ref, out_ref,
    req_in, len_in, k_in, v_in, keys_ref, values_ref, sems
):
    loads = [
        pltpu.make_async_copy(source, target, sems.at[i])
        for i, (source, target) in enumerate(
            [(req_ref, req_in), (len_ref, len_in), (k_ref, k_in), (v_ref, v_in)]
        )
    ]
    for load in loads:
        load.start()
    here = lax.axis_index(INST)
    place = (here - FIRST) & 63
    token = iota((32, 128), 0)
    keys_ref[place] = jnp.full((32, 128), ABSENT, F32).astype(BF16)
    values_ref[place] = jnp.zeros((32, 128), F32).astype(BF16)
    for load in loads[:3]:
        load.wait()
    for s in range(63):
        keys = jnp.where(token < len_in[s], k_in[s].astype(F32), ABSENT)
        keys_ref[((req_in[63 * here + s] >> 2) - FIRST) & 63] = keys.astype(BF16)
    send_keys = pltpu.make_async_copy(keys_ref, out_ref.at[:, pl.ds(0, 32)], sems.at[4])
    send_keys.start()
    loads[3].wait()
    for s in range(63):
        values_ref[((req_in[63 * here + s] >> 2) - FIRST) & 63] = v_in[s]
    send_values = pltpu.make_async_copy(values_ref, out_ref.at[:, pl.ds(32, 32)], sems.at[5])
    send_values.start()
    send_keys.wait()
    send_values.wait()


def home_kernel(
    len_ref, q_ref, nk_ref, nv_ref, k_ref, v_ref, residual_ref, out_ref, stat_ref, base_ref
):
    query = q_ref[...].reshape(64, 128)
    query = jnp.concatenate([query, query], axis=0)
    owner = (iota((256, 128), 1) >> 4) & 3
    token = iota((256, 128), 0)
    scores = jnp.zeros((256, 128), F32)
    length = jnp.zeros((256, 128), jnp.int32)
    for r in range(4):
        scores = jnp.where(owner == r, dot(k_ref[r], query, NT), scores)
        length = jnp.where(owner == r, len_ref[r], length)
    scores = jnp.where(token < length, scores * SCALE, VERY_LOW)
    mine = ((iota((4, 128), 1) >> 4) & 3) == iota((4, 128), 0)
    fresh = dot(nk_ref[...], query, NT) * SCALE
    fresh = jnp.sum(jnp.where(mine, fresh, 0.0), axis=0, keepdims=True)
    top = jnp.maximum(jnp.max(scores, axis=0, keepdims=True), fresh)
    weights = jnp.exp(scores - top)
    own = jnp.exp(fresh - top)
    total = jnp.sum(weights, axis=0, keepdims=True) + own
    mixed = dot(jnp.where(mine, own, 0.0).astype(BF16), nv_ref[...], TN)
    for r in range(4):
        mixed += dot(jnp.where(owner == r, weights, 0.0).astype(BF16), v_ref[r], TN)
    out_ref[...] = mixed[:64]
    stat_ref[...] = jnp.concatenate([top, total], axis=0)
    base_ref[...] = residual_ref[...].astype(F32)


def attend_kernel(q_ref, req_ref, stat_ref, home_ref, recv_ref, out_ref, mixed_ref):
    owner = iota((32, 128), 1) >> 4
    far_tops, far_totals = [], []
    for g in range(8):
        here = pl.ds(8 * g, 8)
        keys = recv_ref[here, :32, :].reshape(256, 128)
        raw = dot(keys, q_ref[g], NN)
        mark = keys.astype(F32)
        scores, marks = raw[:32], mark[:32]
        for j in range(1, 8):
            scores = jnp.where(owner == j, raw[32 * j : 32 * j + 32], scores)
            marks = jnp.where(owner == j, mark[32 * j : 32 * j + 32], marks)
        scores = jnp.where(marks < 0.5 * ABSENT, scores * SCALE, VERY_LOW)
        top = jnp.max(scores, axis=0, keepdims=True)
        weights = jnp.exp(scores - top)
        far_tops.append(top)
        far_totals.append(jnp.sum(weights, axis=0, keepdims=True))
        blocks = jnp.concatenate(
            [jnp.where(owner == j, weights, 0.0) for j in range(8)], axis=0
        ).astype(BF16)
        values = recv_ref[here, 32:, :].reshape(256, 128)
        mixed_ref[128 * g : 128 * g + 128] = dot(blocks, values, TN)
    far_top = jnp.concatenate(far_tops, axis=0)
    far_total = jnp.concatenate(far_totals, axis=0)
    near_top, near_total = stat_ref[0:1], stat_ref[1:2]
    which = iota((1, 128), 1) >> 4
    req = req_ref[...]
    tops = []
    for r in range(4):
        t = jnp.max(jnp.where(req == r, far_top, VERY_LOW), axis=0, keepdims=True)
        tops.append(jnp.maximum(t, jnp.where(which == r, near_top, VERY_LOW)))
    peak = jnp.concatenate(tops, axis=0)
    for shift in (16, 32, 64):
        peak = jnp.maximum(peak, pltpu.roll(peak, shift, 1))
    far_w, near_w, totals = [], [], []
    for r in range(4):
        p = peak[r : r + 1]
        f = jnp.where(req == r, jnp.exp(far_top - p), 0.0)
        n = jnp.where(which == r, jnp.exp(near_top - p), 0.0)
        far_w.append(f)
        near_w.append(n)
        totals.append(jnp.sum(f * far_total, axis=0, keepdims=True) + n * near_total)
    total = jnp.concatenate(totals, axis=0)
    for shift in (16, 32, 64):
        total = total + pltpu.roll(total, shift, 1)
    scale = 1.0 / total
    same = (iota((16, 128), 1) & 15) == iota((16, 128), 0)

    def spread_rows(rows):
        return halves(jnp.concatenate([jnp.where(same, row, 0.0) for row in rows], axis=0))

    high, low = spread_rows([near_w[r] * scale[r : r + 1] for r in range(4)])
    home_high, home_low = halves(home_ref[...])
    acc = dot(high[:, :64], home_high, NN) + dot(high[:, :64], home_low, NN)
    acc += dot(low[:, :64], home_high, NN)
    far_w = [far_w[r] * scale[r : r + 1] for r in range(4)]
    for g in range(8):
        high, low = spread_rows([far_w[r][g : g + 1] for r in range(4)])
        mixed_high, mixed_low = halves(mixed_ref[128 * g : 128 * g + 128])
        acc += dot(high, mixed_high, NN) + dot(high, mixed_low, NN) + dot(low, mixed_high, NN)
    lower = jnp.concatenate([acc[16 * r : 16 * r + 8] for r in range(4)], axis=0)
    upper = jnp.concatenate([acc[16 * r + 8 : 16 * r + 16] for r in range(4)], axis=0)
    split = jnp.concatenate([lower, upper], axis=0).astype(BF16).reshape(1, 2, 32, 128)
    out_ref[...] = jnp.broadcast_to(split, (32, 2, 32, 128)).reshape(64, 32, 128)


def join_kernel(mine_ref, received_ref, out_ref):
    zp = lax.axis_index("zp")
    out_ref[zp] = mine_ref[pl.ds(pl.multiple_of(zp * 1024, 1024), 1024)]
    out_ref[1 - zp] = received_ref[...]


def project_kernel(rows_ref, weight_ref, out_ref, wide_ref):
    q = iota((256, 256), 0)
    p = iota((256, 256), 1)
    move = p == 32 * ((q >> 2) & 7) + 8 * (q & 3) + (q >> 5)
    move = move.astype(F32).astype(BF16)
    for b in range(8):
        moved = dot(move, rows_ref[8 * b : 8 * b + 8].reshape(256, 128), NN).astype(BF16)
        for h in range(8):
            wide_ref[32 * b : 32 * b + 32, 128 * h : 128 * h + 128] = moved[32 * h : 32 * h + 32]
    wide = wide_ref[...]
    for c in range(2):
        out_ref[c] = dot(wide, weight_ref[c], NN).astype(BF16).reshape(8, 32, 256)


def finish_kernel(sums_ref, base_ref, out_ref):
    total = base_ref[...]
    for s in range(16):
        total = total + sums_ref[s].astype(F32)
    out_ref[...] = total.astype(BF16)


def body(
    queries,
    new_keys,
    new_values,
    home_keys,
    home_values,
    home_len,
    lent_keys,
    lent_values,
    lent_req,
    lent_len,
    out_weight,
    residual,
):
    here = lax.axis_index(INST)
    packed = pl.pallas_call(
        pack_kernel,
        out_shape=jax.ShapeDtypeStruct((64, 64, 128), BF16),
        in_specs=[ANY] * 4,
        out_specs=ANY,
        scratch_shapes=[
            pltpu.SMEM((4032,), jnp.int32),
            pltpu.SMEM((63,), jnp.int32),
            pltpu.VMEM((63, 32, 128), BF16),
            pltpu.VMEM((63, 32, 128), BF16),
            pltpu.VMEM((64, 32, 128), BF16),
            pltpu.VMEM((64, 32, 128), BF16),
            pltpu.SemaphoreType.DMA((6,)),
        ],
        name="pack_lent",
    )(
        lent_req,
        lent_len,
        lent_keys.reshape(63, 32, 128),
        lent_values.reshape(63, 32, 128),
    )
    recv = lax.all_to_all(
        packed, INST, split_axis=0, concat_axis=0, tiled=True, axis_index_groups=ORDER
    )
    asked, req, sent = pl.pallas_call(
        ask_kernel,
        out_shape=(
            jax.ShapeDtypeStruct((8, 128, 128), BF16),
            jax.ShapeDtypeStruct((8, 128), F32),
            jax.ShapeDtypeStruct((1024, 256), BF16),
        ),
        in_specs=[SMEM, VMEM, VMEM, VMEM, ANY],
        out_specs=(VMEM,) * 3,
        compiler_params=PARAMS,
        name="ask_queries",
    )(
        here.reshape(1),
        jnp.pad(lent_req, (0, 64), constant_values=-4).reshape(32, 128),
        queries,
        out_weight,
        packed,
    )
    received = lax.ppermute(sent, "zp", [(0, 1), (1, 0)])
    home_out, home_stat, base = pl.pallas_call(
        home_kernel,
        out_shape=(
            jax.ShapeDtypeStruct((64, 128), F32),
            jax.ShapeDtypeStruct((2, 128), F32),
            jax.ShapeDtypeStruct((32, 256), F32),
        ),
        in_specs=[SMEM] + [VMEM] * 6,
        out_specs=(VMEM,) * 3,
        compiler_params=PARAMS,
        name="home_part",
    )(
        home_len,
        queries,
        new_keys.reshape(4, 128),
        new_values.reshape(4, 128),
        home_keys.reshape(4, 256, 128),
        home_values.reshape(4, 256, 128),
        residual,
    )
    copies = pl.pallas_call(
        attend_kernel,
        out_shape=jax.ShapeDtypeStruct((64, 32, 128), BF16),
        in_specs=[VMEM] * 5,
        out_specs=VMEM,
        scratch_shapes=[pltpu.VMEM((1024, 128), F32)],
        compiler_params=PARAMS,
        name="attend",
    )(asked, req, home_stat, home_out, recv)
    rows = lax.all_to_all(copies, INST, split_axis=0, concat_axis=0, tiled=True)
    weights = pl.pallas_call(
        join_kernel,
        out_shape=jax.ShapeDtypeStruct((2, 1024, 256), BF16),
        in_specs=[VMEM, VMEM],
        out_specs=VMEM,
        compiler_params=PARAMS,
        cost_estimate=pl.CostEstimate(flops=10**11, bytes_accessed=2**21, transcendentals=0),
        name="join_weights",
    )(out_weight, received)
    partial = pl.pallas_call(
        project_kernel,
        out_shape=jax.ShapeDtypeStruct((2, 8, 32, 256), BF16),
        in_specs=[VMEM, VMEM],
        out_specs=VMEM,
        scratch_shapes=[pltpu.VMEM((256, 1024), BF16)],
        compiler_params=PARAMS,
        name="project",
    )(rows, weights)
    sums = lax.all_to_all(
        partial.reshape(16, 32, 256), ("zp", "tp"), split_axis=0, concat_axis=0, tiled=True
    )
    return pl.pallas_call(
        finish_kernel,
        out_shape=jax.ShapeDtypeStruct((32, 256), BF16),
        in_specs=[VMEM, VMEM],
        out_specs=VMEM,
        compiler_params=PARAMS,
        name="finish",
    )(sums, base)


def solution(mesh):
    placed = (
        P(INST, "tp", None),
        P(INST, "tp", None),
        P(INST, "tp", None),
        P(INST, None, "tp", None),
        P(INST, None, "tp", None),
        P(INST),
        P(INST, None, "tp", None),
        P(INST, None, "tp", None),
        P(),
        P(INST),
        P("tp", INST),
        P("tp", INST),
    )
    fine = Mesh(mesh.devices.reshape(8, 4, 2, 8), INST + ("tp",))
    return jax.shard_map(
        body, mesh=fine, in_specs=placed, out_specs=P("tp", INST), check_vma=False
    )
```

```python
import math

import jax
import jax.numpy as jnp
from jax import lax
from jax.experimental import pallas as pl
from jax.experimental.pallas import tpu as pltpu
from jax.sharding import Mesh, PartitionSpec as P

VERY_LOW = -1e30
ABSENT = 64.0
SCALE = 1.0 / math.sqrt(128.0)
F32 = jnp.float32
BF16 = jnp.bfloat16
NT = (((1,), (1,)), ((), ()))
TN = (((0,), (0,)), ((), ()))
NN = (((1,), (0,)), ((), ()))
INST = ("y", "zh", "zp")
FIRST = 52
ORDER = [[(FIRST + k) % 64 for k in range(64)]]
PARAMS = pltpu.CompilerParams(vmem_limit_bytes=16 * 2**20)
SMEM = pl.BlockSpec(memory_space=pltpu.SMEM)
ANY = pl.BlockSpec(memory_space=pl.ANY)
VMEM = pl.BlockSpec(memory_space=pltpu.VMEM)


def dot(a, b, dims):
    return lax.dot_general(a, b, dims, preferred_element_type=F32)


def iota(shape, axis):
    return lax.broadcasted_iota(jnp.int32, shape, axis)


def halves(x):
    high = x.astype(BF16)
    return high, (x - high.astype(F32)).astype(BF16)


def ask_kernel(
    here_ref, table_ref, q_ref, weight_ref, packed_ref, asked_ref, req_ref, sent_ref
):
    first = pl.multiple_of((1 - lax.axis_index("zp")) * 1024, 1024)
    sent_ref[...] = weight_ref[pl.ds(first, 1024)]
    here = here_ref[0]
    table = table_ref[...]
    found = jnp.where((table >> 2) == here, (table & 3) + 1, 0).astype(F32)
    lane = iota((1, 128), 1)
    rows = []
    for j in ORDER[0]:
        line, first = divmod(63 * j, 128)
        row = jnp.where(lane >= first, found[line : line + 1], 0.0)
        if first + 63 <= 128:
            row = jnp.where(lane < first + 63, row, 0.0)
        else:
            row = jnp.where(lane < first + 63 - 128, found[line + 1 : line + 2], row)
        rows.append(row)
    source = jnp.sum(jnp.concatenate(rows, axis=0), axis=1, keepdims=True) - 1.0
    source = jnp.broadcast_to(source, (64, 128))
    query = [q_ref[r].astype(F32) for r in range(4)]
    for g in range(8):
        rows = []
        for j in range(8 * g, 8 * g + 8):
            s = jnp.broadcast_to(source[j : j + 1], (16, 128))
            picked = jnp.where(s == 1.0, query[1], query[0])
            picked = jnp.where(s == 2.0, query[2], picked)
            rows.append(jnp.where(s == 3.0, query[3], picked))
        asked_ref[g, :128] = jnp.concatenate(rows, axis=0).astype(BF16)
        asked_ref[g, 128:] = (iota((16, 128), 1) == 0).astype(F32).astype(BF16)
    group = iota((8, 128), 1) >> 4
    split = source.reshape(8, 8, 128)
    req = jnp.zeros((8, 128), F32)
    for n in range(8):
        req = jnp.where(group == n, split[:, n], req)
    req_ref[...] = req


def pack_kernel(
    req_ref, len_ref, k_ref, v_ref, out_ref,
    req_in, len_in, k_in, v_in, keys_ref, values_ref, sems
):
    loads = [
        pltpu.make_async_copy(source, target, sems.at[i])
        for i, (source, target) in enumerate(
            [(req_ref, req_in), (len_ref, len_in), (k_ref, k_in), (v_ref, v_in)]
        )
    ]
    for load in loads:
        load.start()
    here = lax.axis_index(INST)
    place = (here - FIRST) & 63
    token = iota((32, 128), 0)
    keys_ref[place] = jnp.full((32, 128), ABSENT, F32).astype(BF16)
    values_ref[place] = jnp.zeros((32, 128), F32).astype(BF16)
    for load in loads[:3]:
        load.wait()
    for s in range(63):
        keys = jnp.where(token < len_in[s], k_in[s].astype(F32), ABSENT)
        keys_ref[((req_in[63 * here + s] >> 2) - FIRST) & 63] = keys.astype(BF16)
    send_keys = pltpu.make_async_copy(keys_ref, out_ref.at[:, pl.ds(0, 32)], sems.at[4])
    send_keys.start()
    loads[3].wait()
    for s in range(63):
        values_ref[((req_in[63 * here + s] >> 2) - FIRST) & 63] = v_in[s]
    send_values = pltpu.make_async_copy(values_ref, out_ref.at[:, pl.ds(32, 32)], sems.at[5])
    send_values.start()
    send_keys.wait()
    send_values.wait()


def home_kernel(
    len_ref, q_ref, nk_ref, nv_ref, k_ref, v_ref, residual_ref, out_ref, stat_ref, base_ref
):
    query = q_ref[...].reshape(64, 128)
    query = jnp.concatenate([query, query], axis=0)
    owner = (iota((256, 128), 1) >> 4) & 3
    token = iota((256, 128), 0)
    scores = jnp.zeros((256, 128), F32)
    length = jnp.zeros((256, 128), jnp.int32)
    for r in range(4):
        scores = jnp.where(owner == r, dot(k_ref[r], query, NT), scores)
        length = jnp.where(owner == r, len_ref[r], length)
    scores = jnp.where(token < length, scores * SCALE, VERY_LOW)
    mine = ((iota((4, 128), 1) >> 4) & 3) == iota((4, 128), 0)
    fresh = dot(nk_ref[...], query, NT) * SCALE
    fresh = jnp.sum(jnp.where(mine, fresh, 0.0), axis=0, keepdims=True)
    top = jnp.maximum(jnp.max(scores, axis=0, keepdims=True), fresh)
    weights = jnp.exp(scores - top)
    own = jnp.exp(fresh - top)
    total = jnp.sum(weights, axis=0, keepdims=True) + own
    mixed = dot(jnp.where(mine, own, 0.0).astype(BF16), nv_ref[...], TN)
    for r in range(4):
        mixed += dot(jnp.where(owner == r, weights, 0.0).astype(BF16), v_ref[r], TN)
    out_ref[...] = mixed[:64]
    stat_ref[...] = jnp.concatenate([top, total], axis=0)
    base_ref[...] = residual_ref[...].astype(F32)


def attend_kernel(q_ref, req_ref, stat_ref, home_ref, recv_ref, out_ref, mixed_ref):
    block = (iota((128, 256), 0) >> 4) == (iota((128, 256), 1) >> 5)
    lane = iota((128, 128), 1)
    columns = jnp.zeros((128, 128), F32)
    for g in range(8):
        group = pl.ds(8 * g, 8)
        keys = recv_ref[group, :32, :].reshape(256, 128)
        raw = dot(q_ref[g], keys, NT)
        valid = block & (raw[128:129] < 0.5 * ABSENT)
        scores = jnp.where(valid, raw[:128] * SCALE, VERY_LOW)
        top = jnp.max(scores, axis=1, keepdims=True)
        weights = jnp.exp(scores - top)
        total = jnp.sum(weights, axis=1, keepdims=True)
        columns = jnp.where(lane == g, top, jnp.where(lane == 8 + g, total, columns))
        values = recv_ref[group, 32:, :].reshape(256, 128)
        mixed_ref[128 * g : 128 * g + 128] = dot(weights.astype(BF16), values, NN)
    stats = columns.T
    far_top, far_total = stats[:8], stats[8:16]
    near_top, near_total = stat_ref[0:1], stat_ref[1:2]
    which = iota((1, 128), 1) >> 4
    req = req_ref[...]
    tops = []
    for r in range(4):
        t = jnp.max(jnp.where(req == r, far_top, VERY_LOW), axis=0, keepdims=True)
        tops.append(jnp.maximum(t, jnp.where(which == r, near_top, VERY_LOW)))
    peak = jnp.concatenate(tops, axis=0)
    for shift in (16, 32, 64):
        peak = jnp.maximum(peak, pltpu.roll(peak, shift, 1))
    far_w, near_w, totals = [], [], []
    for r in range(4):
        p = peak[r : r + 1]
        f = jnp.where(req == r, jnp.exp(far_top - p), 0.0)
        n = jnp.where(which == r, jnp.exp(near_top - p), 0.0)
        far_w.append(f)
        near_w.append(n)
        totals.append(jnp.sum(f * far_total, axis=0, keepdims=True) + n * near_total)
    total = jnp.concatenate(totals, axis=0)
    for shift in (16, 32, 64):
        total = total + pltpu.roll(total, shift, 1)
    scale = 1.0 / total
    same = (iota((16, 128), 1) & 15) == iota((16, 128), 0)

    def spread_rows(rows):
        return halves(jnp.concatenate([jnp.where(same, row, 0.0) for row in rows], axis=0))

    high, low = spread_rows([near_w[r] * scale[r : r + 1] for r in range(4)])
    home_high, home_low = halves(home_ref[...])
    acc = dot(high[:, :64], home_high, NN) + dot(high[:, :64], home_low, NN)
    acc += dot(low[:, :64], home_high, NN)
    far_w = [far_w[r] * scale[r : r + 1] for r in range(4)]
    for g in range(8):
        high, low = spread_rows([far_w[r][g : g + 1] for r in range(4)])
        mixed_high, mixed_low = halves(mixed_ref[128 * g : 128 * g + 128])
        acc += dot(high, mixed_high, NN) + dot(high, mixed_low, NN) + dot(low, mixed_high, NN)
    lower = jnp.concatenate([acc[16 * r : 16 * r + 8] for r in range(4)], axis=0)
    upper = jnp.concatenate([acc[16 * r + 8 : 16 * r + 16] for r in range(4)], axis=0)
    split = jnp.concatenate([lower, upper], axis=0).astype(BF16).reshape(1, 2, 32, 128)
    out_ref[...] = jnp.broadcast_to(split, (32, 2, 32, 128)).reshape(64, 32, 128)


def join_kernel(mine_ref, received_ref, out_ref):
    zp = lax.axis_index("zp")
    out_ref[zp] = mine_ref[pl.ds(pl.multiple_of(zp * 1024, 1024), 1024)]
    out_ref[1 - zp] = received_ref[...]


def project_kernel(rows_ref, weight_ref, out_ref, wide_ref):
    q = iota((256, 256), 0)
    p = iota((256, 256), 1)
    move = p == 32 * ((q >> 2) & 7) + 8 * (q & 3) + (q >> 5)
    move = move.astype(F32).astype(BF16)
    for b in range(8):
        parts = [rows_ref[(8 * b + i - FIRST) % 64] for i in range(8)]
        moved = dot(move, jnp.concatenate(parts, axis=0), NN).astype(BF16)
        for h in range(8):
            wide_ref[32 * b : 32 * b + 32, 128 * h : 128 * h + 128] = moved[32 * h : 32 * h + 32]
    wide = wide_ref[...]
    for c in range(2):
        out_ref[c] = dot(wide, weight_ref[c], NN).astype(BF16).reshape(8, 32, 256)


def finish_kernel(sums_ref, base_ref, out_ref):
    total = base_ref[...]
    for s in range(16):
        total = total + sums_ref[s].astype(F32)
    out_ref[...] = total.astype(BF16)


def body(
    queries,
    new_keys,
    new_values,
    home_keys,
    home_values,
    home_len,
    lent_keys,
    lent_values,
    lent_req,
    lent_len,
    out_weight,
    residual,
):
    here = lax.axis_index(INST)
    packed = pl.pallas_call(
        pack_kernel,
        out_shape=jax.ShapeDtypeStruct((64, 64, 128), BF16),
        in_specs=[ANY] * 4,
        out_specs=ANY,
        scratch_shapes=[
            pltpu.SMEM((4032,), jnp.int32),
            pltpu.SMEM((63,), jnp.int32),
            pltpu.VMEM((63, 32, 128), BF16),
            pltpu.VMEM((63, 32, 128), BF16),
            pltpu.VMEM((64, 32, 128), BF16),
            pltpu.VMEM((64, 32, 128), BF16),
            pltpu.SemaphoreType.DMA((6,)),
        ],
        name="pack_lent",
    )(
        lent_req,
        lent_len,
        lent_keys.reshape(63, 32, 128),
        lent_values.reshape(63, 32, 128),
    )
    recv = lax.all_to_all(
        packed, INST, split_axis=0, concat_axis=0, tiled=True, axis_index_groups=ORDER
    )
    asked, req, sent = pl.pallas_call(
        ask_kernel,
        out_shape=(
            jax.ShapeDtypeStruct((8, 144, 128), BF16),
            jax.ShapeDtypeStruct((8, 128), F32),
            jax.ShapeDtypeStruct((1024, 256), BF16),
        ),
        in_specs=[SMEM, VMEM, VMEM, VMEM, ANY],
        out_specs=(VMEM,) * 3,
        compiler_params=PARAMS,
        name="ask_queries",
    )(
        here.reshape(1),
        jnp.pad(lent_req, (0, 64), constant_values=-4).reshape(32, 128),
        queries,
        out_weight,
        packed,
    )
    received = lax.ppermute(sent, "zp", [(0, 1), (1, 0)])
    home_out, home_stat, base = pl.pallas_call(
        home_kernel,
        out_shape=(
            jax.ShapeDtypeStruct((64, 128), F32),
            jax.ShapeDtypeStruct((2, 128), F32),
            jax.ShapeDtypeStruct((32, 256), F32),
        ),
        in_specs=[SMEM] + [VMEM] * 6,
        out_specs=(VMEM,) * 3,
        compiler_params=PARAMS,
        name="home_part",
    )(
        home_len,
        queries,
        new_keys.reshape(4, 128),
        new_values.reshape(4, 128),
        home_keys.reshape(4, 256, 128),
        home_values.reshape(4, 256, 128),
        residual,
    )
    copies = pl.pallas_call(
        attend_kernel,
        out_shape=jax.ShapeDtypeStruct((64, 32, 128), BF16),
        in_specs=[VMEM] * 5,
        out_specs=VMEM,
        scratch_shapes=[pltpu.VMEM((1024, 128), F32)],
        compiler_params=PARAMS,
        name="attend",
    )(asked, req, home_stat, home_out, recv)
    rows = lax.all_to_all(
        copies, INST, split_axis=0, concat_axis=0, tiled=True, axis_index_groups=ORDER
    )
    weights = pl.pallas_call(
        join_kernel,
        out_shape=jax.ShapeDtypeStruct((2, 1024, 256), BF16),
        in_specs=[VMEM, VMEM],
        out_specs=VMEM,
        compiler_params=PARAMS,
        cost_estimate=pl.CostEstimate(flops=10**11, bytes_accessed=2**21, transcendentals=0),
        name="join_weights",
    )(out_weight, received)
    partial = pl.pallas_call(
        project_kernel,
        out_shape=jax.ShapeDtypeStruct((2, 8, 32, 256), BF16),
        in_specs=[VMEM, VMEM],
        out_specs=VMEM,
        scratch_shapes=[pltpu.VMEM((256, 1024), BF16)],
        compiler_params=PARAMS,
        name="project",
    )(rows, weights)
    sums = lax.all_to_all(
        partial.reshape(16, 32, 256), ("zp", "tp"), split_axis=0, concat_axis=0, tiled=True
    )
    return pl.pallas_call(
        finish_kernel,
        out_shape=jax.ShapeDtypeStruct((32, 256), BF16),
        in_specs=[VMEM, VMEM],
        out_specs=VMEM,
        compiler_params=PARAMS,
        name="finish",
    )(sums, base)


def solution(mesh):
    placed = (
        P(INST, "tp", None),
        P(INST, "tp", None),
        P(INST, "tp", None),
        P(INST, None, "tp", None),
        P(INST, None, "tp", None),
        P(INST),
        P(INST, None, "tp", None),
        P(INST, None, "tp", None),
        P(),
        P(INST),
        P("tp", INST),
        P("tp", INST),
    )
    fine = Mesh(mesh.devices.reshape(8, 4, 2, 8), INST + ("tp",))
    return jax.shard_map(
        body, mesh=fine, in_specs=placed, out_specs=P("tp", INST), check_vma=False
    )
```

```python
import math

import jax
import jax.numpy as jnp
from jax import lax
from jax.experimental import pallas as pl
from jax.experimental.pallas import tpu as pltpu
from jax.sharding import Mesh, PartitionSpec as P

VERY_LOW = -1e30
ABSENT = 64.0
SCALE = 1.0 / math.sqrt(128.0)
F32 = jnp.float32
BF16 = jnp.bfloat16
NT = (((1,), (1,)), ((), ()))
TN = (((0,), (0,)), ((), ()))
NN = (((1,), (0,)), ((), ()))
INST = ("y", "zh", "zp")
FIRST = 52
ORDER = [[(FIRST + k) % 64 for k in range(64)]]
PARAMS = pltpu.CompilerParams(vmem_limit_bytes=16 * 2**20)
SMEM = pl.BlockSpec(memory_space=pltpu.SMEM)
ANY = pl.BlockSpec(memory_space=pl.ANY)
VMEM = pl.BlockSpec(memory_space=pltpu.VMEM)


def dot(a, b, dims):
    return lax.dot_general(a, b, dims, preferred_element_type=F32)


def iota(shape, axis):
    return lax.broadcasted_iota(jnp.int32, shape, axis)


def halves(x):
    high = x.astype(BF16)
    return high, (x - high.astype(F32)).astype(BF16)


def ask_kernel(
    here_ref, table_ref, q_ref, weight_ref, packed_ref, asked_ref, req_ref, sent_ref
):
    first = pl.multiple_of((1 - lax.axis_index("zp")) * 1024, 1024)
    sent_ref[...] = weight_ref[pl.ds(first, 1024)]
    here = here_ref[0]
    table = table_ref[...]
    found = jnp.where((table >> 2) == here, (table & 3) + 1, 0).astype(F32)
    lane = iota((1, 128), 1)
    rows = []
    for j in ORDER[0]:
        line, first = divmod(63 * j, 128)
        row = jnp.where(lane >= first, found[line : line + 1], 0.0)
        if first + 63 <= 128:
            row = jnp.where(lane < first + 63, row, 0.0)
        else:
            row = jnp.where(lane < first + 63 - 128, found[line + 1 : line + 2], row)
        rows.append(row)
    source = jnp.sum(jnp.concatenate(rows, axis=0), axis=1, keepdims=True) - 1.0
    source = jnp.broadcast_to(source, (64, 128))
    query = [q_ref[r].astype(F32) for r in range(4)]
    for g in range(8):
        rows = []
        for j in range(8 * g, 8 * g + 8):
            s = jnp.broadcast_to(source[j : j + 1], (16, 128))
            picked = jnp.where(s == 1.0, query[1], query[0])
            picked = jnp.where(s == 2.0, query[2], picked)
            rows.append(jnp.where(s == 3.0, query[3], picked))
        asked_ref[g] = jnp.concatenate(rows, axis=0).T.astype(BF16)
    group = iota((8, 128), 1) >> 4
    split = source.reshape(8, 8, 128)
    req = jnp.zeros((8, 128), F32)
    for n in range(8):
        req = jnp.where(group == n, split[:, n], req)
    req_ref[...] = req


def pack_kernel(
    req_ref, len_ref, k_ref, v_ref, out_ref,
    req_in, len_in, k_in, v_in, keys_ref, values_ref, sems
):
    loads = [
        pltpu.make_async_copy(source, target, sems.at[i])
        for i, (source, target) in enumerate(
            [(req_ref, req_in), (len_ref, len_in), (k_ref, k_in), (v_ref, v_in)]
        )
    ]
    for load in loads:
        load.start()
    here = lax.axis_index(INST)
    place = (here - FIRST) & 63
    token = iota((32, 128), 0)
    keys_ref[place] = jnp.full((32, 128), ABSENT, F32).astype(BF16)
    values_ref[place] = jnp.zeros((32, 128), F32).astype(BF16)
    for load in loads[:3]:
        load.wait()
    for s in range(63):
        length = len_in[s]
        absent = ABSENT + length.astype(F32)
        keys = jnp.where(token < length, k_in[s].astype(F32), absent)
        keys_ref[((req_in[63 * here + s] >> 2) - FIRST) & 63] = keys.astype(BF16)
    send_keys = pltpu.make_async_copy(keys_ref, out_ref.at[:, pl.ds(0, 32)], sems.at[4])
    send_keys.start()
    loads[3].wait()
    for s in range(63):
        values_ref[((req_in[63 * here + s] >> 2) - FIRST) & 63] = v_in[s]
    send_values = pltpu.make_async_copy(values_ref, out_ref.at[:, pl.ds(32, 32)], sems.at[5])
    send_values.start()
    send_keys.wait()
    send_values.wait()


def home_kernel(
    len_ref, q_ref, nk_ref, nv_ref, k_ref, v_ref, residual_ref, out_ref, stat_ref, base_ref
):
    query = q_ref[...].reshape(64, 128)
    query = jnp.concatenate([query, query], axis=0)
    owner = (iota((256, 128), 1) >> 4) & 3
    token = iota((256, 128), 0)
    scores = jnp.zeros((256, 128), F32)
    length = jnp.zeros((256, 128), jnp.int32)
    for r in range(4):
        scores = jnp.where(owner == r, dot(k_ref[r], query, NT), scores)
        length = jnp.where(owner == r, len_ref[r], length)
    scores = jnp.where(token < length, scores * SCALE, VERY_LOW)
    mine = ((iota((4, 128), 1) >> 4) & 3) == iota((4, 128), 0)
    fresh = dot(nk_ref[...], query, NT) * SCALE
    fresh = jnp.sum(jnp.where(mine, fresh, 0.0), axis=0, keepdims=True)
    top = jnp.maximum(jnp.max(scores, axis=0, keepdims=True), fresh)
    weights = jnp.exp(scores - top)
    own = jnp.exp(fresh - top)
    total = jnp.sum(weights, axis=0, keepdims=True) + own
    mixed = dot(jnp.where(mine, own, 0.0).astype(BF16), nv_ref[...], TN)
    for r in range(4):
        mixed += dot(jnp.where(owner == r, weights, 0.0).astype(BF16), v_ref[r], TN)
    out_ref[...] = mixed[:64]
    stat_ref[...] = jnp.concatenate([top, total], axis=0)
    base_ref[...] = residual_ref[...].astype(F32)


def attend_kernel(q_ref, req_ref, stat_ref, home_ref, recv_ref, out_ref, mixed_ref):
    owner = iota((32, 128), 1) >> 4
    token = iota((32, 128), 0).astype(F32)
    holder = (iota((8, 128), 1) >> 4) == iota((8, 128), 0)
    keep = [(owner == j).astype(F32).astype(BF16) for j in range(8)]
    far_tops, far_totals = [], []
    for g in range(8):
        group = pl.ds(8 * g, 8)
        keys = recv_ref[group, :32, :].reshape(256, 128)
        raw = dot(keys, q_ref[g], NN)
        last = recv_ref[group, 31, :].astype(F32)
        length = jnp.where(last < 0.5 * ABSENT, 32.0, last - ABSENT)
        length = jnp.sum(jnp.where(holder, length, 0.0), axis=0, keepdims=True)
        scores = raw[:32]
        for j in range(1, 8):
            scores = jnp.where(owner == j, raw[32 * j : 32 * j + 32], scores)
        scores = jnp.where(token < length, scores * SCALE, VERY_LOW)
        top = jnp.max(scores, axis=0, keepdims=True)
        weights = jnp.exp(scores - top)
        far_tops.append(top)
        far_totals.append(jnp.sum(weights, axis=0, keepdims=True))
        weights = weights.astype(BF16)
        blocks = jnp.concatenate([weights * keep[j] for j in range(8)], axis=0)
        values = recv_ref[group, 32:, :].reshape(256, 128)
        mixed_ref[128 * g : 128 * g + 128] = dot(blocks, values, TN)
    far_top = jnp.concatenate(far_tops, axis=0)
    far_total = jnp.concatenate(far_totals, axis=0)
    near_top, near_total = stat_ref[0:1], stat_ref[1:2]
    which = iota((1, 128), 1) >> 4
    req = req_ref[...]
    tops = []
    for r in range(4):
        t = jnp.max(jnp.where(req == r, far_top, VERY_LOW), axis=0, keepdims=True)
        tops.append(jnp.maximum(t, jnp.where(which == r, near_top, VERY_LOW)))
    peak = jnp.concatenate(tops, axis=0)
    for shift in (16, 32, 64):
        peak = jnp.maximum(peak, pltpu.roll(peak, shift, 1))
    far_w, near_w, totals = [], [], []
    for r in range(4):
        p = peak[r : r + 1]
        f = jnp.where(req == r, jnp.exp(far_top - p), 0.0)
        n = jnp.where(which == r, jnp.exp(near_top - p), 0.0)
        far_w.append(f)
        near_w.append(n)
        totals.append(jnp.sum(f * far_total, axis=0, keepdims=True) + n * near_total)
    total = jnp.concatenate(totals, axis=0)
    for shift in (16, 32, 64):
        total = total + pltpu.roll(total, shift, 1)
    scale = 1.0 / total
    same = (iota((16, 128), 1) & 15) == iota((16, 128), 0)

    def spread_rows(rows):
        return halves(jnp.concatenate([jnp.where(same, row, 0.0) for row in rows], axis=0))

    high, low = spread_rows([near_w[r] * scale[r : r + 1] for r in range(4)])
    home_high, home_low = halves(home_ref[...])
    acc = dot(high[:, :64], home_high, NN) + dot(high[:, :64], home_low, NN)
    acc += dot(low[:, :64], home_high, NN)
    far_w = [far_w[r] * scale[r : r + 1] for r in range(4)]
    for g in range(8):
        high, low = spread_rows([far_w[r][g : g + 1] for r in range(4)])
        mixed_high, mixed_low = halves(mixed_ref[128 * g : 128 * g + 128])
        acc += dot(high, mixed_high, NN) + dot(high, mixed_low, NN) + dot(low, mixed_high, NN)
    lower = jnp.concatenate([acc[16 * r : 16 * r + 8] for r in range(4)], axis=0)
    upper = jnp.concatenate([acc[16 * r + 8 : 16 * r + 16] for r in range(4)], axis=0)
    split = jnp.concatenate([lower, upper], axis=0).astype(BF16).reshape(1, 2, 32, 128)
    out_ref[...] = jnp.broadcast_to(split, (32, 2, 32, 128)).reshape(64, 32, 128)


def join_kernel(mine_ref, received_ref, out_ref):
    zp = lax.axis_index("zp")
    out_ref[zp] = mine_ref[pl.ds(pl.multiple_of(zp * 1024, 1024), 1024)]
    out_ref[1 - zp] = received_ref[...]


def project_kernel(rows_ref, weight_ref, out_ref, wide_ref):
    q = iota((256, 256), 0)
    p = iota((256, 256), 1)
    move = p == 32 * ((q >> 2) & 7) + 8 * (q & 3) + (q >> 5)
    move = move.astype(F32).astype(BF16)
    for b in range(8):
        parts = [rows_ref[(8 * b + i - FIRST) % 64] for i in range(8)]
        moved = dot(move, jnp.concatenate(parts, axis=0), NN).astype(BF16)
        for h in range(8):
            wide_ref[32 * b : 32 * b + 32, 128 * h : 128 * h + 128] = moved[32 * h : 32 * h + 32]
    wide = wide_ref[...]
    for c in range(2):
        out_ref[c] = dot(wide, weight_ref[c], NN).astype(BF16).reshape(8, 32, 256)


def finish_kernel(sums_ref, base_ref, out_ref):
    total = base_ref[...]
    for s in range(16):
        total = total + sums_ref[s].astype(F32)
    out_ref[...] = total.astype(BF16)


def body(
    queries,
    new_keys,
    new_values,
    home_keys,
    home_values,
    home_len,
    lent_keys,
    lent_values,
    lent_req,
    lent_len,
    out_weight,
    residual,
):
    here = lax.axis_index(INST)
    packed = pl.pallas_call(
        pack_kernel,
        out_shape=jax.ShapeDtypeStruct((64, 64, 128), BF16),
        in_specs=[ANY] * 4,
        out_specs=ANY,
        scratch_shapes=[
            pltpu.SMEM((4032,), jnp.int32),
            pltpu.SMEM((63,), jnp.int32),
            pltpu.VMEM((63, 32, 128), BF16),
            pltpu.VMEM((63, 32, 128), BF16),
            pltpu.VMEM((64, 32, 128), BF16),
            pltpu.VMEM((64, 32, 128), BF16),
            pltpu.SemaphoreType.DMA((6,)),
        ],
        name="pack_lent",
    )(
        lent_req,
        lent_len,
        lent_keys.reshape(63, 32, 128),
        lent_values.reshape(63, 32, 128),
    )
    recv = lax.all_to_all(
        packed, INST, split_axis=0, concat_axis=0, tiled=True, axis_index_groups=ORDER
    )
    asked, req, sent = pl.pallas_call(
        ask_kernel,
        out_shape=(
            jax.ShapeDtypeStruct((8, 128, 128), BF16),
            jax.ShapeDtypeStruct((8, 128), F32),
            jax.ShapeDtypeStruct((1024, 256), BF16),
        ),
        in_specs=[SMEM, VMEM, VMEM, VMEM, ANY],
        out_specs=(VMEM,) * 3,
        compiler_params=PARAMS,
        name="ask_queries",
    )(
        here.reshape(1),
        jnp.pad(lent_req, (0, 64), constant_values=-4).reshape(32, 128),
        queries,
        out_weight,
        packed,
    )
    received = lax.ppermute(sent, "zp", [(0, 1), (1, 0)])
    home_out, home_stat, base = pl.pallas_call(
        home_kernel,
        out_shape=(
            jax.ShapeDtypeStruct((64, 128), F32),
            jax.ShapeDtypeStruct((2, 128), F32),
            jax.ShapeDtypeStruct((32, 256), F32),
        ),
        in_specs=[SMEM] + [VMEM] * 6,
        out_specs=(VMEM,) * 3,
        compiler_params=PARAMS,
        name="home_part",
    )(
        home_len,
        queries,
        new_keys.reshape(4, 128),
        new_values.reshape(4, 128),
        home_keys.reshape(4, 256, 128),
        home_values.reshape(4, 256, 128),
        residual,
    )
    copies = pl.pallas_call(
        attend_kernel,
        out_shape=jax.ShapeDtypeStruct((64, 32, 128), BF16),
        in_specs=[VMEM] * 5,
        out_specs=VMEM,
        scratch_shapes=[pltpu.VMEM((1024, 128), F32)],
        compiler_params=PARAMS,
        name="attend",
    )(asked, req, home_stat, home_out, recv)
    rows = lax.all_to_all(
        copies, INST, split_axis=0, concat_axis=0, tiled=True, axis_index_groups=ORDER
    )
    weights = pl.pallas_call(
        join_kernel,
        out_shape=jax.ShapeDtypeStruct((2, 1024, 256), BF16),
        in_specs=[VMEM, VMEM],
        out_specs=VMEM,
        compiler_params=PARAMS,
        cost_estimate=pl.CostEstimate(flops=10**11, bytes_accessed=2**21, transcendentals=0),
        name="join_weights",
    )(out_weight, received)
    partial = pl.pallas_call(
        project_kernel,
        out_shape=jax.ShapeDtypeStruct((2, 8, 32, 256), BF16),
        in_specs=[VMEM, VMEM],
        out_specs=VMEM,
        scratch_shapes=[pltpu.VMEM((256, 1024), BF16)],
        compiler_params=PARAMS,
        name="project",
    )(rows, weights)
    sums = lax.all_to_all(
        partial.reshape(16, 32, 256), ("zp", "tp"), split_axis=0, concat_axis=0, tiled=True
    )
    return pl.pallas_call(
        finish_kernel,
        out_shape=jax.ShapeDtypeStruct((32, 256), BF16),
        in_specs=[VMEM, VMEM],
        out_specs=VMEM,
        compiler_params=PARAMS,
        name="finish",
    )(sums, base)


def solution(mesh):
    placed = (
        P(INST, "tp", None),
        P(INST, "tp", None),
        P(INST, "tp", None),
        P(INST, None, "tp", None),
        P(INST, None, "tp", None),
        P(INST),
        P(INST, None, "tp", None),
        P(INST, None, "tp", None),
        P(),
        P(INST),
        P("tp", INST),
        P("tp", INST),
    )
    fine = Mesh(mesh.devices.reshape(8, 4, 2, 8), INST + ("tp",))
    return jax.shard_map(
        body, mesh=fine, in_specs=placed, out_specs=P("tp", INST), check_vma=False
    )
```

```python
import math

import jax
import jax.numpy as jnp
from jax import lax
from jax.experimental import pallas as pl
from jax.experimental.pallas import tpu as pltpu
from jax.sharding import Mesh, PartitionSpec as P

VERY_LOW = -1e30
ABSENT = 64.0
SCALE = 1.0 / math.sqrt(128.0)
F32 = jnp.float32
BF16 = jnp.bfloat16
NT = (((1,), (1,)), ((), ()))
TN = (((0,), (0,)), ((), ()))
NN = (((1,), (0,)), ((), ()))
INST = ("y", "zh", "zp")
FIRST = 52
ORDER = [[(FIRST + k) % 64 for k in range(64)]]
PARAMS = pltpu.CompilerParams(vmem_limit_bytes=16 * 2**20)
SMEM = pl.BlockSpec(memory_space=pltpu.SMEM)
ANY = pl.BlockSpec(memory_space=pl.ANY)
VMEM = pl.BlockSpec(memory_space=pltpu.VMEM)


def dot(a, b, dims):
    return lax.dot_general(a, b, dims, preferred_element_type=F32)


def iota(shape, axis):
    return lax.broadcasted_iota(jnp.int32, shape, axis)


def halves(x):
    high = x.astype(BF16)
    return high, (x - high.astype(F32)).astype(BF16)


def ask_kernel(
    here_ref, table_ref, q_ref, weight_ref, packed_ref, asked_ref, req_ref, sent_ref
):
    first = pl.multiple_of((1 - lax.axis_index("zp")) * 1024, 1024)
    sent_ref[...] = weight_ref[pl.ds(first, 1024)]
    here = here_ref[0]
    table = table_ref[...]
    found = jnp.where((table >> 2) == here, (table & 3) + 1, 0).astype(F32)
    lane = iota((1, 128), 1)
    rows = []
    for j in ORDER[0]:
        line, first = divmod(63 * j, 128)
        row = jnp.where(lane >= first, found[line : line + 1], 0.0)
        if first + 63 <= 128:
            row = jnp.where(lane < first + 63, row, 0.0)
        else:
            row = jnp.where(lane < first + 63 - 128, found[line + 1 : line + 2], row)
        rows.append(row)
    source = jnp.sum(jnp.concatenate(rows, axis=0), axis=1, keepdims=True) - 1.0
    source = jnp.broadcast_to(source, (64, 128))
    query = [q_ref[r].astype(F32) for r in range(4)]
    for g in range(8):
        rows = []
        for j in range(8 * g, 8 * g + 8):
            s = jnp.broadcast_to(source[j : j + 1], (16, 128))
            picked = jnp.where(s == 1.0, query[1], query[0])
            picked = jnp.where(s == 2.0, query[2], picked)
            rows.append(jnp.where(s == 3.0, query[3], picked))
        asked_ref[g] = jnp.concatenate(rows, axis=0).T.astype(BF16)
    group = iota((8, 128), 1) >> 4
    split = source.reshape(8, 8, 128)
    req = jnp.zeros((8, 128), F32)
    for n in range(8):
        req = jnp.where(group == n, split[:, n], req)
    req_ref[...] = req


def pack_kernel(
    req_ref, len_ref, k_ref, v_ref, out_ref,
    req_in, len_in, k_in, v_in, keys_ref, values_ref, sems
):
    loads = [
        pltpu.make_async_copy(source, target, sems.at[i])
        for i, (source, target) in enumerate(
            [(req_ref, req_in), (len_ref, len_in), (k_ref, k_in), (v_ref, v_in)]
        )
    ]
    for load in loads:
        load.start()
    here = lax.axis_index(INST)
    place = (here - FIRST) & 63
    token = iota((32, 128), 0)
    keys_ref[place] = jnp.full((32, 128), ABSENT, F32).astype(BF16)
    values_ref[place] = jnp.zeros((32, 128), F32).astype(BF16)
    for load in loads[:3]:
        load.wait()
    for s in range(63):
        length = len_in[s]
        absent = ABSENT + length.astype(F32)
        keys = jnp.where(token < length, k_in[s].astype(F32), absent)
        keys_ref[((req_in[63 * here + s] >> 2) - FIRST) & 63] = keys.astype(BF16)
    send_keys = pltpu.make_async_copy(keys_ref, out_ref.at[:, pl.ds(0, 32)], sems.at[4])
    send_keys.start()
    loads[3].wait()
    for s in range(63):
        values_ref[((req_in[63 * here + s] >> 2) - FIRST) & 63] = v_in[s]
    send_values = pltpu.make_async_copy(values_ref, out_ref.at[:, pl.ds(32, 32)], sems.at[5])
    send_values.start()
    send_keys.wait()
    send_values.wait()


def home_kernel(
    len_ref, q_ref, nk_ref, nv_ref, k_ref, v_ref, residual_ref, out_ref, stat_ref, base_ref
):
    query = q_ref[...].reshape(64, 128)
    query = jnp.concatenate([query, query], axis=0)
    owner = (iota((256, 128), 1) >> 4) & 3
    token = iota((256, 128), 0)
    scores = jnp.zeros((256, 128), F32)
    length = jnp.zeros((256, 128), jnp.int32)
    for r in range(4):
        scores = jnp.where(owner == r, dot(k_ref[r], query, NT), scores)
        length = jnp.where(owner == r, len_ref[r], length)
    scores = jnp.where(token < length, scores * SCALE, VERY_LOW)
    mine = ((iota((4, 128), 1) >> 4) & 3) == iota((4, 128), 0)
    fresh = dot(nk_ref[...], query, NT) * SCALE
    fresh = jnp.sum(jnp.where(mine, fresh, 0.0), axis=0, keepdims=True)
    top = jnp.maximum(jnp.max(scores, axis=0, keepdims=True), fresh)
    weights = jnp.exp(scores - top)
    own = jnp.exp(fresh - top)
    total = jnp.sum(weights, axis=0, keepdims=True) + own
    mixed = dot(jnp.where(mine, own, 0.0).astype(BF16), nv_ref[...], TN)
    for r in range(4):
        mixed += dot(jnp.where(owner == r, weights, 0.0).astype(BF16), v_ref[r], TN)
    out_ref[...] = mixed[:64]
    stat_ref[...] = jnp.concatenate([top, total], axis=0)
    base_ref[...] = residual_ref[...].astype(F32)


def attend_kernel(q_ref, req_ref, stat_ref, home_ref, recv_ref, out_ref, mixed_ref):
    owner = iota((32, 128), 1) >> 4
    token = iota((32, 128), 0).astype(F32)
    holder = (iota((8, 128), 1) >> 4) == iota((8, 128), 0)
    repeat = ((iota((32, 256), 1) & 31) == iota((32, 256), 0)).astype(F32).astype(BF16)
    block = (iota((128, 256), 0) >> 4) == (iota((128, 256), 1) >> 5)
    block = block.astype(F32).astype(BF16)
    far_tops, far_totals = [], []
    for g in range(8):
        group = pl.ds(8 * g, 8)
        keys = recv_ref[group, :32, :].reshape(256, 128)
        raw = dot(keys, q_ref[g], NN)
        last = recv_ref[group, 31, :].astype(F32)
        length = jnp.where(last < 0.5 * ABSENT, 32.0, last - ABSENT)
        length = jnp.sum(jnp.where(holder, length, 0.0), axis=0, keepdims=True)
        scores = raw[:32]
        for j in range(1, 8):
            scores = jnp.where(owner == j, raw[32 * j : 32 * j + 32], scores)
        scores = jnp.where(token < length, scores * SCALE, VERY_LOW)
        top = jnp.max(scores, axis=0, keepdims=True)
        weights = jnp.exp(scores - top)
        far_tops.append(top)
        far_totals.append(jnp.sum(weights, axis=0, keepdims=True))
        blocks = dot(weights.astype(BF16), repeat, TN).astype(BF16) * block
        values = recv_ref[group, 32:, :].reshape(256, 128)
        mixed_ref[128 * g : 128 * g + 128] = dot(blocks, values, NN)
    far_top = jnp.concatenate(far_tops, axis=0)
    far_total = jnp.concatenate(far_totals, axis=0)
    near_top, near_total = stat_ref[0:1], stat_ref[1:2]
    which = iota((1, 128), 1) >> 4
    req = req_ref[...]
    tops = []
    for r in range(4):
        t = jnp.max(jnp.where(req == r, far_top, VERY_LOW), axis=0, keepdims=True)
        tops.append(jnp.maximum(t, jnp.where(which == r, near_top, VERY_LOW)))
    peak = jnp.concatenate(tops, axis=0)
    for shift in (16, 32, 64):
        peak = jnp.maximum(peak, pltpu.roll(peak, shift, 1))
    far_w, near_w, totals = [], [], []
    for r in range(4):
        p = peak[r : r + 1]
        f = jnp.where(req == r, jnp.exp(far_top - p), 0.0)
        n = jnp.where(which == r, jnp.exp(near_top - p), 0.0)
        far_w.append(f)
        near_w.append(n)
        totals.append(jnp.sum(f * far_total, axis=0, keepdims=True) + n * near_total)
    total = jnp.concatenate(totals, axis=0)
    for shift in (16, 32, 64):
        total = total + pltpu.roll(total, shift, 1)
    scale = 1.0 / total
    same = (iota((16, 128), 1) & 15) == iota((16, 128), 0)

    def spread_rows(rows):
        return halves(jnp.concatenate([jnp.where(same, row, 0.0) for row in rows], axis=0))

    high, low = spread_rows([near_w[r] * scale[r : r + 1] for r in range(4)])
    home_high, home_low = halves(home_ref[...])
    acc = dot(high[:, :64], home_high, NN) + dot(high[:, :64], home_low, NN)
    acc += dot(low[:, :64], home_high, NN)
    far_w = [far_w[r] * scale[r : r + 1] for r in range(4)]
    for g in range(8):
        high, low = spread_rows([far_w[r][g : g + 1] for r in range(4)])
        mixed_high, mixed_low = halves(mixed_ref[128 * g : 128 * g + 128])
        acc += dot(high, mixed_high, NN) + dot(high, mixed_low, NN) + dot(low, mixed_high, NN)
    lower = jnp.concatenate([acc[16 * r : 16 * r + 8] for r in range(4)], axis=0)
    upper = jnp.concatenate([acc[16 * r + 8 : 16 * r + 16] for r in range(4)], axis=0)
    split = jnp.concatenate([lower, upper], axis=0).astype(BF16).reshape(1, 2, 32, 128)
    out_ref[...] = jnp.broadcast_to(split, (32, 2, 32, 128)).reshape(64, 32, 128)


def join_kernel(mine_ref, received_ref, out_ref):
    zp = lax.axis_index("zp")
    out_ref[zp] = mine_ref[pl.ds(pl.multiple_of(zp * 1024, 1024), 1024)]
    out_ref[1 - zp] = received_ref[...]


def project_kernel(rows_ref, weight_ref, out_ref, wide_ref):
    q = iota((256, 256), 0)
    p = iota((256, 256), 1)
    move = p == 32 * ((q >> 2) & 7) + 8 * (q & 3) + (q >> 5)
    move = move.astype(F32).astype(BF16)
    for b in range(8):
        parts = [rows_ref[(8 * b + i - FIRST) % 64] for i in range(8)]
        moved = dot(move, jnp.concatenate(parts, axis=0), NN).astype(BF16)
        for h in range(8):
            wide_ref[32 * b : 32 * b + 32, 128 * h : 128 * h + 128] = moved[32 * h : 32 * h + 32]
    wide = wide_ref[...]
    for c in range(2):
        out_ref[c] = dot(wide, weight_ref[c], NN).astype(BF16).reshape(8, 32, 256)


def finish_kernel(sums_ref, base_ref, out_ref):
    total = base_ref[...]
    for s in range(16):
        total = total + sums_ref[s].astype(F32)
    out_ref[...] = total.astype(BF16)


def body(
    queries,
    new_keys,
    new_values,
    home_keys,
    home_values,
    home_len,
    lent_keys,
    lent_values,
    lent_req,
    lent_len,
    out_weight,
    residual,
):
    here = lax.axis_index(INST)
    packed = pl.pallas_call(
        pack_kernel,
        out_shape=jax.ShapeDtypeStruct((64, 64, 128), BF16),
        in_specs=[ANY] * 4,
        out_specs=ANY,
        scratch_shapes=[
            pltpu.SMEM((4032,), jnp.int32),
            pltpu.SMEM((63,), jnp.int32),
            pltpu.VMEM((63, 32, 128), BF16),
            pltpu.VMEM((63, 32, 128), BF16),
            pltpu.VMEM((64, 32, 128), BF16),
            pltpu.VMEM((64, 32, 128), BF16),
            pltpu.SemaphoreType.DMA((6,)),
        ],
        name="pack_lent",
    )(
        lent_req,
        lent_len,
        lent_keys.reshape(63, 32, 128),
        lent_values.reshape(63, 32, 128),
    )
    recv = lax.all_to_all(
        packed, INST, split_axis=0, concat_axis=0, tiled=True, axis_index_groups=ORDER
    )
    asked, req, sent = pl.pallas_call(
        ask_kernel,
        out_shape=(
            jax.ShapeDtypeStruct((8, 128, 128), BF16),
            jax.ShapeDtypeStruct((8, 128), F32),
            jax.ShapeDtypeStruct((1024, 256), BF16),
        ),
        in_specs=[SMEM, VMEM, VMEM, VMEM, ANY],
        out_specs=(VMEM,) * 3,
        compiler_params=PARAMS,
        name="ask_queries",
    )(
        here.reshape(1),
        jnp.pad(lent_req, (0, 64), constant_values=-4).reshape(32, 128),
        queries,
        out_weight,
        packed,
    )
    received = lax.ppermute(sent, "zp", [(0, 1), (1, 0)])
    home_out, home_stat, base = pl.pallas_call(
        home_kernel,
        out_shape=(
            jax.ShapeDtypeStruct((64, 128), F32),
            jax.ShapeDtypeStruct((2, 128), F32),
            jax.ShapeDtypeStruct((32, 256), F32),
        ),
        in_specs=[SMEM] + [VMEM] * 6,
        out_specs=(VMEM,) * 3,
        compiler_params=PARAMS,
        name="home_part",
    )(
        home_len,
        queries,
        new_keys.reshape(4, 128),
        new_values.reshape(4, 128),
        home_keys.reshape(4, 256, 128),
        home_values.reshape(4, 256, 128),
        residual,
    )
    copies = pl.pallas_call(
        attend_kernel,
        out_shape=jax.ShapeDtypeStruct((64, 32, 128), BF16),
        in_specs=[VMEM] * 5,
        out_specs=VMEM,
        scratch_shapes=[pltpu.VMEM((1024, 128), F32)],
        compiler_params=PARAMS,
        name="attend",
    )(asked, req, home_stat, home_out, recv)
    rows = lax.all_to_all(
        copies, INST, split_axis=0, concat_axis=0, tiled=True, axis_index_groups=ORDER
    )
    weights = pl.pallas_call(
        join_kernel,
        out_shape=jax.ShapeDtypeStruct((2, 1024, 256), BF16),
        in_specs=[VMEM, VMEM],
        out_specs=VMEM,
        compiler_params=PARAMS,
        cost_estimate=pl.CostEstimate(flops=10**11, bytes_accessed=2**21, transcendentals=0),
        name="join_weights",
    )(out_weight, received)
    partial = pl.pallas_call(
        project_kernel,
        out_shape=jax.ShapeDtypeStruct((2, 8, 32, 256), BF16),
        in_specs=[VMEM, VMEM],
        out_specs=VMEM,
        scratch_shapes=[pltpu.VMEM((256, 1024), BF16)],
        compiler_params=PARAMS,
        name="project",
    )(rows, weights)
    sums = lax.all_to_all(
        partial.reshape(16, 32, 256), ("zp", "tp"), split_axis=0, concat_axis=0, tiled=True
    )
    return pl.pallas_call(
        finish_kernel,
        out_shape=jax.ShapeDtypeStruct((32, 256), BF16),
        in_specs=[VMEM, VMEM],
        out_specs=VMEM,
        compiler_params=PARAMS,
        name="finish",
    )(sums, base)


def solution(mesh):
    placed = (
        P(INST, "tp", None),
        P(INST, "tp", None),
        P(INST, "tp", None),
        P(INST, None, "tp", None),
        P(INST, None, "tp", None),
        P(INST),
        P(INST, None, "tp", None),
        P(INST, None, "tp", None),
        P(),
        P(INST),
        P("tp", INST),
        P("tp", INST),
    )
    fine = Mesh(mesh.devices.reshape(8, 4, 2, 8), INST + ("tp",))
    return jax.shard_map(
        body, mesh=fine, in_specs=placed, out_specs=P("tp", INST), check_vma=False
    )
```

```python
import math

import jax
import jax.numpy as jnp
from jax import lax
from jax.experimental import pallas as pl
from jax.experimental.pallas import tpu as pltpu
from jax.sharding import Mesh, PartitionSpec as P

VERY_LOW = -1e30
ABSENT = 64.0
SCALE = 1.0 / math.sqrt(128.0)
F32 = jnp.float32
BF16 = jnp.bfloat16
NT = (((1,), (1,)), ((), ()))
TN = (((0,), (0,)), ((), ()))
NN = (((1,), (0,)), ((), ()))
INST = ("y", "zh", "zp")
FIRST = 52
ORDER = [[(FIRST + k) % 64 for k in range(64)]]
PARAMS = pltpu.CompilerParams(vmem_limit_bytes=16 * 2**20)
SMEM = pl.BlockSpec(memory_space=pltpu.SMEM)
ANY = pl.BlockSpec(memory_space=pl.ANY)
VMEM = pl.BlockSpec(memory_space=pltpu.VMEM)


def dot(a, b, dims):
    return lax.dot_general(a, b, dims, preferred_element_type=F32)


def iota(shape, axis):
    return lax.broadcasted_iota(jnp.int32, shape, axis)


def halves(x):
    high = x.astype(BF16)
    return high, (x - high.astype(F32)).astype(BF16)


def ask_kernel(
    here_ref, table_ref, q_ref, weight_ref, packed_ref, asked_ref, req_ref, sent_ref
):
    first = pl.multiple_of((1 - lax.axis_index("zp")) * 1024, 1024)
    sent_ref[...] = weight_ref[pl.ds(first, 1024)]
    here = here_ref[0]
    table = table_ref[...]
    found = jnp.where((table >> 2) == here, (table & 3) + 1, 0).astype(F32)
    lane = iota((1, 128), 1)
    rows = []
    for j in ORDER[0]:
        line, first = divmod(63 * j, 128)
        row = jnp.where(lane >= first, found[line : line + 1], 0.0)
        if first + 63 <= 128:
            row = jnp.where(lane < first + 63, row, 0.0)
        else:
            row = jnp.where(lane < first + 63 - 128, found[line + 1 : line + 2], row)
        rows.append(row)
    source = jnp.sum(jnp.concatenate(rows, axis=0), axis=1, keepdims=True) - 1.0
    source = jnp.broadcast_to(source, (64, 128))
    query = [q_ref[r].astype(F32) for r in range(4)]
    for g in range(8):
        rows = []
        for j in range(8 * g, 8 * g + 8):
            s = jnp.broadcast_to(source[j : j + 1], (16, 128))
            picked = jnp.where(s == 1.0, query[1], query[0])
            picked = jnp.where(s == 2.0, query[2], picked)
            rows.append(jnp.where(s == 3.0, query[3], picked))
        asked_ref[g] = jnp.concatenate(rows, axis=0).astype(BF16)
    group = iota((8, 128), 1) >> 4
    split = source.reshape(8, 8, 128)
    req = jnp.zeros((8, 128), F32)
    for n in range(8):
        req = jnp.where(group == n, split[:, n], req)
    req_ref[...] = req


def pack_kernel(
    req_ref, len_ref, k_ref, v_ref, out_ref,
    req_in, len_in, k_in, v_in, keys_ref, values_ref, sems
):
    loads = [
        pltpu.make_async_copy(source, target, sems.at[i])
        for i, (source, target) in enumerate(
            [(req_ref, req_in), (len_ref, len_in), (k_ref, k_in), (v_ref, v_in)]
        )
    ]
    for load in loads:
        load.start()
    here = lax.axis_index(INST)
    place = (here - FIRST) & 63
    token = iota((32, 128), 0)
    keys_ref[place] = jnp.full((32, 128), ABSENT, F32).astype(BF16)
    values_ref[place] = jnp.zeros((32, 128), F32).astype(BF16)
    for load in loads[:3]:
        load.wait()
    for s in range(63):
        length = len_in[s]
        absent = ABSENT + length.astype(F32)
        keys = jnp.where(token < length, k_in[s].astype(F32), absent)
        keys_ref[((req_in[63 * here + s] >> 2) - FIRST) & 63] = keys.astype(BF16)
    send_keys = pltpu.make_async_copy(keys_ref, out_ref.at[:, pl.ds(0, 32)], sems.at[4])
    send_keys.start()
    loads[3].wait()
    for s in range(63):
        values_ref[((req_in[63 * here + s] >> 2) - FIRST) & 63] = v_in[s]
    send_values = pltpu.make_async_copy(values_ref, out_ref.at[:, pl.ds(32, 32)], sems.at[5])
    send_values.start()
    send_keys.wait()
    send_values.wait()


def home_kernel(
    len_ref, q_ref, nk_ref, nv_ref, k_ref, v_ref, residual_ref, out_ref, stat_ref, base_ref
):
    query = q_ref[...].reshape(64, 128)
    query = jnp.concatenate([query, query], axis=0)
    owner = (iota((256, 128), 1) >> 4) & 3
    token = iota((256, 128), 0)
    scores = jnp.zeros((256, 128), F32)
    length = jnp.zeros((256, 128), jnp.int32)
    for r in range(4):
        scores = jnp.where(owner == r, dot(k_ref[r], query, NT), scores)
        length = jnp.where(owner == r, len_ref[r], length)
    scores = jnp.where(token < length, scores * SCALE, VERY_LOW)
    mine = ((iota((4, 128), 1) >> 4) & 3) == iota((4, 128), 0)
    fresh = dot(nk_ref[...], query, NT) * SCALE
    fresh = jnp.sum(jnp.where(mine, fresh, 0.0), axis=0, keepdims=True)
    top = jnp.maximum(jnp.max(scores, axis=0, keepdims=True), fresh)
    weights = jnp.exp(scores - top)
    own = jnp.exp(fresh - top)
    total = jnp.sum(weights, axis=0, keepdims=True) + own
    mixed = dot(jnp.where(mine, own, 0.0).astype(BF16), nv_ref[...], TN)
    for r in range(4):
        mixed += dot(jnp.where(owner == r, weights, 0.0).astype(BF16), v_ref[r], TN)
    out_ref[...] = mixed[:64]
    stat_ref[...] = jnp.concatenate([top, total], axis=0)
    base_ref[...] = residual_ref[...].astype(F32)


def attend_kernel(q_ref, req_ref, stat_ref, home_ref, recv_ref, out_ref, mixed_ref):
    lane = iota((64, 128), 1)
    block = (iota((64, 128), 0) >> 4) == (lane >> 5)
    token = (lane & 31).astype(F32)
    lane = iota((128, 128), 1)
    columns = jnp.zeros((128, 128), F32)
    for g in range(8):
        tops, totals = [], []
        for first in (8 * g, 8 * g + 4):
            group = pl.ds(first, 4)
            keys = recv_ref[group, :32, :].reshape(128, 128)
            query = q_ref[g, 16 * (first - 8 * g) : 16 * (first - 8 * g) + 64]
            raw = dot(query, keys, NT)
            last = recv_ref[group, 31, :].astype(F32)
            length = jnp.where(last < 0.5 * ABSENT, 32.0, last - ABSENT)
            length = jnp.concatenate(
                [jnp.broadcast_to(length[j : j + 1], (16, 128)) for j in range(4)], axis=0
            )
            scores = jnp.where(block & (token < length), raw * SCALE, VERY_LOW)
            top = jnp.max(scores, axis=1, keepdims=True)
            weights = jnp.exp(scores - top)
            tops.append(top)
            totals.append(jnp.sum(weights, axis=1, keepdims=True))
            values = recv_ref[group, 32:, :].reshape(128, 128)
            high, low = halves(dot(weights.astype(BF16), values, NN))
            mixed_ref[16 * first : 16 * first + 64] = high
            mixed_ref[1024 + 16 * first : 1024 + 16 * first + 64] = low
        top, total = jnp.concatenate(tops, axis=0), jnp.concatenate(totals, axis=0)
        columns = jnp.where(lane == g, top, jnp.where(lane == 8 + g, total, columns))
    stats = columns.T
    far_top, far_total = stats[:8], stats[8:16]
    near_top, near_total = stat_ref[0:1], stat_ref[1:2]
    which = iota((1, 128), 1) >> 4
    req = req_ref[...]
    tops = []
    for r in range(4):
        t = jnp.max(jnp.where(req == r, far_top, VERY_LOW), axis=0, keepdims=True)
        tops.append(jnp.maximum(t, jnp.where(which == r, near_top, VERY_LOW)))
    peak = jnp.concatenate(tops, axis=0)
    for shift in (16, 32, 64):
        peak = jnp.maximum(peak, pltpu.roll(peak, shift, 1))
    far_w, near_w, totals = [], [], []
    for r in range(4):
        p = peak[r : r + 1]
        f = jnp.where(req == r, jnp.exp(far_top - p), 0.0)
        n = jnp.where(which == r, jnp.exp(near_top - p), 0.0)
        far_w.append(f)
        near_w.append(n)
        totals.append(jnp.sum(f * far_total, axis=0, keepdims=True) + n * near_total)
    total = jnp.concatenate(totals, axis=0)
    for shift in (16, 32, 64):
        total = total + pltpu.roll(total, shift, 1)
    scale = 1.0 / total
    same = (iota((16, 128), 1) & 15) == iota((16, 128), 0)

    def spread_rows(rows):
        return halves(jnp.concatenate([jnp.where(same, row, 0.0) for row in rows], axis=0))

    high, low = spread_rows([near_w[r] * scale[r : r + 1] for r in range(4)])
    home_high, home_low = halves(home_ref[...])
    acc = dot(high[:, :64], home_high, NN) + dot(high[:, :64], home_low, NN)
    acc += dot(low[:, :64], home_high, NN)
    far_w = [far_w[r] * scale[r : r + 1] for r in range(4)]
    spread = [spread_rows([far_w[r][g : g + 1] for r in range(4)]) for g in range(8)]
    high = jnp.concatenate([h for h, _ in spread], axis=1)
    low = jnp.concatenate([l for _, l in spread], axis=1)
    mixed_high, mixed_low = mixed_ref[:1024], mixed_ref[1024:]
    acc += dot(high, mixed_high, NN) + dot(high, mixed_low, NN) + dot(low, mixed_high, NN)
    lower = jnp.concatenate([acc[16 * r : 16 * r + 8] for r in range(4)], axis=0)
    upper = jnp.concatenate([acc[16 * r + 8 : 16 * r + 16] for r in range(4)], axis=0)
    split = jnp.concatenate([lower, upper], axis=0).astype(BF16).reshape(1, 2, 32, 128)
    out_ref[...] = jnp.broadcast_to(split, (32, 2, 32, 128)).reshape(64, 32, 128)


def join_kernel(mine_ref, received_ref, out_ref):
    zp = lax.axis_index("zp")
    out_ref[zp] = mine_ref[pl.ds(pl.multiple_of(zp * 1024, 1024), 1024)]
    out_ref[1 - zp] = received_ref[...]


def project_kernel(rows_ref, weight_ref, out_ref, wide_ref):
    q = iota((256, 256), 0)
    p = iota((256, 256), 1)
    move = p == 32 * ((q >> 2) & 7) + 8 * (q & 3) + (q >> 5)
    move = move.astype(F32).astype(BF16)
    for b in range(8):
        parts = [rows_ref[(8 * b + i - FIRST) % 64] for i in range(8)]
        moved = dot(move, jnp.concatenate(parts, axis=0), NN).astype(BF16)
        for h in range(8):
            wide_ref[32 * b : 32 * b + 32, 128 * h : 128 * h + 128] = moved[32 * h : 32 * h + 32]
    wide = wide_ref[...]
    for c in range(2):
        out_ref[c] = dot(wide, weight_ref[c], NN).astype(BF16).reshape(8, 32, 256)


def finish_kernel(sums_ref, base_ref, out_ref):
    total = base_ref[...]
    for s in range(16):
        total = total + sums_ref[s].astype(F32)
    out_ref[...] = total.astype(BF16)


def body(
    queries,
    new_keys,
    new_values,
    home_keys,
    home_values,
    home_len,
    lent_keys,
    lent_values,
    lent_req,
    lent_len,
    out_weight,
    residual,
):
    here = lax.axis_index(INST)
    packed = pl.pallas_call(
        pack_kernel,
        out_shape=jax.ShapeDtypeStruct((64, 64, 128), BF16),
        in_specs=[ANY] * 4,
        out_specs=ANY,
        scratch_shapes=[
            pltpu.SMEM((4032,), jnp.int32),
            pltpu.SMEM((63,), jnp.int32),
            pltpu.VMEM((63, 32, 128), BF16),
            pltpu.VMEM((63, 32, 128), BF16),
            pltpu.VMEM((64, 32, 128), BF16),
            pltpu.VMEM((64, 32, 128), BF16),
            pltpu.SemaphoreType.DMA((6,)),
        ],
        name="pack_lent",
    )(
        lent_req,
        lent_len,
        lent_keys.reshape(63, 32, 128),
        lent_values.reshape(63, 32, 128),
    )
    recv = lax.all_to_all(
        packed, INST, split_axis=0, concat_axis=0, tiled=True, axis_index_groups=ORDER
    )
    asked, req, sent = pl.pallas_call(
        ask_kernel,
        out_shape=(
            jax.ShapeDtypeStruct((8, 128, 128), BF16),
            jax.ShapeDtypeStruct((8, 128), F32),
            jax.ShapeDtypeStruct((1024, 256), BF16),
        ),
        in_specs=[SMEM, VMEM, VMEM, VMEM, ANY],
        out_specs=(VMEM,) * 3,
        compiler_params=PARAMS,
        name="ask_queries",
    )(
        here.reshape(1),
        jnp.pad(lent_req, (0, 64), constant_values=-4).reshape(32, 128),
        queries,
        out_weight,
        packed,
    )
    received = lax.ppermute(sent, "zp", [(0, 1), (1, 0)])
    home_out, home_stat, base = pl.pallas_call(
        home_kernel,
        out_shape=(
            jax.ShapeDtypeStruct((64, 128), F32),
            jax.ShapeDtypeStruct((2, 128), F32),
            jax.ShapeDtypeStruct((32, 256), F32),
        ),
        in_specs=[SMEM] + [VMEM] * 6,
        out_specs=(VMEM,) * 3,
        compiler_params=PARAMS,
        name="home_part",
    )(
        home_len,
        queries,
        new_keys.reshape(4, 128),
        new_values.reshape(4, 128),
        home_keys.reshape(4, 256, 128),
        home_values.reshape(4, 256, 128),
        residual,
    )
    copies = pl.pallas_call(
        attend_kernel,
        out_shape=jax.ShapeDtypeStruct((64, 32, 128), BF16),
        in_specs=[VMEM] * 5,
        out_specs=VMEM,
        scratch_shapes=[pltpu.VMEM((2048, 128), BF16)],
        compiler_params=PARAMS,
        name="attend",
    )(asked, req, home_stat, home_out, recv)
    rows = lax.all_to_all(
        copies, INST, split_axis=0, concat_axis=0, tiled=True, axis_index_groups=ORDER
    )
    weights = pl.pallas_call(
        join_kernel,
        out_shape=jax.ShapeDtypeStruct((2, 1024, 256), BF16),
        in_specs=[VMEM, VMEM],
        out_specs=VMEM,
        compiler_params=PARAMS,
        cost_estimate=pl.CostEstimate(flops=10**11, bytes_accessed=2**21, transcendentals=0),
        name="join_weights",
    )(out_weight, received)
    partial = pl.pallas_call(
        project_kernel,
        out_shape=jax.ShapeDtypeStruct((2, 8, 32, 256), BF16),
        in_specs=[VMEM, VMEM],
        out_specs=VMEM,
        scratch_shapes=[pltpu.VMEM((256, 1024), BF16)],
        compiler_params=PARAMS,
        name="project",
    )(rows, weights)
    sums = lax.all_to_all(
        partial.reshape(16, 32, 256), ("zp", "tp"), split_axis=0, concat_axis=0, tiled=True
    )
    return pl.pallas_call(
        finish_kernel,
        out_shape=jax.ShapeDtypeStruct((32, 256), BF16),
        in_specs=[VMEM, VMEM],
        out_specs=VMEM,
        compiler_params=PARAMS,
        name="finish",
    )(sums, base)


def solution(mesh):
    placed = (
        P(INST, "tp", None),
        P(INST, "tp", None),
        P(INST, "tp", None),
        P(INST, None, "tp", None),
        P(INST, None, "tp", None),
        P(INST),
        P(INST, None, "tp", None),
        P(INST, None, "tp", None),
        P(),
        P(INST),
        P("tp", INST),
        P("tp", INST),
    )
    fine = Mesh(mesh.devices.reshape(8, 4, 2, 8), INST + ("tp",))
    return jax.shard_map(
        body, mesh=fine, in_specs=placed, out_specs=P("tp", INST), check_vma=False
    )
```

```python
import math

import jax
import jax.numpy as jnp
from jax import lax
from jax.experimental import pallas as pl
from jax.experimental.pallas import tpu as pltpu
from jax.sharding import Mesh, PartitionSpec as P

VERY_LOW = -1e30
ABSENT = 64.0
SCALE = 1.0 / math.sqrt(128.0)
F32 = jnp.float32
BF16 = jnp.bfloat16
NT = (((1,), (1,)), ((), ()))
TN = (((0,), (0,)), ((), ()))
NN = (((1,), (0,)), ((), ()))
INST = ("y", "zh", "zp")
FIRST = 52
ORDER = [[(FIRST + k) % 64 for k in range(64)]]
PARAMS = pltpu.CompilerParams(vmem_limit_bytes=16 * 2**20)
SMEM = pl.BlockSpec(memory_space=pltpu.SMEM)
ANY = pl.BlockSpec(memory_space=pl.ANY)
VMEM = pl.BlockSpec(memory_space=pltpu.VMEM)


def dot(a, b, dims):
    return lax.dot_general(a, b, dims, preferred_element_type=F32)


def iota(shape, axis):
    return lax.broadcasted_iota(jnp.int32, shape, axis)


def halves(x):
    high = x.astype(BF16)
    return high, (x - high.astype(F32)).astype(BF16)


def ask_kernel(
    here_ref, table_ref, q_ref, weight_ref, packed_ref, asked_ref, req_ref, sent_ref
):
    first = pl.multiple_of((1 - lax.axis_index("zp")) * 1024, 1024)
    sent_ref[...] = weight_ref[pl.ds(first, 1024)]
    here = here_ref[0]
    table = table_ref[...]
    found = jnp.where((table >> 2) == here, (table & 3) + 1, 0).astype(F32)
    lane = iota((1, 128), 1)
    rows = []
    for j in ORDER[0]:
        line, first = divmod(63 * j, 128)
        row = jnp.where(lane >= first, found[line : line + 1], 0.0)
        if first + 63 <= 128:
            row = jnp.where(lane < first + 63, row, 0.0)
        else:
            row = jnp.where(lane < first + 63 - 128, found[line + 1 : line + 2], row)
        rows.append(row)
    source = jnp.sum(jnp.concatenate(rows, axis=0), axis=1, keepdims=True) - 1.0
    source = jnp.broadcast_to(source, (64, 128))
    query = [q_ref[r].astype(F32) for r in range(4)]
    for g in range(8):
        rows = []
        for j in range(8 * g, 8 * g + 8):
            s = jnp.broadcast_to(source[j : j + 1], (16, 128))
            picked = jnp.where(s == 1.0, query[1], query[0])
            picked = jnp.where(s == 2.0, query[2], picked)
            rows.append(jnp.where(s == 3.0, query[3], picked))
        asked_ref[g] = jnp.concatenate(rows, axis=0).T.astype(BF16)
    group = iota((8, 128), 1) >> 4
    split = source.reshape(8, 8, 128)
    req = jnp.zeros((8, 128), F32)
    for n in range(8):
        req = jnp.where(group == n, split[:, n], req)
    req_ref[...] = req


def pack_kernel(
    req_ref, len_ref, k_ref, v_ref, out_ref,
    req_in, len_in, k_in, v_in, keys_ref, values_ref, sems
):
    loads = [
        pltpu.make_async_copy(source, target, sems.at[i])
        for i, (source, target) in enumerate(
            [(req_ref, req_in), (len_ref, len_in), (k_ref, k_in), (v_ref, v_in)]
        )
    ]
    for load in loads:
        load.start()
    here = lax.axis_index(INST)
    place = (here - FIRST) & 63
    token = iota((32, 128), 0)
    keys_ref[place] = jnp.full((32, 128), ABSENT, F32).astype(BF16)
    values_ref[place] = jnp.zeros((32, 128), F32).astype(BF16)
    for load in loads[:3]:
        load.wait()
    for s in range(63):
        length = len_in[s]
        absent = ABSENT + length.astype(F32)
        keys = jnp.where(token < length, k_in[s].astype(F32), absent)
        keys_ref[((req_in[63 * here + s] >> 2) - FIRST) & 63] = keys.astype(BF16)
    send_keys = pltpu.make_async_copy(keys_ref, out_ref.at[:, pl.ds(0, 32)], sems.at[4])
    send_keys.start()
    loads[3].wait()
    for s in range(63):
        values_ref[((req_in[63 * here + s] >> 2) - FIRST) & 63] = v_in[s]
    send_values = pltpu.make_async_copy(values_ref, out_ref.at[:, pl.ds(32, 32)], sems.at[5])
    send_values.start()
    send_keys.wait()
    send_values.wait()


def home_kernel(
    len_ref, q_ref, nk_ref, nv_ref, k_ref, v_ref, residual_ref, out_ref, stat_ref, base_ref
):
    query = q_ref[...].reshape(64, 128)
    query = jnp.concatenate([query, query], axis=0)
    owner = (iota((256, 128), 1) >> 4) & 3
    token = iota((256, 128), 0)
    scores = jnp.zeros((256, 128), F32)
    length = jnp.zeros((256, 128), jnp.int32)
    for r in range(4):
        scores = jnp.where(owner == r, dot(k_ref[r], query, NT), scores)
        length = jnp.where(owner == r, len_ref[r], length)
    scores = jnp.where(token < length, scores * SCALE, VERY_LOW)
    mine = ((iota((4, 128), 1) >> 4) & 3) == iota((4, 128), 0)
    fresh = dot(nk_ref[...], query, NT) * SCALE
    fresh = jnp.sum(jnp.where(mine, fresh, 0.0), axis=0, keepdims=True)
    top = jnp.maximum(jnp.max(scores, axis=0, keepdims=True), fresh)
    weights = jnp.exp(scores - top)
    own = jnp.exp(fresh - top)
    total = jnp.sum(weights, axis=0, keepdims=True) + own
    mixed = dot(jnp.where(mine, own, 0.0).astype(BF16), nv_ref[...], TN)
    for r in range(4):
        mixed += dot(jnp.where(owner == r, weights, 0.0).astype(BF16), v_ref[r], TN)
    out_ref[...] = mixed[:64]
    stat_ref[...] = jnp.concatenate([top, total], axis=0)
    base_ref[...] = residual_ref[...].astype(F32)


def attend_kernel(
    q_ref, req_ref, stat_ref, home_ref, recv_ref, out_ref, raw_ref, mixed_ref
):
    owner = iota((32, 128), 1) >> 4
    token = iota((8, 32, 128), 1).astype(F32)
    holder = (iota((8, 8, 128), 2) >> 4) == iota((8, 8, 128), 1)
    keep = [(owner == j).astype(F32).astype(BF16) for j in range(8)]
    for g in range(8):
        keys = recv_ref[8 * g : 8 * g + 8, :32, :].reshape(256, 128)
        raw_ref[256 * g : 256 * g + 256] = dot(keys, q_ref[g], NN)
    last = recv_ref[:, 31, :].astype(F32).reshape(8, 8, 128)
    length = jnp.where(last < 0.5 * ABSENT, 32.0, last - ABSENT)
    length = jnp.sum(jnp.where(holder, length, 0.0), axis=1, keepdims=True)
    scores = []
    for g in range(8):
        picked = raw_ref[256 * g : 256 * g + 32]
        for j in range(1, 8):
            first = 256 * g + 32 * j
            picked = jnp.where(owner == j, raw_ref[first : first + 32], picked)
        scores.append(picked)
    scores = jnp.concatenate(scores, axis=0).reshape(8, 32, 128)
    scores = jnp.where(token < length, scores * SCALE, VERY_LOW)
    far_top = jnp.max(scores, axis=1, keepdims=True)
    weights = jnp.exp(scores - far_top)
    far_total = jnp.sum(weights, axis=1, keepdims=True).reshape(8, 128)
    far_top = far_top.reshape(8, 128)
    weights = weights.astype(BF16)
    for g in range(8):
        blocks = jnp.concatenate([weights[g] * keep[j] for j in range(8)], axis=0)
        values = recv_ref[8 * g : 8 * g + 8, 32:, :].reshape(256, 128)
        high, low = halves(dot(blocks, values, TN))
        mixed_ref[128 * g : 128 * g + 128] = high
        mixed_ref[1024 + 128 * g : 1024 + 128 * g + 128] = low
    near_top, near_total = stat_ref[0:1], stat_ref[1:2]
    which = iota((1, 128), 1) >> 4
    req = req_ref[...]
    tops = []
    for r in range(4):
        t = jnp.max(jnp.where(req == r, far_top, VERY_LOW), axis=0, keepdims=True)
        tops.append(jnp.maximum(t, jnp.where(which == r, near_top, VERY_LOW)))
    peak = jnp.concatenate(tops, axis=0)
    for shift in (16, 32, 64):
        peak = jnp.maximum(peak, pltpu.roll(peak, shift, 1))
    far_w, near_w, totals = [], [], []
    for r in range(4):
        p = peak[r : r + 1]
        f = jnp.where(req == r, jnp.exp(far_top - p), 0.0)
        n = jnp.where(which == r, jnp.exp(near_top - p), 0.0)
        far_w.append(f)
        near_w.append(n)
        totals.append(jnp.sum(f * far_total, axis=0, keepdims=True) + n * near_total)
    total = jnp.concatenate(totals, axis=0)
    for shift in (16, 32, 64):
        total = total + pltpu.roll(total, shift, 1)
    scale = 1.0 / total
    same = (iota((16, 128), 1) & 15) == iota((16, 128), 0)

    def spread_rows(rows):
        return halves(jnp.concatenate([jnp.where(same, row, 0.0) for row in rows], axis=0))

    high, low = spread_rows([near_w[r] * scale[r : r + 1] for r in range(4)])
    home_high, home_low = halves(home_ref[...])
    acc = dot(high[:, :64], home_high, NN) + dot(high[:, :64], home_low, NN)
    acc += dot(low[:, :64], home_high, NN)
    far_w = [far_w[r] * scale[r : r + 1] for r in range(4)]
    spread = [spread_rows([far_w[r][g : g + 1] for r in range(4)]) for g in range(8)]
    high = jnp.concatenate([h for h, _ in spread], axis=1)
    low = jnp.concatenate([l for _, l in spread], axis=1)
    mixed_high, mixed_low = mixed_ref[:1024], mixed_ref[1024:]
    acc += dot(high, mixed_high, NN) + dot(high, mixed_low, NN) + dot(low, mixed_high, NN)
    lower = jnp.concatenate([acc[16 * r : 16 * r + 8] for r in range(4)], axis=0)
    upper = jnp.concatenate([acc[16 * r + 8 : 16 * r + 16] for r in range(4)], axis=0)
    split = jnp.concatenate([lower, upper], axis=0).astype(BF16).reshape(1, 2, 32, 128)
    out_ref[...] = jnp.broadcast_to(split, (32, 2, 32, 128)).reshape(64, 32, 128)


def join_kernel(mine_ref, received_ref, out_ref):
    zp = lax.axis_index("zp")
    out_ref[zp] = mine_ref[pl.ds(pl.multiple_of(zp * 1024, 1024), 1024)]
    out_ref[1 - zp] = received_ref[...]


def project_kernel(rows_ref, weight_ref, out_ref, wide_ref):
    q = iota((256, 256), 0)
    p = iota((256, 256), 1)
    move = p == 32 * ((q >> 2) & 7) + 8 * (q & 3) + (q >> 5)
    move = move.astype(F32).astype(BF16)
    for b in range(8):
        parts = [rows_ref[(8 * b + i - FIRST) % 64] for i in range(8)]
        moved = dot(move, jnp.concatenate(parts, axis=0), NN).astype(BF16)
        for h in range(8):
            wide_ref[32 * b : 32 * b + 32, 128 * h : 128 * h + 128] = moved[32 * h : 32 * h + 32]
    wide = wide_ref[...]
    for c in range(2):
        out_ref[c] = dot(wide, weight_ref[c], NN).astype(BF16).reshape(8, 32, 256)


def finish_kernel(sums_ref, base_ref, out_ref):
    total = base_ref[...]
    for s in range(16):
        total = total + sums_ref[s].astype(F32)
    out_ref[...] = total.astype(BF16)


def body(
    queries,
    new_keys,
    new_values,
    home_keys,
    home_values,
    home_len,
    lent_keys,
    lent_values,
    lent_req,
    lent_len,
    out_weight,
    residual,
):
    here = lax.axis_index(INST)
    packed = pl.pallas_call(
        pack_kernel,
        out_shape=jax.ShapeDtypeStruct((64, 64, 128), BF16),
        in_specs=[ANY] * 4,
        out_specs=ANY,
        scratch_shapes=[
            pltpu.SMEM((4032,), jnp.int32),
            pltpu.SMEM((63,), jnp.int32),
            pltpu.VMEM((63, 32, 128), BF16),
            pltpu.VMEM((63, 32, 128), BF16),
            pltpu.VMEM((64, 32, 128), BF16),
            pltpu.VMEM((64, 32, 128), BF16),
            pltpu.SemaphoreType.DMA((6,)),
        ],
        name="pack_lent",
    )(
        lent_req,
        lent_len,
        lent_keys.reshape(63, 32, 128),
        lent_values.reshape(63, 32, 128),
    )
    recv = lax.all_to_all(
        packed, INST, split_axis=0, concat_axis=0, tiled=True, axis_index_groups=ORDER
    )
    asked, req, sent = pl.pallas_call(
        ask_kernel,
        out_shape=(
            jax.ShapeDtypeStruct((8, 128, 128), BF16),
            jax.ShapeDtypeStruct((8, 128), F32),
            jax.ShapeDtypeStruct((1024, 256), BF16),
        ),
        in_specs=[SMEM, VMEM, VMEM, VMEM, ANY],
        out_specs=(VMEM,) * 3,
        compiler_params=PARAMS,
        name="ask_queries",
    )(
        here.reshape(1),
        jnp.pad(lent_req, (0, 64), constant_values=-4).reshape(32, 128),
        queries,
        out_weight,
        packed,
    )
    received = lax.ppermute(sent, "zp", [(0, 1), (1, 0)])
    home_out, home_stat, base = pl.pallas_call(
        home_kernel,
        out_shape=(
            jax.ShapeDtypeStruct((64, 128), F32),
            jax.ShapeDtypeStruct((2, 128), F32),
            jax.ShapeDtypeStruct((32, 256), F32),
        ),
        in_specs=[SMEM] + [VMEM] * 6,
        out_specs=(VMEM,) * 3,
        compiler_params=PARAMS,
        name="home_part",
    )(
        home_len,
        queries,
        new_keys.reshape(4, 128),
        new_values.reshape(4, 128),
        home_keys.reshape(4, 256, 128),
        home_values.reshape(4, 256, 128),
        residual,
    )
    copies = pl.pallas_call(
        attend_kernel,
        out_shape=jax.ShapeDtypeStruct((64, 32, 128), BF16),
        in_specs=[VMEM] * 5,
        out_specs=VMEM,
        scratch_shapes=[pltpu.VMEM((2048, 128), F32), pltpu.VMEM((2048, 128), BF16)],
        compiler_params=PARAMS,
        name="attend",
    )(asked, req, home_stat, home_out, recv)
    rows = lax.all_to_all(
        copies, INST, split_axis=0, concat_axis=0, tiled=True, axis_index_groups=ORDER
    )
    weights = pl.pallas_call(
        join_kernel,
        out_shape=jax.ShapeDtypeStruct((2, 1024, 256), BF16),
        in_specs=[VMEM, VMEM],
        out_specs=VMEM,
        compiler_params=PARAMS,
        cost_estimate=pl.CostEstimate(flops=10**11, bytes_accessed=2**21, transcendentals=0),
        name="join_weights",
    )(out_weight, received)
    partial = pl.pallas_call(
        project_kernel,
        out_shape=jax.ShapeDtypeStruct((2, 8, 32, 256), BF16),
        in_specs=[VMEM, VMEM],
        out_specs=VMEM,
        scratch_shapes=[pltpu.VMEM((256, 1024), BF16)],
        compiler_params=PARAMS,
        name="project",
    )(rows, weights)
    sums = lax.all_to_all(
        partial.reshape(16, 32, 256), ("zp", "tp"), split_axis=0, concat_axis=0, tiled=True
    )
    return pl.pallas_call(
        finish_kernel,
        out_shape=jax.ShapeDtypeStruct((32, 256), BF16),
        in_specs=[VMEM, VMEM],
        out_specs=VMEM,
        compiler_params=PARAMS,
        name="finish",
    )(sums, base)


def solution(mesh):
    placed = (
        P(INST, "tp", None),
        P(INST, "tp", None),
        P(INST, "tp", None),
        P(INST, None, "tp", None),
        P(INST, None, "tp", None),
        P(INST),
        P(INST, None, "tp", None),
        P(INST, None, "tp", None),
        P(),
        P(INST),
        P("tp", INST),
        P("tp", INST),
    )
    fine = Mesh(mesh.devices.reshape(8, 4, 2, 8), INST + ("tp",))
    return jax.shard_map(
        body, mesh=fine, in_specs=placed, out_specs=P("tp", INST), check_vma=False
    )
```

```python
import math

import jax
import jax.numpy as jnp
from jax import lax
from jax.experimental import pallas as pl
from jax.experimental.pallas import tpu as pltpu
from jax.sharding import Mesh, PartitionSpec as P

VERY_LOW = -1e30
ABSENT = 64.0
SCALE = 1.0 / math.sqrt(128.0)
F32 = jnp.float32
BF16 = jnp.bfloat16
NT = (((1,), (1,)), ((), ()))
TN = (((0,), (0,)), ((), ()))
NN = (((1,), (0,)), ((), ()))
INST = ("y", "zh", "zp")
FIRST = 52
ORDER = [[(FIRST + k) % 64 for k in range(64)]]
PARAMS = pltpu.CompilerParams(vmem_limit_bytes=16 * 2**20)
SMEM = pl.BlockSpec(memory_space=pltpu.SMEM)
ANY = pl.BlockSpec(memory_space=pl.ANY)
VMEM = pl.BlockSpec(memory_space=pltpu.VMEM)


def dot(a, b, dims):
    return lax.dot_general(a, b, dims, preferred_element_type=F32)


def iota(shape, axis):
    return lax.broadcasted_iota(jnp.int32, shape, axis)


def halves(x):
    high = x.astype(BF16)
    return high, (x - high.astype(F32)).astype(BF16)


def ask_kernel(
    here_ref, table_ref, q_ref, weight_ref, packed_ref, asked_ref, req_ref, sent_ref
):
    first = pl.multiple_of((1 - lax.axis_index("zp")) * 1024, 1024)
    sent_ref[...] = weight_ref[pl.ds(first, 1024)]
    here = here_ref[0]
    table = table_ref[...]
    found = jnp.where((table >> 2) == here, (table & 3) + 1, 0).astype(F32)
    lane = iota((1, 128), 1)
    rows = []
    for j in ORDER[0]:
        line, first = divmod(63 * j, 128)
        row = jnp.where(lane >= first, found[line : line + 1], 0.0)
        if first + 63 <= 128:
            row = jnp.where(lane < first + 63, row, 0.0)
        else:
            row = jnp.where(lane < first + 63 - 128, found[line + 1 : line + 2], row)
        rows.append(row)
    source = jnp.sum(jnp.concatenate(rows, axis=0), axis=1, keepdims=True) - 1.0
    source = jnp.broadcast_to(source, (64, 128))
    query = [q_ref[r].astype(F32) for r in range(4)]
    for g in range(8):
        rows = []
        for j in range(8 * g, 8 * g + 8):
            s = jnp.broadcast_to(source[j : j + 1], (16, 128))
            picked = jnp.where(s == 1.0, query[1], query[0])
            picked = jnp.where(s == 2.0, query[2], picked)
            rows.append(jnp.where(s == 3.0, query[3], picked))
        asked_ref[g] = jnp.concatenate(rows, axis=0).T.astype(BF16)
    group = iota((8, 128), 1) >> 4
    split = source.reshape(8, 8, 128)
    req = jnp.zeros((8, 128), F32)
    for n in range(8):
        req = jnp.where(group == n, split[:, n], req)
    req_ref[...] = req


def pack_kernel(
    req_ref, len_ref, k_ref, v_ref, out_ref,
    req_in, len_in, k_in, v_in, keys_ref, values_ref, sems
):
    loads = [
        pltpu.make_async_copy(source, target, sems.at[i])
        for i, (source, target) in enumerate(
            [(req_ref, req_in), (len_ref, len_in), (k_ref, k_in), (v_ref, v_in)]
        )
    ]
    for load in loads:
        load.start()
    here = lax.axis_index(INST)
    place = (here - FIRST) & 63
    token = iota((32, 128), 0).astype(F32).astype(BF16)
    keys_ref[place] = jnp.full((32, 128), ABSENT, F32).astype(BF16)
    values_ref[place] = jnp.zeros((32, 128), F32).astype(BF16)
    for load in loads[:3]:
        load.wait()
    for s in range(63):
        length = jnp.full((32, 128), len_in[s].astype(F32), F32).astype(BF16)
        keys = jnp.where(token < length, k_in[s], length + ABSENT)
        keys_ref[((req_in[63 * here + s] >> 2) - FIRST) & 63] = keys
    send_keys = pltpu.make_async_copy(keys_ref, out_ref.at[:, pl.ds(0, 32)], sems.at[4])
    send_keys.start()
    loads[3].wait()
    for s in range(63):
        values_ref[((req_in[63 * here + s] >> 2) - FIRST) & 63] = v_in[s]
    send_values = pltpu.make_async_copy(values_ref, out_ref.at[:, pl.ds(32, 32)], sems.at[5])
    send_values.start()
    send_keys.wait()
    send_values.wait()


def home_kernel(
    len_ref, q_ref, nk_ref, nv_ref, k_ref, v_ref, residual_ref, out_ref, stat_ref, base_ref
):
    query = q_ref[...].reshape(64, 128)
    query = jnp.concatenate([query, query], axis=0)
    owner = (iota((256, 128), 1) >> 4) & 3
    token = iota((256, 128), 0)
    scores = jnp.zeros((256, 128), F32)
    length = jnp.zeros((256, 128), jnp.int32)
    for r in range(4):
        scores = jnp.where(owner == r, dot(k_ref[r], query, NT), scores)
        length = jnp.where(owner == r, len_ref[r], length)
    scores = jnp.where(token < length, scores * SCALE, VERY_LOW)
    mine = ((iota((4, 128), 1) >> 4) & 3) == iota((4, 128), 0)
    fresh = dot(nk_ref[...], query, NT) * SCALE
    fresh = jnp.sum(jnp.where(mine, fresh, 0.0), axis=0, keepdims=True)
    top = jnp.maximum(jnp.max(scores, axis=0, keepdims=True), fresh)
    weights = jnp.exp(scores - top)
    own = jnp.exp(fresh - top)
    total = jnp.sum(weights, axis=0, keepdims=True) + own
    mixed = dot(jnp.where(mine, own, 0.0).astype(BF16), nv_ref[...], TN)
    for r in range(4):
        mixed += dot(jnp.where(owner == r, weights, 0.0).astype(BF16), v_ref[r], TN)
    out_ref[...] = mixed[:64]
    stat_ref[...] = jnp.concatenate([top, total], axis=0)
    base_ref[...] = residual_ref[...].astype(F32)


def attend_kernel(
    q_ref, req_ref, stat_ref, home_ref, recv_ref, out_ref, raw_ref, mixed_ref
):
    owner = iota((32, 128), 1) >> 4
    token = iota((8, 32, 128), 1).astype(F32)
    holder = (iota((8, 8, 128), 2) >> 4) == iota((8, 8, 128), 1)
    keep = [(owner == j).astype(F32).astype(BF16) for j in range(8)]
    for g in range(8):
        keys = recv_ref[8 * g : 8 * g + 8, :32, :].reshape(256, 128)
        raw_ref[256 * g : 256 * g + 256] = dot(keys, q_ref[g], NN)
    last = recv_ref[:, 31, :].astype(F32).reshape(8, 8, 128)
    length = jnp.where(last < 0.5 * ABSENT, 32.0, last - ABSENT)
    length = jnp.sum(jnp.where(holder, length, 0.0), axis=1, keepdims=True)
    scores = []
    for g in range(8):
        picked = raw_ref[256 * g : 256 * g + 32]
        for j in range(1, 8):
            first = 256 * g + 32 * j
            picked = jnp.where(owner == j, raw_ref[first : first + 32], picked)
        scores.append(picked)
    scores = jnp.concatenate(scores, axis=0).reshape(8, 32, 128)
    scores = jnp.where(token < length, scores * SCALE, VERY_LOW)
    far_top = jnp.max(scores, axis=1, keepdims=True)
    weights = jnp.exp(scores - far_top)
    far_total = jnp.sum(weights, axis=1, keepdims=True).reshape(8, 128)
    far_top = far_top.reshape(8, 128)
    weights = weights.astype(BF16)
    for g in range(8):
        blocks = jnp.concatenate([weights[g] * keep[j] for j in range(8)], axis=0)
        values = recv_ref[8 * g : 8 * g + 8, 32:, :].reshape(256, 128)
        high, low = halves(dot(blocks, values, TN))
        mixed_ref[128 * g : 128 * g + 128] = high
        mixed_ref[1024 + 128 * g : 1024 + 128 * g + 128] = low
    near_top, near_total = stat_ref[0:1], stat_ref[1:2]
    which = iota((1, 128), 1) >> 4
    req = req_ref[...]
    tops = []
    for r in range(4):
        t = jnp.max(jnp.where(req == r, far_top, VERY_LOW), axis=0, keepdims=True)
        tops.append(jnp.maximum(t, jnp.where(which == r, near_top, VERY_LOW)))
    peak = jnp.concatenate(tops, axis=0)
    for shift in (16, 32, 64):
        peak = jnp.maximum(peak, pltpu.roll(peak, shift, 1))
    far_w, near_w, totals = [], [], []
    for r in range(4):
        p = peak[r : r + 1]
        f = jnp.where(req == r, jnp.exp(far_top - p), 0.0)
        n = jnp.where(which == r, jnp.exp(near_top - p), 0.0)
        far_w.append(f)
        near_w.append(n)
        totals.append(jnp.sum(f * far_total, axis=0, keepdims=True) + n * near_total)
    total = jnp.concatenate(totals, axis=0)
    for shift in (16, 32, 64):
        total = total + pltpu.roll(total, shift, 1)
    scale = 1.0 / total
    same = (iota((16, 128), 1) & 15) == iota((16, 128), 0)

    def spread_rows(rows):
        return halves(jnp.concatenate([jnp.where(same, row, 0.0) for row in rows], axis=0))

    high, low = spread_rows([near_w[r] * scale[r : r + 1] for r in range(4)])
    home_high, home_low = halves(home_ref[...])
    acc = dot(high[:, :64], home_high, NN) + dot(high[:, :64], home_low, NN)
    acc += dot(low[:, :64], home_high, NN)
    far_w = [far_w[r] * scale[r : r + 1] for r in range(4)]
    spread = [spread_rows([far_w[r][g : g + 1] for r in range(4)]) for g in range(8)]
    high = jnp.concatenate([h for h, _ in spread], axis=1)
    low = jnp.concatenate([l for _, l in spread], axis=1)
    mixed_high, mixed_low = mixed_ref[:1024], mixed_ref[1024:]
    acc += dot(high, mixed_high, NN) + dot(high, mixed_low, NN) + dot(low, mixed_high, NN)
    lower = jnp.concatenate([acc[16 * r : 16 * r + 8] for r in range(4)], axis=0)
    upper = jnp.concatenate([acc[16 * r + 8 : 16 * r + 16] for r in range(4)], axis=0)
    split = jnp.concatenate([lower, upper], axis=0).astype(BF16).reshape(1, 2, 32, 128)
    out_ref[...] = jnp.broadcast_to(split, (32, 2, 32, 128)).reshape(64, 32, 128)


def join_kernel(mine_ref, received_ref, out_ref):
    zp = lax.axis_index("zp")
    out_ref[zp] = mine_ref[pl.ds(pl.multiple_of(zp * 1024, 1024), 1024)]
    out_ref[1 - zp] = received_ref[...]


def project_kernel(rows_ref, weight_ref, out_ref, wide_ref):
    q = iota((256, 256), 0)
    p = iota((256, 256), 1)
    move = p == 32 * ((q >> 2) & 7) + 8 * (q & 3) + (q >> 5)
    move = move.astype(F32).astype(BF16)
    for b in range(8):
        parts = [rows_ref[(8 * b + i - FIRST) % 64] for i in range(8)]
        moved = dot(move, jnp.concatenate(parts, axis=0), NN).astype(BF16)
        for h in range(8):
            wide_ref[32 * b : 32 * b + 32, 128 * h : 128 * h + 128] = moved[32 * h : 32 * h + 32]
    wide = wide_ref[...]
    for c in range(2):
        out_ref[c] = dot(wide, weight_ref[c], NN).astype(BF16).reshape(8, 32, 256)


def finish_kernel(sums_ref, base_ref, out_ref):
    total = base_ref[...]
    for s in range(16):
        total = total + sums_ref[s].astype(F32)
    out_ref[...] = total.astype(BF16)


def body(
    queries,
    new_keys,
    new_values,
    home_keys,
    home_values,
    home_len,
    lent_keys,
    lent_values,
    lent_req,
    lent_len,
    out_weight,
    residual,
):
    here = lax.axis_index(INST)
    packed = pl.pallas_call(
        pack_kernel,
        out_shape=jax.ShapeDtypeStruct((64, 64, 128), BF16),
        in_specs=[ANY] * 4,
        out_specs=ANY,
        scratch_shapes=[
            pltpu.SMEM((4032,), jnp.int32),
            pltpu.SMEM((63,), jnp.int32),
            pltpu.VMEM((63, 32, 128), BF16),
            pltpu.VMEM((63, 32, 128), BF16),
            pltpu.VMEM((64, 32, 128), BF16),
            pltpu.VMEM((64, 32, 128), BF16),
            pltpu.SemaphoreType.DMA((6,)),
        ],
        name="pack_lent",
    )(
        lent_req,
        lent_len,
        lent_keys.reshape(63, 32, 128),
        lent_values.reshape(63, 32, 128),
    )
    recv = lax.all_to_all(
        packed, INST, split_axis=0, concat_axis=0, tiled=True, axis_index_groups=ORDER
    )
    asked, req, sent = pl.pallas_call(
        ask_kernel,
        out_shape=(
            jax.ShapeDtypeStruct((8, 128, 128), BF16),
            jax.ShapeDtypeStruct((8, 128), F32),
            jax.ShapeDtypeStruct((1024, 256), BF16),
        ),
        in_specs=[SMEM, VMEM, VMEM, VMEM, ANY],
        out_specs=(VMEM,) * 3,
        compiler_params=PARAMS,
        name="ask_queries",
    )(
        here.reshape(1),
        jnp.pad(lent_req, (0, 64), constant_values=-4).reshape(32, 128),
        queries,
        out_weight,
        packed,
    )
    received = lax.ppermute(sent, "zp", [(0, 1), (1, 0)])
    home_out, home_stat, base = pl.pallas_call(
        home_kernel,
        out_shape=(
            jax.ShapeDtypeStruct((64, 128), F32),
            jax.ShapeDtypeStruct((2, 128), F32),
            jax.ShapeDtypeStruct((32, 256), F32),
        ),
        in_specs=[SMEM] + [VMEM] * 6,
        out_specs=(VMEM,) * 3,
        compiler_params=PARAMS,
        name="home_part",
    )(
        home_len,
        queries,
        new_keys.reshape(4, 128),
        new_values.reshape(4, 128),
        home_keys.reshape(4, 256, 128),
        home_values.reshape(4, 256, 128),
        residual,
    )
    copies = pl.pallas_call(
        attend_kernel,
        out_shape=jax.ShapeDtypeStruct((64, 32, 128), BF16),
        in_specs=[VMEM] * 5,
        out_specs=VMEM,
        scratch_shapes=[pltpu.VMEM((2048, 128), F32), pltpu.VMEM((2048, 128), BF16)],
        compiler_params=PARAMS,
        name="attend",
    )(asked, req, home_stat, home_out, recv)
    rows = lax.all_to_all(
        copies, INST, split_axis=0, concat_axis=0, tiled=True, axis_index_groups=ORDER
    )
    weights = pl.pallas_call(
        join_kernel,
        out_shape=jax.ShapeDtypeStruct((2, 1024, 256), BF16),
        in_specs=[VMEM, VMEM],
        out_specs=VMEM,
        compiler_params=PARAMS,
        cost_estimate=pl.CostEstimate(flops=10**11, bytes_accessed=2**21, transcendentals=0),
        name="join_weights",
    )(out_weight, received)
    partial = pl.pallas_call(
        project_kernel,
        out_shape=jax.ShapeDtypeStruct((2, 8, 32, 256), BF16),
        in_specs=[VMEM, VMEM],
        out_specs=VMEM,
        scratch_shapes=[pltpu.VMEM((256, 1024), BF16)],
        compiler_params=PARAMS,
        name="project",
    )(rows, weights)
    sums = lax.all_to_all(
        partial.reshape(16, 32, 256), ("zp", "tp"), split_axis=0, concat_axis=0, tiled=True
    )
    return pl.pallas_call(
        finish_kernel,
        out_shape=jax.ShapeDtypeStruct((32, 256), BF16),
        in_specs=[VMEM, VMEM],
        out_specs=VMEM,
        compiler_params=PARAMS,
        name="finish",
    )(sums, base)


def solution(mesh):
    placed = (
        P(INST, "tp", None),
        P(INST, "tp", None),
        P(INST, "tp", None),
        P(INST, None, "tp", None),
        P(INST, None, "tp", None),
        P(INST),
        P(INST, None, "tp", None),
        P(INST, None, "tp", None),
        P(),
        P(INST),
        P("tp", INST),
        P("tp", INST),
    )
    fine = Mesh(mesh.devices.reshape(8, 4, 2, 8), INST + ("tp",))
    return jax.shard_map(
        body, mesh=fine, in_specs=placed, out_specs=P("tp", INST), check_vma=False
    )
```

```python
import math

import jax
import jax.numpy as jnp
from jax import lax
from jax.experimental import pallas as pl
from jax.experimental.pallas import tpu as pltpu
from jax.sharding import Mesh, PartitionSpec as P

VERY_LOW = -1e30
ABSENT = 64.0
SCALE = 1.0 / math.sqrt(128.0)
F32 = jnp.float32
BF16 = jnp.bfloat16
NT = (((1,), (1,)), ((), ()))
TN = (((0,), (0,)), ((), ()))
NN = (((1,), (0,)), ((), ()))
INST = ("y", "zh", "zp")
FIRST = 52
ORDER = [[(FIRST + k) % 64 for k in range(64)]]
PARAMS = pltpu.CompilerParams(vmem_limit_bytes=16 * 2**20)
SMEM = pl.BlockSpec(memory_space=pltpu.SMEM)
ANY = pl.BlockSpec(memory_space=pl.ANY)
VMEM = pl.BlockSpec(memory_space=pltpu.VMEM)


def dot(a, b, dims):
    return lax.dot_general(a, b, dims, preferred_element_type=F32)


def iota(shape, axis):
    return lax.broadcasted_iota(jnp.int32, shape, axis)


def halves(x):
    high = x.astype(BF16)
    return high, (x - high.astype(F32)).astype(BF16)


def ask_kernel(
    here_ref, table_ref, q_ref, weight_ref, packed_ref, asked_ref, req_ref, sent_ref
):
    first = pl.multiple_of((1 - lax.axis_index("zp")) * 1024, 1024)
    sent_ref[...] = weight_ref[pl.ds(first, 1024)]
    here = here_ref[0]
    table = table_ref[...]
    found = jnp.where((table >> 2) == here, (table & 3) + 1, 0).astype(F32)
    lane = iota((1, 128), 1)
    rows = []
    for j in ORDER[0]:
        line, first = divmod(63 * j, 128)
        row = jnp.where(lane >= first, found[line : line + 1], 0.0)
        if first + 63 <= 128:
            row = jnp.where(lane < first + 63, row, 0.0)
        else:
            row = jnp.where(lane < first + 63 - 128, found[line + 1 : line + 2], row)
        rows.append(row)
    source = jnp.sum(jnp.concatenate(rows, axis=0), axis=1, keepdims=True) - 1.0
    source = jnp.broadcast_to(source, (64, 128))
    query = [q_ref[r].astype(F32) for r in range(4)]
    for g in range(8):
        rows = []
        for j in range(8 * g, 8 * g + 8):
            s = jnp.broadcast_to(source[j : j + 1], (16, 128))
            picked = jnp.where(s == 1.0, query[1], query[0])
            picked = jnp.where(s == 2.0, query[2], picked)
            rows.append(jnp.where(s == 3.0, query[3], picked))
        asked_ref[g] = jnp.concatenate(rows, axis=0).T.astype(BF16)
    group = iota((8, 128), 1) >> 4
    split = source.reshape(8, 8, 128)
    req = jnp.zeros((8, 128), F32)
    for n in range(8):
        req = jnp.where(group == n, split[:, n], req)
    req_ref[...] = req


def pack_kernel(
    req_ref, len_ref, k_ref, v_ref, out_ref,
    req_in, len_in, k_in, v_in, keys_ref, values_ref, sems
):
    loads = [
        pltpu.make_async_copy(source, target, sems.at[i])
        for i, (source, target) in enumerate(
            [(req_ref, req_in), (len_ref, len_in), (k_ref, k_in), (v_ref, v_in)]
        )
    ]
    for load in loads:
        load.start()
    here = lax.axis_index(INST)
    place = (here - FIRST) & 63
    token = iota((32, 128), 0).astype(F32).astype(BF16)
    keys_ref[place] = jnp.full((32, 128), ABSENT, F32).astype(BF16)
    values_ref[place] = jnp.zeros((32, 128), F32).astype(BF16)
    for load in loads[:3]:
        load.wait()
    places = [((req_in[63 * here + s] >> 2) - FIRST) & 63 for s in range(63)]
    for s in range(63):
        length = jnp.full((32, 128), len_in[s].astype(F32), F32).astype(BF16)
        keys = jnp.where(token < length, k_in[s], length + ABSENT)
        keys_ref[places[s]] = keys
    send_keys = pltpu.make_async_copy(keys_ref, out_ref.at[:, pl.ds(0, 32)], sems.at[4])
    send_keys.start()
    loads[3].wait()
    for s in range(63):
        values_ref[places[s]] = v_in[s]
    send_values = pltpu.make_async_copy(values_ref, out_ref.at[:, pl.ds(32, 32)], sems.at[5])
    send_values.start()
    send_keys.wait()
    send_values.wait()


def home_kernel(
    len_ref, q_ref, nk_ref, nv_ref, k_ref, v_ref, residual_ref, out_ref, stat_ref, base_ref
):
    query = q_ref[...].reshape(64, 128)
    query = jnp.concatenate([query, query], axis=0)
    owner = (iota((256, 128), 1) >> 4) & 3
    token = iota((256, 128), 0)
    scores = jnp.zeros((256, 128), F32)
    length = jnp.zeros((256, 128), jnp.int32)
    for r in range(4):
        scores = jnp.where(owner == r, dot(k_ref[r], query, NT), scores)
        length = jnp.where(owner == r, len_ref[r], length)
    scores = jnp.where(token < length, scores * SCALE, VERY_LOW)
    mine = ((iota((4, 128), 1) >> 4) & 3) == iota((4, 128), 0)
    fresh = dot(nk_ref[...], query, NT) * SCALE
    fresh = jnp.sum(jnp.where(mine, fresh, 0.0), axis=0, keepdims=True)
    top = jnp.maximum(jnp.max(scores, axis=0, keepdims=True), fresh)
    weights = jnp.exp(scores - top)
    own = jnp.exp(fresh - top)
    total = jnp.sum(weights, axis=0, keepdims=True) + own
    mixed = dot(jnp.where(mine, own, 0.0).astype(BF16), nv_ref[...], TN)
    for r in range(4):
        mixed += dot(jnp.where(owner == r, weights, 0.0).astype(BF16), v_ref[r], TN)
    out_ref[...] = mixed[:64]
    stat_ref[...] = jnp.concatenate([top, total], axis=0)
    base_ref[...] = residual_ref[...].astype(F32)


def attend_kernel(
    q_ref, req_ref, stat_ref, home_ref, recv_ref, out_ref, raw_ref, mixed_ref
):
    owner = iota((32, 128), 1) >> 4
    token = iota((8, 32, 128), 1).astype(F32)
    holder = (iota((8, 8, 128), 2) >> 4) == iota((8, 8, 128), 1)
    keep = [(owner == j).astype(F32).astype(BF16) for j in range(8)]
    for g in range(8):
        keys = recv_ref[8 * g : 8 * g + 8, :32, :].reshape(256, 128)
        raw_ref[256 * g : 256 * g + 256] = dot(keys, q_ref[g], NN)
    last = recv_ref[:, 31, :].astype(F32).reshape(8, 8, 128)
    length = jnp.where(last < 0.5 * ABSENT, 32.0, last - ABSENT)
    length = jnp.sum(jnp.where(holder, length, 0.0), axis=1, keepdims=True)
    scores = []
    for g in range(8):
        picked = raw_ref[256 * g : 256 * g + 32]
        for j in range(1, 8):
            first = 256 * g + 32 * j
            picked = jnp.where(owner == j, raw_ref[first : first + 32], picked)
        scores.append(picked)
    scores = jnp.concatenate(scores, axis=0).reshape(8, 32, 128)
    scores = jnp.where(token < length, scores * SCALE, VERY_LOW)
    far_top = jnp.max(scores, axis=1, keepdims=True)
    weights = jnp.exp(scores - far_top)
    far_total = jnp.sum(weights, axis=1, keepdims=True).reshape(8, 128)
    far_top = far_top.reshape(8, 128)
    weights = weights.astype(BF16)
    for g in range(8):
        blocks = jnp.concatenate([weights[g] * keep[j] for j in range(8)], axis=0)
        values = recv_ref[8 * g : 8 * g + 8, 32:, :].reshape(256, 128)
        high, low = halves(dot(blocks, values, TN))
        mixed_ref[128 * g : 128 * g + 128] = high
        mixed_ref[1024 + 128 * g : 1024 + 128 * g + 128] = low
    near_top, near_total = stat_ref[0:1], stat_ref[1:2]
    which = iota((1, 128), 1) >> 4
    req = req_ref[...]
    tops = []
    for r in range(4):
        t = jnp.max(jnp.where(req == r, far_top, VERY_LOW), axis=0, keepdims=True)
        tops.append(jnp.maximum(t, jnp.where(which == r, near_top, VERY_LOW)))
    peak = jnp.concatenate(tops, axis=0)
    for shift in (16, 32, 64):
        peak = jnp.maximum(peak, pltpu.roll(peak, shift, 1))
    far_w, near_w, totals = [], [], []
    for r in range(4):
        p = peak[r : r + 1]
        f = jnp.where(req == r, jnp.exp(far_top - p), 0.0)
        n = jnp.where(which == r, jnp.exp(near_top - p), 0.0)
        far_w.append(f)
        near_w.append(n)
        totals.append(jnp.sum(f * far_total, axis=0, keepdims=True) + n * near_total)
    total = jnp.concatenate(totals, axis=0)
    for shift in (16, 32, 64):
        total = total + pltpu.roll(total, shift, 1)
    scale = 1.0 / total
    same = (iota((16, 128), 1) & 15) == iota((16, 128), 0)

    def spread_rows(rows):
        return halves(jnp.concatenate([jnp.where(same, row, 0.0) for row in rows], axis=0))

    high, low = spread_rows([near_w[r] * scale[r : r + 1] for r in range(4)])
    home_high, home_low = halves(home_ref[...])
    acc = dot(high[:, :64], home_high, NN) + dot(high[:, :64], home_low, NN)
    acc += dot(low[:, :64], home_high, NN)
    far_w = [far_w[r] * scale[r : r + 1] for r in range(4)]
    spread = [spread_rows([far_w[r][g : g + 1] for r in range(4)]) for g in range(8)]
    high = jnp.concatenate([h for h, _ in spread], axis=1)
    low = jnp.concatenate([l for _, l in spread], axis=1)
    mixed_high, mixed_low = mixed_ref[:1024], mixed_ref[1024:]
    acc += dot(high, mixed_high, NN) + dot(high, mixed_low, NN) + dot(low, mixed_high, NN)
    lower = jnp.concatenate([acc[16 * r : 16 * r + 8] for r in range(4)], axis=0)
    upper = jnp.concatenate([acc[16 * r + 8 : 16 * r + 16] for r in range(4)], axis=0)
    split = jnp.concatenate([lower, upper], axis=0).astype(BF16).reshape(1, 2, 32, 128)
    out_ref[...] = jnp.broadcast_to(split, (32, 2, 32, 128)).reshape(64, 32, 128)


def join_kernel(mine_ref, received_ref, out_ref):
    zp = lax.axis_index("zp")
    out_ref[zp] = mine_ref[pl.ds(pl.multiple_of(zp * 1024, 1024), 1024)]
    out_ref[1 - zp] = received_ref[...]


def project_kernel(rows_ref, weight_ref, out_ref, wide_ref):
    q = iota((256, 256), 0)
    p = iota((256, 256), 1)
    move = p == 32 * ((q >> 2) & 7) + 8 * (q & 3) + (q >> 5)
    move = move.astype(F32).astype(BF16)
    for b in range(8):
        parts = [rows_ref[(8 * b + i - FIRST) % 64] for i in range(8)]
        moved = dot(move, jnp.concatenate(parts, axis=0), NN).astype(BF16)
        for h in range(8):
            wide_ref[32 * b : 32 * b + 32, 128 * h : 128 * h + 128] = moved[32 * h : 32 * h + 32]
    wide = wide_ref[...]
    for c in range(2):
        out_ref[c] = dot(wide, weight_ref[c], NN).astype(BF16).reshape(8, 32, 256)


def finish_kernel(sums_ref, base_ref, out_ref):
    total = base_ref[...]
    for s in range(16):
        total = total + sums_ref[s].astype(F32)
    out_ref[...] = total.astype(BF16)


def body(
    queries,
    new_keys,
    new_values,
    home_keys,
    home_values,
    home_len,
    lent_keys,
    lent_values,
    lent_req,
    lent_len,
    out_weight,
    residual,
):
    here = lax.axis_index(INST)
    packed = pl.pallas_call(
        pack_kernel,
        out_shape=jax.ShapeDtypeStruct((64, 64, 128), BF16),
        in_specs=[ANY] * 4,
        out_specs=ANY,
        scratch_shapes=[
            pltpu.SMEM((4032,), jnp.int32),
            pltpu.SMEM((63,), jnp.int32),
            pltpu.VMEM((63, 32, 128), BF16),
            pltpu.VMEM((63, 32, 128), BF16),
            pltpu.VMEM((64, 32, 128), BF16),
            pltpu.VMEM((64, 32, 128), BF16),
            pltpu.SemaphoreType.DMA((6,)),
        ],
        name="pack_lent",
    )(
        lent_req,
        lent_len,
        lent_keys.reshape(63, 32, 128),
        lent_values.reshape(63, 32, 128),
    )
    recv = lax.all_to_all(
        packed, INST, split_axis=0, concat_axis=0, tiled=True, axis_index_groups=ORDER
    )
    asked, req, sent = pl.pallas_call(
        ask_kernel,
        out_shape=(
            jax.ShapeDtypeStruct((8, 128, 128), BF16),
            jax.ShapeDtypeStruct((8, 128), F32),
            jax.ShapeDtypeStruct((1024, 256), BF16),
        ),
        in_specs=[SMEM, VMEM, VMEM, VMEM, ANY],
        out_specs=(VMEM,) * 3,
        compiler_params=PARAMS,
        name="ask_queries",
    )(
        here.reshape(1),
        jnp.pad(lent_req, (0, 64), constant_values=-4).reshape(32, 128),
        queries,
        out_weight,
        packed,
    )
    received = lax.ppermute(sent, "zp", [(0, 1), (1, 0)])
    home_out, home_stat, base = pl.pallas_call(
        home_kernel,
        out_shape=(
            jax.ShapeDtypeStruct((64, 128), F32),
            jax.ShapeDtypeStruct((2, 128), F32),
            jax.ShapeDtypeStruct((32, 256), F32),
        ),
        in_specs=[SMEM] + [VMEM] * 6,
        out_specs=(VMEM,) * 3,
        compiler_params=PARAMS,
        name="home_part",
    )(
        home_len,
        queries,
        new_keys.reshape(4, 128),
        new_values.reshape(4, 128),
        home_keys.reshape(4, 256, 128),
        home_values.reshape(4, 256, 128),
        residual,
    )
    copies = pl.pallas_call(
        attend_kernel,
        out_shape=jax.ShapeDtypeStruct((64, 32, 128), BF16),
        in_specs=[VMEM] * 5,
        out_specs=VMEM,
        scratch_shapes=[pltpu.VMEM((2048, 128), F32), pltpu.VMEM((2048, 128), BF16)],
        compiler_params=PARAMS,
        name="attend",
    )(asked, req, home_stat, home_out, recv)
    rows = lax.all_to_all(
        copies, INST, split_axis=0, concat_axis=0, tiled=True, axis_index_groups=ORDER
    )
    weights = pl.pallas_call(
        join_kernel,
        out_shape=jax.ShapeDtypeStruct((2, 1024, 256), BF16),
        in_specs=[VMEM, VMEM],
        out_specs=VMEM,
        compiler_params=PARAMS,
        cost_estimate=pl.CostEstimate(flops=10**11, bytes_accessed=2**21, transcendentals=0),
        name="join_weights",
    )(out_weight, received)
    partial = pl.pallas_call(
        project_kernel,
        out_shape=jax.ShapeDtypeStruct((2, 8, 32, 256), BF16),
        in_specs=[VMEM, VMEM],
        out_specs=VMEM,
        scratch_shapes=[pltpu.VMEM((256, 1024), BF16)],
        compiler_params=PARAMS,
        name="project",
    )(rows, weights)
    sums = lax.all_to_all(
        partial.reshape(16, 32, 256), ("zp", "tp"), split_axis=0, concat_axis=0, tiled=True
    )
    return pl.pallas_call(
        finish_kernel,
        out_shape=jax.ShapeDtypeStruct((32, 256), BF16),
        in_specs=[VMEM, VMEM],
        out_specs=VMEM,
        compiler_params=PARAMS,
        name="finish",
    )(sums, base)


def solution(mesh):
    placed = (
        P(INST, "tp", None),
        P(INST, "tp", None),
        P(INST, "tp", None),
        P(INST, None, "tp", None),
        P(INST, None, "tp", None),
        P(INST),
        P(INST, None, "tp", None),
        P(INST, None, "tp", None),
        P(),
        P(INST),
        P("tp", INST),
        P("tp", INST),
    )
    fine = Mesh(mesh.devices.reshape(8, 4, 2, 8), INST + ("tp",))
    return jax.shard_map(
        body, mesh=fine, in_specs=placed, out_specs=P("tp", INST), check_vma=False
    )
```

```python
import math

import jax
import jax.numpy as jnp
from jax import lax
from jax.experimental import pallas as pl
from jax.experimental.pallas import tpu as pltpu
from jax.sharding import Mesh, PartitionSpec as P

VERY_LOW = -1e30
ABSENT = 64.0
SCALE = 1.0 / math.sqrt(128.0)
F32 = jnp.float32
BF16 = jnp.bfloat16
NT = (((1,), (1,)), ((), ()))
TN = (((0,), (0,)), ((), ()))
NN = (((1,), (0,)), ((), ()))
INST = ("y", "zh", "zp")
FIRST = 60
ORDER = [[(FIRST + k) % 64 for k in range(64)]]
PARAMS = pltpu.CompilerParams(vmem_limit_bytes=16 * 2**20)
SMEM = pl.BlockSpec(memory_space=pltpu.SMEM)
ANY = pl.BlockSpec(memory_space=pl.ANY)
VMEM = pl.BlockSpec(memory_space=pltpu.VMEM)


def dot(a, b, dims):
    return lax.dot_general(a, b, dims, preferred_element_type=F32)


def iota(shape, axis):
    return lax.broadcasted_iota(jnp.int32, shape, axis)


def halves(x):
    high = x.astype(BF16)
    return high, (x - high.astype(F32)).astype(BF16)


def ask_kernel(
    here_ref, table_ref, q_ref, weight_ref, packed_ref, asked_ref, req_ref, sent_ref
):
    first = pl.multiple_of((1 - lax.axis_index("zp")) * 1024, 1024)
    sent_ref[...] = weight_ref[pl.ds(first, 1024)]
    here = here_ref[0]
    table = table_ref[...]
    found = jnp.where((table >> 2) == here, (table & 3) + 1, 0).astype(F32)
    lane = iota((1, 128), 1)
    rows = []
    for j in ORDER[0]:
        line, first = divmod(63 * j, 128)
        row = jnp.where(lane >= first, found[line : line + 1], 0.0)
        if first + 63 <= 128:
            row = jnp.where(lane < first + 63, row, 0.0)
        else:
            row = jnp.where(lane < first + 63 - 128, found[line + 1 : line + 2], row)
        rows.append(row)
    source = jnp.sum(jnp.concatenate(rows, axis=0), axis=1, keepdims=True) - 1.0
    source = jnp.broadcast_to(source, (64, 128))
    query = [q_ref[r].astype(F32) for r in range(4)]
    for g in range(8):
        rows = []
        for j in range(8 * g, 8 * g + 8):
            s = jnp.broadcast_to(source[j : j + 1], (16, 128))
            picked = jnp.where(s == 1.0, query[1], query[0])
            picked = jnp.where(s == 2.0, query[2], picked)
            rows.append(jnp.where(s == 3.0, query[3], picked))
        asked_ref[g] = jnp.concatenate(rows, axis=0).T.astype(BF16)
    group = iota((8, 128), 1) >> 4
    split = source.reshape(8, 8, 128)
    req = jnp.zeros((8, 128), F32)
    for n in range(8):
        req = jnp.where(group == n, split[:, n], req)
    req_ref[...] = req


def pack_kernel(
    req_ref, len_ref, k_ref, v_ref, out_ref,
    req_in, len_in, k_in, v_in, keys_ref, values_ref, sems
):
    loads = [
        pltpu.make_async_copy(source, target, sems.at[i])
        for i, (source, target) in enumerate(
            [(req_ref, req_in), (len_ref, len_in), (k_ref, k_in), (v_ref, v_in)]
        )
    ]
    for load in loads:
        load.start()
    here = lax.axis_index(INST)
    place = (here - FIRST) & 63
    token = iota((32, 128), 0).astype(F32).astype(BF16)
    keys_ref[place] = jnp.full((32, 128), ABSENT, F32).astype(BF16)
    values_ref[place] = jnp.zeros((32, 128), F32).astype(BF16)
    for load in loads[:3]:
        load.wait()
    places = [((req_in[63 * here + s] >> 2) - FIRST) & 63 for s in range(63)]
    for s in range(63):
        length = jnp.full((32, 128), len_in[s].astype(F32), F32).astype(BF16)
        keys = jnp.where(token < length, k_in[s], length + ABSENT)
        keys_ref[places[s]] = keys
    send_keys = pltpu.make_async_copy(keys_ref, out_ref.at[:, pl.ds(0, 32)], sems.at[4])
    send_keys.start()
    loads[3].wait()
    for s in range(63):
        values_ref[places[s]] = v_in[s]
    send_values = pltpu.make_async_copy(values_ref, out_ref.at[:, pl.ds(32, 32)], sems.at[5])
    send_values.start()
    send_keys.wait()
    send_values.wait()


def home_kernel(
    len_ref, q_ref, nk_ref, nv_ref, k_ref, v_ref, residual_ref, out_ref, stat_ref, base_ref
):
    query = q_ref[...].reshape(64, 128)
    query = jnp.concatenate([query, query], axis=0)
    owner = (iota((256, 128), 1) >> 4) & 3
    token = iota((256, 128), 0)
    scores = jnp.zeros((256, 128), F32)
    length = jnp.zeros((256, 128), jnp.int32)
    for r in range(4):
        scores = jnp.where(owner == r, dot(k_ref[r], query, NT), scores)
        length = jnp.where(owner == r, len_ref[r], length)
    scores = jnp.where(token < length, scores * SCALE, VERY_LOW)
    mine = ((iota((4, 128), 1) >> 4) & 3) == iota((4, 128), 0)
    fresh = dot(nk_ref[...], query, NT) * SCALE
    fresh = jnp.sum(jnp.where(mine, fresh, 0.0), axis=0, keepdims=True)
    top = jnp.maximum(jnp.max(scores, axis=0, keepdims=True), fresh)
    weights = jnp.exp(scores - top)
    own = jnp.exp(fresh - top)
    total = jnp.sum(weights, axis=0, keepdims=True) + own
    mixed = dot(jnp.where(mine, own, 0.0).astype(BF16), nv_ref[...], TN)
    for r in range(4):
        mixed += dot(jnp.where(owner == r, weights, 0.0).astype(BF16), v_ref[r], TN)
    out_ref[...] = mixed[:64]
    stat_ref[...] = jnp.concatenate([top, total], axis=0)
    base_ref[...] = residual_ref[...].astype(F32)


def attend_kernel(
    q_ref, req_ref, stat_ref, home_ref, recv_ref, out_ref, raw_ref, mixed_ref
):
    owner = iota((32, 128), 1) >> 4
    token = iota((8, 32, 128), 1).astype(F32)
    holder = (iota((8, 8, 128), 2) >> 4) == iota((8, 8, 128), 1)
    keep = [(owner == j).astype(F32).astype(BF16) for j in range(8)]
    for g in range(8):
        keys = recv_ref[8 * g : 8 * g + 8, :32, :].reshape(256, 128)
        raw_ref[256 * g : 256 * g + 256] = dot(keys, q_ref[g], NN)
    last = recv_ref[:, 31, :].astype(F32).reshape(8, 8, 128)
    length = jnp.where(last < 0.5 * ABSENT, 32.0, last - ABSENT)
    length = jnp.sum(jnp.where(holder, length, 0.0), axis=1, keepdims=True)
    scores = []
    for g in range(8):
        picked = raw_ref[256 * g : 256 * g + 32]
        for j in range(1, 8):
            first = 256 * g + 32 * j
            picked = jnp.where(owner == j, raw_ref[first : first + 32], picked)
        scores.append(picked)
    scores = jnp.concatenate(scores, axis=0).reshape(8, 32, 128)
    scores = jnp.where(token < length, scores * SCALE, VERY_LOW)
    far_top = jnp.max(scores, axis=1, keepdims=True)
    weights = jnp.exp(scores - far_top)
    far_total = jnp.sum(weights, axis=1, keepdims=True).reshape(8, 128)
    far_top = far_top.reshape(8, 128)
    weights = weights.astype(BF16)
    for g in range(8):
        blocks = jnp.concatenate([weights[g] * keep[j] for j in range(8)], axis=0)
        values = recv_ref[8 * g : 8 * g + 8, 32:, :].reshape(256, 128)
        high, low = halves(dot(blocks, values, TN))
        mixed_ref[128 * g : 128 * g + 128] = high
        mixed_ref[1024 + 128 * g : 1024 + 128 * g + 128] = low
    near_top, near_total = stat_ref[0:1], stat_ref[1:2]
    which = iota((1, 128), 1) >> 4
    req = req_ref[...]
    tops = []
    for r in range(4):
        t = jnp.max(jnp.where(req == r, far_top, VERY_LOW), axis=0, keepdims=True)
        tops.append(jnp.maximum(t, jnp.where(which == r, near_top, VERY_LOW)))
    peak = jnp.concatenate(tops, axis=0)
    for shift in (16, 32, 64):
        peak = jnp.maximum(peak, pltpu.roll(peak, shift, 1))
    far_w, near_w, totals = [], [], []
    for r in range(4):
        p = peak[r : r + 1]
        f = jnp.where(req == r, jnp.exp(far_top - p), 0.0)
        n = jnp.where(which == r, jnp.exp(near_top - p), 0.0)
        far_w.append(f)
        near_w.append(n)
        totals.append(jnp.sum(f * far_total, axis=0, keepdims=True) + n * near_total)
    total = jnp.concatenate(totals, axis=0)
    for shift in (16, 32, 64):
        total = total + pltpu.roll(total, shift, 1)
    scale = 1.0 / total
    same = (iota((16, 128), 1) & 15) == iota((16, 128), 0)

    def spread_rows(rows):
        return halves(jnp.concatenate([jnp.where(same, row, 0.0) for row in rows], axis=0))

    high, low = spread_rows([near_w[r] * scale[r : r + 1] for r in range(4)])
    home_high, home_low = halves(home_ref[...])
    acc = dot(high[:, :64], home_high, NN) + dot(high[:, :64], home_low, NN)
    acc += dot(low[:, :64], home_high, NN)
    far_w = [far_w[r] * scale[r : r + 1] for r in range(4)]
    spread = [spread_rows([far_w[r][g : g + 1] for r in range(4)]) for g in range(8)]
    high = jnp.concatenate([h for h, _ in spread], axis=1)
    low = jnp.concatenate([l for _, l in spread], axis=1)
    mixed_high, mixed_low = mixed_ref[:1024], mixed_ref[1024:]
    acc += dot(high, mixed_high, NN) + dot(high, mixed_low, NN) + dot(low, mixed_high, NN)
    lower = jnp.concatenate([acc[16 * r : 16 * r + 8] for r in range(4)], axis=0)
    upper = jnp.concatenate([acc[16 * r + 8 : 16 * r + 16] for r in range(4)], axis=0)
    split = jnp.concatenate([lower, upper], axis=0).astype(BF16).reshape(1, 2, 32, 128)
    out_ref[...] = jnp.broadcast_to(split, (32, 2, 32, 128)).reshape(64, 32, 128)


def join_kernel(mine_ref, received_ref, out_ref):
    zp = lax.axis_index("zp")
    out_ref[zp] = mine_ref[pl.ds(pl.multiple_of(zp * 1024, 1024), 1024)]
    out_ref[1 - zp] = received_ref[...]


def project_kernel(rows_ref, weight_ref, out_ref, wide_ref):
    q = iota((256, 256), 0)
    p = iota((256, 256), 1)
    move = p == 32 * ((q >> 2) & 7) + 8 * (q & 3) + (q >> 5)
    move = move.astype(F32).astype(BF16)
    for b in range(8):
        parts = [rows_ref[(8 * b + i - FIRST) % 64] for i in range(8)]
        moved = dot(move, jnp.concatenate(parts, axis=0), NN).astype(BF16)
        for h in range(8):
            wide_ref[32 * b : 32 * b + 32, 128 * h : 128 * h + 128] = moved[32 * h : 32 * h + 32]
    wide = wide_ref[...]
    for c in range(2):
        out_ref[c] = dot(wide, weight_ref[c], NN).astype(BF16).reshape(8, 32, 256)


def finish_kernel(sums_ref, base_ref, out_ref):
    total = base_ref[...]
    for s in range(16):
        total = total + sums_ref[s].astype(F32)
    out_ref[...] = total.astype(BF16)


def body(
    queries,
    new_keys,
    new_values,
    home_keys,
    home_values,
    home_len,
    lent_keys,
    lent_values,
    lent_req,
    lent_len,
    out_weight,
    residual,
):
    here = lax.axis_index(INST)
    packed = pl.pallas_call(
        pack_kernel,
        out_shape=jax.ShapeDtypeStruct((64, 64, 128), BF16),
        in_specs=[ANY] * 4,
        out_specs=ANY,
        scratch_shapes=[
            pltpu.SMEM((4032,), jnp.int32),
            pltpu.SMEM((63,), jnp.int32),
            pltpu.VMEM((63, 32, 128), BF16),
            pltpu.VMEM((63, 32, 128), BF16),
            pltpu.VMEM((64, 32, 128), BF16),
            pltpu.VMEM((64, 32, 128), BF16),
            pltpu.SemaphoreType.DMA((6,)),
        ],
        name="pack_lent",
    )(
        lent_req,
        lent_len,
        lent_keys.reshape(63, 32, 128),
        lent_values.reshape(63, 32, 128),
    )
    recv = lax.all_to_all(
        packed, INST, split_axis=0, concat_axis=0, tiled=True, axis_index_groups=ORDER
    )
    asked, req, sent = pl.pallas_call(
        ask_kernel,
        out_shape=(
            jax.ShapeDtypeStruct((8, 128, 128), BF16),
            jax.ShapeDtypeStruct((8, 128), F32),
            jax.ShapeDtypeStruct((1024, 256), BF16),
        ),
        in_specs=[SMEM, VMEM, VMEM, VMEM, ANY],
        out_specs=(VMEM,) * 3,
        compiler_params=PARAMS,
        name="ask_queries",
    )(
        here.reshape(1),
        jnp.pad(lent_req, (0, 64), constant_values=-4).reshape(32, 128),
        queries,
        out_weight,
        packed,
    )
    received = lax.ppermute(sent, "zp", [(0, 1), (1, 0)])
    home_out, home_stat, base = pl.pallas_call(
        home_kernel,
        out_shape=(
            jax.ShapeDtypeStruct((64, 128), F32),
            jax.ShapeDtypeStruct((2, 128), F32),
            jax.ShapeDtypeStruct((32, 256), F32),
        ),
        in_specs=[SMEM] + [VMEM] * 6,
        out_specs=(VMEM,) * 3,
        compiler_params=PARAMS,
        name="home_part",
    )(
        home_len,
        queries,
        new_keys.reshape(4, 128),
        new_values.reshape(4, 128),
        home_keys.reshape(4, 256, 128),
        home_values.reshape(4, 256, 128),
        residual,
    )
    copies = pl.pallas_call(
        attend_kernel,
        out_shape=jax.ShapeDtypeStruct((64, 32, 128), BF16),
        in_specs=[VMEM] * 5,
        out_specs=VMEM,
        scratch_shapes=[pltpu.VMEM((2048, 128), F32), pltpu.VMEM((2048, 128), BF16)],
        compiler_params=PARAMS,
        name="attend",
    )(asked, req, home_stat, home_out, recv)
    rows = lax.all_to_all(
        copies, INST, split_axis=0, concat_axis=0, tiled=True, axis_index_groups=ORDER
    )
    weights = pl.pallas_call(
        join_kernel,
        out_shape=jax.ShapeDtypeStruct((2, 1024, 256), BF16),
        in_specs=[VMEM, VMEM],
        out_specs=VMEM,
        compiler_params=PARAMS,
        cost_estimate=pl.CostEstimate(flops=10**11, bytes_accessed=2**21, transcendentals=0),
        name="join_weights",
    )(out_weight, received)
    partial = pl.pallas_call(
        project_kernel,
        out_shape=jax.ShapeDtypeStruct((2, 8, 32, 256), BF16),
        in_specs=[VMEM, VMEM],
        out_specs=VMEM,
        scratch_shapes=[pltpu.VMEM((256, 1024), BF16)],
        compiler_params=PARAMS,
        name="project",
    )(rows, weights)
    sums = lax.all_to_all(
        partial.reshape(16, 32, 256), ("zp", "tp"), split_axis=0, concat_axis=0, tiled=True
    )
    return pl.pallas_call(
        finish_kernel,
        out_shape=jax.ShapeDtypeStruct((32, 256), BF16),
        in_specs=[VMEM, VMEM],
        out_specs=VMEM,
        compiler_params=PARAMS,
        name="finish",
    )(sums, base)


def solution(mesh):
    placed = (
        P(INST, "tp", None),
        P(INST, "tp", None),
        P(INST, "tp", None),
        P(INST, None, "tp", None),
        P(INST, None, "tp", None),
        P(INST),
        P(INST, None, "tp", None),
        P(INST, None, "tp", None),
        P(),
        P(INST),
        P("tp", INST),
        P("tp", INST),
    )
    fine = Mesh(mesh.devices.reshape(8, 4, 2, 8), INST + ("tp",))
    return jax.shard_map(
        body, mesh=fine, in_specs=placed, out_specs=P("tp", INST), check_vma=False
    )
```
